256 devices in a mesh: slab: 32 (over z, x), pencil: 8 (over y, core).
Axes of the slice: x: 4, y: 4, z: 8, core: 2. Of those that a mesh axis runs over, the one named last changes fastest.
Arguments:
- strength: float32 [65536], P(('slab', 'pencil')), may hold values from -6 to 6
- stencil_weight: float32 [64, 65536], P(None, ('slab', 'pencil')), may hold values from -1.5 to 1.5
- slot_panel: int32 [32, 8, 768], P('slab', 'pencil'), may hold values from 0 to 256, as said below
- slot_anchor: int32 [32, 8, 768], P('slab', 'pencil'), may hold values from 0 to 105724, as said below
- green_spectrum: float32 [256, 256, 512], P('slab', 'pencil'), may hold values from 0.1 to 10, as said below
- near_index: int32 [32, 65536], P(None, ('slab', 'pencil')), may hold values from 0 to 767
- near_factor: float32 [32, 65536], P(None, ('slab', 'pencil')), may hold values from -1.2 to 1.2
Outputs:
- applied: float32 [65536], P(('slab', 'pencil'))
The draws below stay inside these ranges and needn't reach their ends.
Inputs may be any that keep to these rules, and one draw needn't show every extreme that they name: `slot_panel`: on each sending device every one of its 256 panels stands in exactly one slot; the value 256 marks an empty slot. On each sending device the 24 slots of some destination slab are all occupied, and for each pencil index some destination slab receives full blocks of 24 from every sending slab. `slot_anchor`: each entry is (ox * 32 + oy) * 256 + oz with ox <= 12, oy <= 28, oz <= 252, so that every stencil lies inside the receiving device's cells. green_spectrum[y, z, x] equals green_spectrum[(-y) mod 256, (-z) mod 256, (-x) mod 512]: the spectrum of a real even Green's function.
All inputs are finite; a program needn't handle non-finite values.
Results may differ from the reference program's by a relative error of at most 0.0003.
Values sent between devices are 32-bit elements; how exact they have to be, the bound alone decides.
No kernel may reach another device: no remote copies, remote signals or barrier semaphores. Data moves between devices by JAX's collectives and lax.ppermute only.
A program may use at most 128 MiB of HBM per device.

```python
import jax
import jax.numpy as jnp
from jax import lax

GX = 512
GY = 256
GZ = 256
EDGE = 4
NEAR = 32
PAN_DEV = 256
STENCIL = 64
CAP = 24
PANELS = 65536
N_SLAB = 32
N_PENCIL = 8


def shuffled_panels(key):
    return jax.random.permutation(key, PAN_DEV)


def draw_slot_panel(key, part):
    keys = jax.random.split(jax.random.fold_in(key, 11), 4)
    slot_total = N_SLAB * CAP
    shape = (N_SLAB, N_PENCIL, N_SLAB, CAP)
    full_slab = jax.random.randint(keys[0], (N_PENCIL,), 0, N_SLAB)
    leaning = jax.random.randint(keys[1], (N_SLAB, N_PENCIL, N_SLAB, 1), 0, 2000)
    jitter = jax.random.randint(keys[2], shape, 0, 1000)
    destination = lax.broadcasted_iota(jnp.int32, shape, 2)
    forced = destination == full_slab[None, :, None, None]
    score = jnp.where(forced, 0, leaning + jitter + 1).reshape(N_SLAB, N_PENCIL, slot_total)
    position = lax.broadcasted_iota(jnp.int32, score.shape, 2)
    score = score * slot_total + position
    order = jnp.argsort(score, axis=2)
    ranking = jnp.argsort(order, axis=2).astype(jnp.int32)
    panel_keys = jax.random.split(keys[3], N_SLAB * N_PENCIL)
    shuffle = jax.vmap(shuffled_panels)(panel_keys).reshape(N_SLAB, N_PENCIL, PAN_DEV).astype(jnp.int32)
    picked = jnp.take_along_axis(shuffle, jnp.minimum(ranking, PAN_DEV - 1), axis=2)
    return jnp.where(ranking < PAN_DEV, picked, PAN_DEV).astype(jnp.int32)


def draw_slot_anchor(key, part):
    keys = jax.random.split(jax.random.fold_in(key, 23), 4)
    slot_total = N_SLAB * CAP
    shape = (N_SLAB, N_PENCIL, slot_total)
    slab_rows = GX // N_SLAB
    pencil_rows = GY // N_PENCIL
    first_cell = jax.random.randint(keys[0], shape, 0, slab_rows - EDGE + 1)
    second_cell = jax.random.randint(keys[1], shape, 0, pencil_rows - EDGE + 1)
    third_cell = jax.random.randint(keys[2], shape, 0, GZ - EDGE + 1)
    anchor = (first_cell * pencil_rows + second_cell) * GZ + third_cell
    highest_cell = ((slab_rows - EDGE) * pencil_rows + pencil_rows - EDGE) * GZ + GZ - EDGE
    marked = jax.random.randint(keys[3], (N_SLAB, N_PENCIL, 1), 0, slot_total)
    position = lax.broadcasted_iota(jnp.int32, shape, 2)
    anchor = jnp.where(position == marked, highest_cell, anchor)
    return anchor.astype(jnp.int32)


def mirrored(values):
    flipped = jnp.flip(values, axis=(0, 1, 2))
    return jnp.roll(flipped, (1, 1, 1), axis=(0, 1, 2))


def draw_green_spectrum(key, part):
    inner = jax.random.fold_in(key, 37)
    shape = (GY, GZ, GX)
    raw = jnp.exp(jax.random.uniform(inner, shape, jnp.float32, jnp.log(0.1), jnp.log(10.0)))
    return (0.5 * (raw + mirrored(raw))).astype(jnp.float32)


def place_ends(array, key, smallest, high):
    shape = array.shape
    index_at = [jax.random.randint(jax.random.fold_in(key, axis), (), 0, shape[axis]) for axis in range(len(shape))]
    array = array.at[tuple(index_at)].set(smallest)
    longest = shape.index(max(shape))
    index_at[longest] = (index_at[longest] + 1) % shape[longest]
    return array.at[tuple(index_at)].set(high)


def shard_levels(own_key, shape, shards, least, largest):
    loudness = 1.0
    for dim, shards_of in shards:
        heights = jax.random.uniform(jax.random.fold_in(jax.random.fold_in(own_key, 6), dim), (shards_of,), jnp.float32, least / len(shards), largest / len(shards))
        loudness = loudness * jnp.repeat(jnp.exp(heights), shape[dim] // shards_of).reshape((-1,) + (1,) * (len(shape) - 1 - dim))
    return loudness


def gaussian(rng, dims, scale, reach, cuts=(), kind=jnp.bfloat16):
    drawn = scale * jax.random.normal(rng, dims, jnp.float32)
    if cuts:
        drawn = drawn * shard_levels(rng, dims, cuts, -0.22, 0.18)
    return jnp.clip(drawn, -reach, reach).astype(kind)


def setup_inputs(seed: int = 0) -> dict:
    arg_keys = jax.random.split(jax.random.key(seed), 8)
    return {
        "strength": gaussian(arg_keys[0], (PANELS,), 1.0, 6.0, ((0, 256),), jnp.float32),
        "stencil_weight": gaussian(arg_keys[1], (STENCIL, PANELS), 0.25, 1.5, ((1, 256),), jnp.float32),
        "slot_panel": draw_slot_panel(jax.random.fold_in(arg_keys[7], 71), 0),
        "slot_anchor": draw_slot_anchor(jax.random.fold_in(arg_keys[7], 71), 0),
        "green_spectrum": draw_green_spectrum(jax.random.fold_in(arg_keys[7], 71), 0),
        "near_index": place_ends(jax.random.randint(arg_keys[5], (NEAR, PANELS), 0, 3 * PAN_DEV), jax.random.fold_in(arg_keys[5], 1), 0, (3 * PAN_DEV) - 1).astype(jnp.int32),
        "near_factor": gaussian(arg_keys[6], (NEAR, PANELS), 0.2, 1.2, ((1, 256),), jnp.float32),
    }


def reference(strength, stencil_weight, slot_panel, slot_anchor, green_spectrum, near_index, near_factor):
    slab_rows = GX // N_SLAB
    pencil_rows = GY // N_PENCIL
    slot_total = N_SLAB * CAP
    own_strength = strength.reshape(N_SLAB, N_PENCIL, PAN_DEV)
    weight_all = stencil_weight.reshape(STENCIL, N_SLAB, N_PENCIL, PAN_DEV)
    corner = jnp.arange(STENCIL, dtype=jnp.int32)
    offsets = ((corner // (EDGE * EDGE)) * GY + (corner // EDGE) % EDGE) * GZ + corner % EDGE
    pencil_ids = jnp.arange(N_PENCIL, dtype=jnp.int32)
    slab_ids = jnp.arange(N_SLAB, dtype=jnp.int32)

    def slot_terms(source):
        source = jnp.asarray(source).astype(jnp.int32)
        table = lax.dynamic_index_in_dim(slot_panel, source, 0, keepdims=False)
        occupied = table < PAN_DEV
        chosen = jnp.minimum(table, PAN_DEV - 1)
        source_strength = lax.dynamic_index_in_dim(own_strength, source, 0, keepdims=False)
        strengths = jnp.where(occupied, jnp.take_along_axis(source_strength, chosen, axis=1), 0.0)
        source_weight = lax.dynamic_index_in_dim(weight_all, source, 1, keepdims=False)
        chosen_weight = jnp.take_along_axis(source_weight, jnp.broadcast_to(chosen[None], (STENCIL, N_PENCIL, slot_total)), axis=2)
        anchor = lax.dynamic_slice_in_dim(slot_anchor, (source * CAP).astype(jnp.int32), CAP, axis=2)
        anchor = jnp.transpose(anchor, (1, 0, 2))
        first_cell = anchor // (pencil_rows * GZ)
        second_cell = (anchor // GZ) % pencil_rows
        third_cell = anchor % GZ
        base_cell = ((slab_ids[None, :, None] * slab_rows + first_cell) * GY + pencil_ids[:, None, None] * pencil_rows + second_cell) * GZ + third_cell
        grid_cells = base_cell.reshape(N_PENCIL, slot_total)[None] + offsets[:, None, None]
        return table, strengths, chosen_weight, grid_cells

    def project(source, charge):
        table, strengths, chosen_weight, grid_cells = slot_terms(source)
        return charge.at[grid_cells.reshape(-1)].add((chosen_weight * strengths[None]).reshape(-1))

    charge = lax.fori_loop(0, N_SLAB, project, jnp.zeros((GX * GY * GZ,), jnp.float32))
    spectrum = jnp.transpose(green_spectrum, (2, 0, 1))
    transformed = jnp.fft.fftn(charge.reshape(GX, GY, GZ)) * spectrum
    potential = jnp.real(jnp.fft.ifftn(transformed)).astype(jnp.float32).reshape(-1)

    def interpolate(source):
        table, strengths, chosen_weight, grid_cells = slot_terms(source)
        values = jnp.sum(chosen_weight * potential[grid_cells], axis=0)
        empty = jnp.zeros((N_PENCIL, PAN_DEV), jnp.float32)
        return empty.at[pencil_ids[:, None], table].add(values, mode="drop")

    far_field = lax.map(interpolate, slab_ids)
    extended = jnp.concatenate([jnp.roll(own_strength, 1, axis=0), own_strength, jnp.roll(own_strength, -1, axis=0)], axis=2)
    partner_index = near_index.reshape(NEAR, N_SLAB, N_PENCIL, PAN_DEV)
    partners = jnp.take_along_axis(jnp.broadcast_to(extended[None], (NEAR, N_SLAB, N_PENCIL, 3 * PAN_DEV)), partner_index, axis=3)
    near_field = jnp.sum(near_factor.reshape(NEAR, N_SLAB, N_PENCIL, PAN_DEV) * partners, axis=0)
    return (far_field + near_field).reshape(-1)
```

```python
import math

import jax
import jax.numpy as jnp
import numpy as np
from jax import lax
from jax.experimental import pallas as pl
from jax.experimental.pallas import tpu as pltpu
from jax.sharding import PartitionSpec as P

GX = 512
GY = 256
GZ = 256
EDGE = 4
PAN_DEV = 256
CAP = 24
N_SLAB = 32
N_PENCIL = 8
SLOTS = N_SLAB * CAP
SLAB_ROWS = 16
PENCIL_ROWS = 32
KZ = 16
VMEM_LIMIT = 40 * 2**20
F32 = jnp.float32
BF16 = jnp.bfloat16


def kz_of(pencil, place):
    return np.where(
        pencil < 4, 32 * pencil + place, -(32 * (7 - pencil) + 16 + place)
    )


def z_tables():
    pencil, ri, place = np.meshgrid(np.arange(8), np.arange(2), np.arange(KZ), indexing="ij")
    kz = kz_of(pencil, place).reshape(-1)
    ri = ri.reshape(-1)
    shared = (pencil.reshape(-1) == 0) & (place.reshape(-1) == 0)
    z = np.arange(GZ)
    theta = 2 * np.pi * ((z[:, None] * kz[None, :]) % GZ) / GZ
    sign = 1.0 - 2.0 * (z % 2)
    forward = np.where(ri == 0, np.cos(theta), -np.sin(theta))
    forward = np.where(shared & (ri == 1), sign[:, None], forward)
    scale = np.where(shared, 1.0, 2.0) / GZ
    backward = (forward * scale).T
    return forward, backward


def y_tables():
    slab, ro, k8 = (a.reshape(-1) for a in np.meshgrid(np.arange(32), np.arange(2), np.arange(8), indexing="ij"))
    pencil, ri, y32 = (a.reshape(-1) for a in np.meshgrid(np.arange(8), np.arange(2), np.arange(32), indexing="ij"))
    ky = (8 * slab + k8)[:, None]
    ro = ro[:, None]
    y = (32 * pencil + y32)[None, :]
    ri = ri[None, :]
    theta = 2 * np.pi * ((ky * y) % GY) / GY
    cosine, sine = np.cos(theta), np.sin(theta)
    forward = np.where(ro == ri, cosine, np.where(ro == 0, sine, -sine))
    backward = forward.T / GY
    low = (ky > 0) & (ky < 128)
    high = ky > 128
    ends = (ky == 0) | (ky == 128)
    part = np.where(ro == 0, cosine, -sine)
    shared = np.where(low & (ri == 0), part, 0.0)
    shared = np.where(high & (ri == 1), part, shared)
    shared = np.where(ends & (ro == ri), cosine, shared)
    shared_back = (shared * np.where(ends, 1.0, 2.0)).T / GY
    return forward, shared, backward, shared_back


def x_tables():
    k1, ro, ko = (a.reshape(-1)[:, None] for a in np.meshgrid(np.arange(32), np.arange(2), np.arange(8), indexing="ij"))
    slab, ri, ki = (a.reshape(-1)[None, :] for a in np.meshgrid(np.arange(32), np.arange(2), np.arange(8), indexing="ij"))
    theta = 2 * np.pi * ((k1 * slab) % 32) / 32
    rows = np.where(ro == ri, np.cos(theta), np.where(ro == 0, np.sin(theta), -np.sin(theta)))
    rows = rows * (ko == ki)
    rows_back = rows.T / GX
    x16 = np.arange(16)
    twist = 2 * np.pi * np.arange(32)[:, None] * x16[None, :] / GX
    twist = np.repeat(np.repeat(twist, 8, axis=0), KZ, axis=1)
    inner = 2 * np.pi * ((x16[:, None] * x16[None, :]) % 16) / 16
    eye = np.eye(KZ)
    cosine, sine = np.kron(np.cos(inner), eye), np.kron(np.sin(inner), eye)
    lanes = np.block([[cosine, -sine], [sine, cosine]])
    lanes_back = lanes.T
    return rows, rows_back, np.cos(twist), np.sin(twist), lanes, lanes_back


def pair(table):
    high = np.asarray(table, np.float32).astype(jnp.bfloat16)
    low = (np.asarray(table, np.float64) - high.astype(np.float64)).astype(jnp.bfloat16)
    return jnp.asarray(high), jnp.asarray(low)


def split(value):
    high = value.astype(BF16)
    return high, (value - high.astype(F32)).astype(BF16)


def mm(left, right):
    return jnp.dot(left, right, preferred_element_type=F32)


def mm_nt(left, right):
    return lax.dot_general(left, right, (((1,), (1,)), ((), ())), preferred_element_type=F32)


def mm3(left, right):
    return mm(left[0], right[0]) + (mm(left[0], right[1]) + mm(left[1], right[0]))


def call(kernel, out_shape, *args, scratch=(), smem=()):
    specs = [
        pl.BlockSpec(memory_space=pltpu.SMEM) if i in smem else pl.BlockSpec(memory_space=pltpu.VMEM)
        for i in range(len(args))
    ]
    multi = isinstance(out_shape, (list, tuple)) and not isinstance(out_shape, jax.ShapeDtypeStruct)
    out_spec = pl.BlockSpec(memory_space=pltpu.VMEM)
    return pl.pallas_call(
        kernel,
        out_shape=out_shape,
        in_specs=specs,
        out_specs=[out_spec] * len(out_shape) if multi else out_spec,
        scratch_shapes=list(scratch),
        compiler_params=pltpu.CompilerParams(vmem_limit_bytes=VMEM_LIMIT),
        name=kernel.__name__,
    )(*args)


def swap_groups(tiles):
    tiles = list(tiles)
    group = lax.broadcasted_iota(jnp.int32, tiles[0].shape, 1) // 16
    for bit in range(3):
        step = 1 << bit
        upper = (group & step) != 0
        for i in range(8):
            if i & step:
                continue
            low, high = tiles[i], tiles[i + step]
            tiles[i] = jnp.where(upper, pltpu.roll(high, 16 * step, 1), low)
            tiles[i + step] = jnp.where(upper, high, pltpu.roll(low, 128 - 16 * step, 1))
    return tiles


def pack(weight_ref, strength_ref, slot_ref, out_ref):
    slots = jnp.transpose(jnp.broadcast_to(slot_ref[0], (128, SLOTS)))
    panel = lax.broadcasted_iota(jnp.int32, (SLOTS, 128), 1)
    hot = jnp.concatenate([(slots == panel), (slots == panel + 128)], axis=1)
    hot = jnp.where(hot, 1.0, 0.0).astype(BF16)
    row = lax.broadcasted_iota(jnp.int32, (64, PAN_DEV), 0)
    extra = jnp.where(row == 0, jnp.broadcast_to(strength_ref[...], (64, PAN_DEV)), 0.0)
    values = jnp.concatenate([weight_ref[...], extra], axis=0)
    high, low = split(values)
    out_ref[...] = mm_nt(hot, high) + mm_nt(hot, low)


def anchor_parts(anchor):
    return anchor >> 13, (anchor >> 8) & 31, anchor & 255


def weights_by_slot(arrived_ref, order_ref):
    high, low = split(arrived_ref[...])
    return mm_nt(order_ref[...], high) + mm_nt(order_ref[...], low)


def z_hot(third, dz):
    z = lax.broadcasted_iota(jnp.int32, (GZ, SLOTS), 0)
    return jnp.where(z - dz == third, 1.0, 0.0).astype(BF16)


def y_place(second, y_ref, inside_ref):
    rel = lax.broadcasted_iota(jnp.int32, (PENCIL_ROWS, SLOTS), 0) - second
    inside = (rel >= 0) & (rel < EDGE)
    y_ref[...] = jnp.where(inside, rel, 0)
    inside_ref[...] = jnp.where(inside, 1.0, 0.0)


def stencil_row(x, first, weight_ref):
    total = jnp.zeros((16, SLOTS), F32)
    for dx in range(EDGE):
        total = jnp.where(first == x - dx, weight_ref[dx * 16 : (dx + 1) * 16, :], total)
    return total


def place_rows(rows, dz, y_ref, inside_ref):
    half = rows[(dz // 2) * 8 : (dz // 2) * 8 + 8]
    out = []
    for block in range(PENCIL_ROWS // 8):
        pieces = []
        for lane in range(SLOTS // 128):
            index = y_ref[block * 8 : block * 8 + 8, lane * 128 : (lane + 1) * 128] + (dz % 2) * 4
            pieces.append(
                jnp.take_along_axis(half[:, lane * 128 : (lane + 1) * 128], index, axis=0, mode="promise_in_bounds")
            )
        out.append(jnp.concatenate(pieces, axis=1) * inside_ref[block * 8 : block * 8 + 8, :])
    return jnp.concatenate(out, axis=0)


def project(arrived_ref, anchor_ref, order_ref, zh_ref, zl_ref, out_ref, weight_ref, y_ref, inside_ref, high_ref, low_ref, hot_ref):
    first, second, third = anchor_parts(anchor_ref[0])
    weights = weights_by_slot(arrived_ref, order_ref)
    weight_ref[...] = weights[:64] * weights[64:65]
    y_place(second, y_ref, inside_ref)
    for dz in range(EDGE):
        hot_ref[:, dz * SLOTS : (dz + 1) * SLOTS] = z_hot(third, dz)

    def step(x, carry):
        rows = stencil_row(x, first, weight_ref)
        at = pl.ds(pl.multiple_of(x * PENCIL_ROWS, PENCIL_ROWS), PENCIL_ROWS)
        for dz in range(EDGE):
            high, low = split(place_rows(rows, dz, y_ref, inside_ref))
            high_ref[at, dz * SLOTS : (dz + 1) * SLOTS] = high
            low_ref[at, dz * SLOTS : (dz + 1) * SLOTS] = low
        return carry

    lax.fori_loop(0, SLAB_ROWS, step, 0)
    hot = hot_ref[...]
    charge = mm_nt(high_ref[...], hot) + mm_nt(low_ref[...], hot)
    after = mm3(split(charge), (zh_ref[...], zl_ref[...]))
    for half in range(2):
        for quarter in range(2):
            tiles = [
                after[x * 32 : x * 32 + 32, quarter * 128 : quarter * 128 + 128]
                for x in range(half * 8, half * 8 + 8)
            ]
            for g, tile in enumerate(swap_groups(tiles)):
                pencil, ri = quarter * 4 + g // 2, g % 2
                start = pencil * 128 + half * 64 + ri * 32
                out_ref[start : start + 32, :] = tile


def gathered(ref, count, rows):
    block = ref[...].reshape(count, 2, rows, 128)
    return jnp.concatenate([block[:, half].reshape(count * rows, 128) for half in range(2)], axis=1)


def scattered(value, ref, count, rows):
    for half in range(2):
        part = value[:, half * 128 : half * 128 + 128].reshape(count, rows, 128)
        for i in range(count):
            ref[(i * 2 + half) * rows : (i * 2 + half + 1) * rows, :] = part[i]


def shared_lane(shape):
    return lax.broadcasted_iota(jnp.int32, shape, 1) % KZ == 0


def y_stage(source, target):
    def kernel(flag_ref, in_ref, th_ref, tl_ref, sh_ref, sl_ref, out_ref, work_ref):
        data = split(gathered(in_ref, *source))
        work_ref[...] = mm3((th_ref[...], tl_ref[...]), data)

        @pl.when(flag_ref[0] == 1)
        def _():
            other = mm3((sh_ref[...], sl_ref[...]), data)
            work_ref[...] = jnp.where(shared_lane(other.shape), other, work_ref[...])

        scattered(work_ref[...], out_ref, *target)

    return kernel


def y_forward(*refs):
    y_stage((8, 64), (32, 16))(*refs)


def y_backward(*refs):
    y_stage((32, 16), (8, 64))(*refs)


def x_stage(flag_ref, in_ref, rh, rl, rbh, rbl, cos_ref, sin_ref, lh, ll, lbh, lbl, green_ref, other_ref, out_ref, re_ref, im_ref):
    cosine, sine = cos_ref[...], sin_ref[...]
    data = gathered(in_ref, 32, 16)

    def spectrum(value):
        rows = mm3((rh[...], rl[...]), split(value)).reshape(32, 2, 8, 256)
        re, im = rows[:, 0].reshape(256, 256), rows[:, 1].reshape(256, 256)
        turned = jnp.concatenate([re * cosine + im * sine, im * cosine - re * sine], axis=1)
        return mm3(split(turned), (lh[...], ll[...]))

    full = spectrum(data)
    re_ref[...] = full[:, :256] * green_ref[...]
    im_ref[...] = full[:, 256:] * green_ref[...]

    @pl.when(flag_ref[1] == 1)
    def _():
        row = lax.broadcasted_iota(jnp.int32, data.shape, 0)
        mirror = spectrum(jnp.where((row // 8) % 2 == 1, -data, data))
        re_ref[...] += mirror[:, :256] * other_ref[...]
        im_ref[...] += mirror[:, 256:] * other_ref[...]

    product = jnp.concatenate([re_ref[...], im_ref[...]], axis=1)
    back = mm3(split(product), (lbh[...], lbl[...]))
    re, im = back[:, :256], back[:, 256:]
    re, im = re * cosine - im * sine, im * cosine + re * sine
    rows = jnp.stack([re.reshape(32, 8, 256), im.reshape(32, 8, 256)], axis=1).reshape(512, 256)
    scattered(mm3((rbh[...], rbl[...]), split(rows)), out_ref, 32, 16)


def sample(in_ref, arrived_ref, anchor_ref, order_ref, zh_ref, zl_ref, spread_ref, out_ref, weight_ref, y_ref, inside_ref, after_ref, ph_ref, pl_ref, hot_ref, sum_ref):
    for half in range(2):
        for quarter in range(2):
            tiles = []
            for g in range(8):
                pencil, ri = quarter * 4 + g // 2, g % 2
                start = pencil * 128 + half * 64 + ri * 32
                tiles.append(in_ref[start : start + 32, :])
            for i, tile in enumerate(swap_groups(tiles)):
                x = half * 8 + i
                after_ref[x * 32 : x * 32 + 32, quarter * 128 : quarter * 128 + 128] = tile
    potential = mm3(split(after_ref[...]), (zh_ref[...], zl_ref[...]))
    ph_ref[...], pl_ref[...] = split(potential)
    first, second, third = anchor_parts(anchor_ref[0])
    weights = weights_by_slot(arrived_ref, order_ref)
    weight_ref[...] = weights[:64]
    y_place(second, y_ref, inside_ref)
    for dz in range(EDGE):
        hot_ref[:, dz * SLOTS : (dz + 1) * SLOTS] = z_hot(third, dz)
    sum_ref[...] = jnp.zeros((PENCIL_ROWS, SLOTS), F32)

    def step(x, carry):
        rows = stencil_row(x, first, weight_ref)
        at = pl.ds(pl.multiple_of(x * PENCIL_ROWS, PENCIL_ROWS), PENCIL_ROWS)
        high, low = ph_ref[at, :], pl_ref[at, :]
        total = sum_ref[...]
        for dz in range(EDGE):
            hot = hot_ref[:, dz * SLOTS : (dz + 1) * SLOTS]
            total += (mm(high, hot) + mm(low, hot)) * place_rows(rows, dz, y_ref, inside_ref)
        sum_ref[...] = total
        return carry

    lax.fori_loop(0, SLAB_ROWS, step, 0)
    far = jnp.sum(sum_ref[...], axis=0, keepdims=True)
    slab = lax.broadcasted_iota(jnp.int32, (N_SLAB, SLOTS), 0)
    slot = lax.broadcasted_iota(jnp.int32, (N_SLAB, SLOTS), 1)
    own = (slot >= slab * CAP) & (slot < slab * CAP + CAP)
    high, low = split(jnp.where(own, jnp.broadcast_to(far, own.shape), 0.0))
    out_ref[...] = mm(high, spread_ref[...]) + mm(low, spread_ref[...])


def near(low_ref, own_ref, high_ref, index_ref, factor_ref, out_ref):
    table = jnp.concatenate([low_ref[...], own_ref[...], high_ref[...]], axis=1)
    for lane in range(2):
        total = jnp.zeros((8, 128), F32)
        for block in range(4):
            at = (slice(block * 8, block * 8 + 8), slice(lane * 128, lane * 128 + 128))
            index = index_ref[at]
            inner, outer = index & 127, index >> 7
            found = jnp.zeros((8, 128), F32)
            for part in range(6):
                row = jnp.broadcast_to(table[:, part * 128 : part * 128 + 128], (8, 128))
                value = jnp.take_along_axis(row, inner, axis=1, mode="promise_in_bounds")
                found = jnp.where(outer == part, value, found)
            total += found * factor_ref[at]
        out_ref[:, lane * 128 : lane * 128 + 128] = jnp.sum(total, axis=0, keepdims=True)


def finish(far_ref, spread_ref, own_ref, slot_ref, near_ref, out_ref):
    high, low = split(far_ref[...])
    own = own_ref[...]
    rows = (mm(own, high) + mm(own, low)) * spread_ref[...].astype(F32)
    column = jnp.sum(rows, axis=1, keepdims=True)
    slots = jnp.transpose(jnp.broadcast_to(slot_ref[0], (128, SLOTS)))
    panel = lax.broadcasted_iota(jnp.int32, (SLOTS, 128), 1)
    for lane in range(2):
        part = jnp.where(slots == panel + lane * 128, column, 0.0)
        at = slice(lane * 128, lane * 128 + 128)
        out_ref[:, at] = jnp.sum(part, axis=0, keepdims=True) + near_ref[:, at]


def swap(value, axis, count):
    rows = value.shape[0]
    return lax.all_to_all(value.reshape(count, rows // count, 128), axis, 0, 0, tiled=True).reshape(rows, 128)


def arrange_green(green, slab, pencil):
    plane = lax.ppermute(green[:, 0, :], "pencil", [(4, 0)])
    chosen = jnp.where(pencil < 4, green[:, :KZ], jnp.flip(green[:, 1 : KZ + 1], axis=1))
    zero = chosen[:, 0, :]
    line = lax.broadcasted_iota(jnp.int32, zero.shape, 0) == 0
    ends = line & ((slab == 0) | (slab == 16))
    both = jnp.where(ends, 0.5 * (zero + plane), jnp.where(slab >= 16, plane, zero))
    both = jnp.where(pencil == 0, both, zero)
    differ = jnp.where(ends & (pencil == 0), 0.5 * (zero - plane), 0.0)
    place = lax.broadcasted_iota(jnp.int32, chosen.shape, 1) == 0
    chosen = jnp.where(place, both[:, None, :], chosen)
    other = jnp.where(place, differ[:, None, :], 0.0)

    def order(value):
        return value.reshape(8, KZ, 16, 32).transpose(3, 0, 2, 1).reshape(256, 256)

    return order(chosen), order(other)


def per_device(strength, stencil_weight, slot_panel, slot_anchor, green_spectrum, near_index, near_factor):
    slab = lax.axis_index("slab")
    pencil = lax.axis_index("pencil")
    flags = jnp.stack([pencil == 0, (pencil == 0) & ((slab == 0) | (slab == 16))]).astype(jnp.int32)
    row = strength.reshape(1, PAN_DEV)

    z_fwd, z_bwd = (pair(t) for t in z_tables())
    y_fwd, y_fwd_shared, y_bwd, y_bwd_shared = (pair(t) for t in y_tables())
    rows, rows_back, cosine, sine, lanes, lanes_back = x_tables()
    rows, rows_back, lanes, lanes_back = (pair(t) for t in (rows, rows_back, lanes, lanes_back))
    cosine, sine = jnp.asarray(cosine, F32), jnp.asarray(sine, F32)
    order = np.zeros((128, 128))
    for dx in range(4):
        for dy in range(4):
            for dz in range(4):
                order[dx * 16 + dz * 4 + dy, dx * 16 + dy * 4 + dz] = 1.0
    order[64, 64] = 1.0
    order = jnp.asarray(order, BF16)
    index = np.arange(SLOTS)
    spread = jnp.asarray((index % CAP)[:, None] == np.arange(128)[None, :], BF16)
    own = jnp.asarray((index // CAP)[:, None] == np.arange(N_SLAB)[None, :], BF16)

    shape = jax.ShapeDtypeStruct
    payload = call(pack, shape((SLOTS, 128), F32), stencil_weight, row, slot_panel)
    arrived = swap(payload, "slab", N_SLAB)
    common = [
        pltpu.VMEM((64, SLOTS), F32),
        pltpu.VMEM((PENCIL_ROWS, SLOTS), jnp.int32),
        pltpu.VMEM((PENCIL_ROWS, SLOTS), F32),
    ]
    after_z = call(
        project, shape((1024, 128), F32), arrived, slot_anchor, order, *z_fwd,
        scratch=common + [pltpu.VMEM((512, EDGE * SLOTS), BF16)] * 2 + [pltpu.VMEM((GZ, EDGE * SLOTS), BF16)],
    )
    by_y = swap(after_z, "pencil", N_PENCIL)
    after_y = call(
        y_forward, shape((1024, 128), F32), flags, by_y, *y_fwd, *y_fwd_shared,
        scratch=[pltpu.VMEM((512, 256), F32)], smem=(0,),
    )
    by_x = swap(after_y, "slab", N_SLAB)
    green, other = arrange_green(green_spectrum, slab, pencil)
    after_x = call(
        x_stage, shape((1024, 128), F32), flags, by_x, *rows, *rows_back, cosine, sine, *lanes, *lanes_back, green, other,
        scratch=[pltpu.VMEM((256, 256), F32)] * 2, smem=(0,),
    )
    back_x = swap(after_x, "slab", N_SLAB)
    back_y = call(
        y_backward, shape((1024, 128), F32), flags, back_x, *y_bwd, *y_bwd_shared,
        scratch=[pltpu.VMEM((512, 256), F32)], smem=(0,),
    )
    by_z = swap(back_y, "pencil", N_PENCIL)
    sampled = call(
        sample, shape((N_SLAB, 128), F32), by_z, arrived, slot_anchor, order, *z_bwd, spread,
        scratch=common
        + [pltpu.VMEM((512, 256), F32)]
        + [pltpu.VMEM((512, 256), BF16)] * 2
        + [pltpu.VMEM((GZ, EDGE * SLOTS), BF16), pltpu.VMEM((PENCIL_ROWS, SLOTS), F32)],
    )
    far = lax.all_to_all(sampled, "slab", 0, 0, tiled=True)
    forward = [(i, (i + 1) % N_SLAB) for i in range(N_SLAB)]
    backward = [(target, source) for source, target in forward]
    low = lax.ppermute(row, "slab", forward)
    high = lax.ppermute(row, "slab", backward)
    near_field = call(near, shape((1, PAN_DEV), F32), low, row, high, near_index, near_factor)
    return call(finish, shape((1, PAN_DEV), F32), far, spread, own, slot_panel, near_field).reshape(PAN_DEV)


def solution(mesh):
    in_specs = (
        P(("slab", "pencil")),
        P(None, ("slab", "pencil")),
        P("slab", "pencil", None),
        P("slab", "pencil", None),
        P("slab", "pencil", None),
        P(None, ("slab", "pencil")),
        P(None, ("slab", "pencil")),
    )
    out_specs = P(("slab", "pencil"))
    return jax.shard_map(
        per_device, mesh=mesh, in_specs=in_specs, out_specs=out_specs, check_vma=False
    )
```

```python
import math

import jax
import jax.numpy as jnp
import numpy as np
from jax import lax
from jax.experimental import pallas as pl
from jax.experimental.pallas import tpu as pltpu
from jax.sharding import PartitionSpec as P

GX = 512
GY = 256
GZ = 256
EDGE = 4
PAN_DEV = 256
CAP = 24
N_SLAB = 32
N_PENCIL = 8
SLOTS = N_SLAB * CAP
SLAB_ROWS = 16
PENCIL_ROWS = 32
KZ = 16
ROWS = 13 * N_SLAB
F32 = jnp.float32
BF16 = jnp.bfloat16


def kz_of(pencil, place):
    return np.where(
        pencil < 4, 32 * pencil + place, -(32 * (7 - pencil) + 16 + place)
    )


def z_tables():
    pencil, ri, place = np.meshgrid(np.arange(8), np.arange(2), np.arange(KZ), indexing="ij")
    kz = kz_of(pencil, place).reshape(-1)
    ri = ri.reshape(-1)
    shared = (pencil.reshape(-1) == 0) & (place.reshape(-1) == 0)
    z = np.arange(GZ)
    theta = 2 * np.pi * ((z[:, None] * kz[None, :]) % GZ) / GZ
    sign = 1.0 - 2.0 * (z % 2)
    forward = np.where(ri == 0, np.cos(theta), -np.sin(theta))
    forward = np.where(shared & (ri == 1), sign[:, None], forward)
    scale = np.where(shared, 1.0, 2.0) / GZ
    backward = (forward * scale).T
    return forward, backward


def y_tables():
    slab, ro, k8 = (a.reshape(-1) for a in np.meshgrid(np.arange(32), np.arange(2), np.arange(8), indexing="ij"))
    pencil, ri, y32 = (a.reshape(-1) for a in np.meshgrid(np.arange(8), np.arange(2), np.arange(32), indexing="ij"))
    ky = (8 * slab + k8)[:, None]
    ro = ro[:, None]
    y = (32 * pencil + y32)[None, :]
    ri = ri[None, :]
    theta = 2 * np.pi * ((ky * y) % GY) / GY
    cosine, sine = np.cos(theta), np.sin(theta)
    forward = np.where(ro == ri, cosine, np.where(ro == 0, sine, -sine))
    backward = forward.T / GY
    low = (ky > 0) & (ky < 128)
    high = ky > 128
    ends = (ky == 0) | (ky == 128)
    part = np.where(ro == 0, cosine, -sine)
    shared = np.where(low & (ri == 0), part, 0.0)
    shared = np.where(high & (ri == 1), part, shared)
    shared = np.where(ends & (ro == ri), cosine, shared)
    shared_back = (shared * np.where(ends, 1.0, 2.0)).T / GY
    return forward, shared, backward, shared_back


def x_tables():
    k1, ro, ko = (a.reshape(-1)[:, None] for a in np.meshgrid(np.arange(32), np.arange(2), np.arange(8), indexing="ij"))
    slab, ri, ki = (a.reshape(-1)[None, :] for a in np.meshgrid(np.arange(32), np.arange(2), np.arange(8), indexing="ij"))
    theta = 2 * np.pi * ((k1 * slab) % 32) / 32
    rows = np.where(ro == ri, np.cos(theta), np.where(ro == 0, np.sin(theta), -np.sin(theta)))
    rows = rows * (ko == ki)
    rows_back = rows.T / GX
    x16 = np.arange(16)
    twist = 2 * np.pi * np.arange(32)[:, None] * x16[None, :] / GX
    twist = np.repeat(np.repeat(twist, 8, axis=0), KZ, axis=1)
    inner = 2 * np.pi * ((x16[:, None] * x16[None, :]) % 16) / 16
    eye = np.eye(KZ)
    cosine, sine = np.kron(np.cos(inner), eye), np.kron(np.sin(inner), eye)
    lanes = np.block([[cosine, -sine], [sine, cosine]])
    lanes_back = lanes.T
    ro, k1 = (a.reshape(-1)[:, None] for a in np.meshgrid(np.arange(2), np.arange(32), indexing="ij"))
    ri, slab = (a.reshape(-1)[None, :] for a in np.meshgrid(np.arange(2), np.arange(32), indexing="ij"))
    theta = 2 * np.pi * ((k1 * slab) % 32) / 32
    line = np.where(ro == ri, np.cos(theta), np.where(ro == 0, np.sin(theta), -np.sin(theta)))
    line = line * np.where(ri == 1, -1.0, 1.0)
    return rows, rows_back, np.cos(twist), np.sin(twist), lanes, lanes_back, line


def pair(table):
    high = np.asarray(table, np.float32).astype(jnp.bfloat16)
    low = (np.asarray(table, np.float64) - high.astype(np.float64)).astype(jnp.bfloat16)
    return jnp.asarray(high), jnp.asarray(low)


def split(value):
    high = value.astype(BF16)
    return high, (value - high.astype(F32)).astype(BF16)


def mm(left, right):
    return jnp.dot(left, right, preferred_element_type=F32)


def mm_nt(left, right):
    return lax.dot_general(left, right, (((1,), (1,)), ((), ())), preferred_element_type=F32)


def mm3(left, right):
    return mm(left[0], right[0]) + (mm(left[0], right[1]) + mm(left[1], right[0]))


class Late:
    def __init__(self, copy, buffer):
        self.copy, self.buffer, self.here = copy, buffer, False

    def __getitem__(self, index):
        if not self.here:
            self.copy.wait()
            self.here = True
        return self.buffer[index]


def call(kernel, out_shape, *args, scratch=(), smem=(), late=(), limit=20):
    spaces = {i: pltpu.SMEM for i in smem} | {i: pltpu.HBM for i in late}
    specs = [pl.BlockSpec(memory_space=spaces.get(i, pltpu.VMEM)) for i in range(len(args))]
    multi = isinstance(out_shape, list)
    out_spec = pl.BlockSpec(memory_space=pltpu.VMEM)
    buffers = [pltpu.VMEM(args[i].shape, args[i].dtype) for i in late]
    if late:
        buffers.append(pltpu.SemaphoreType.DMA((len(late),)))
    own = len(args) + (len(out_shape) if multi else 1) + len(scratch)

    def wrapped(*refs):
        ins = list(refs[: len(args)])
        for place, i in enumerate(late):
            copy = pltpu.make_async_copy(ins[i], refs[own + place], refs[-1].at[place])
            copy.start()
            ins[i] = Late(copy, refs[own + place])
        kernel(*ins, *refs[len(args) : own])

    return pl.pallas_call(
        wrapped,
        out_shape=out_shape,
        in_specs=specs,
        out_specs=[out_spec] * len(out_shape) if multi else out_spec,
        scratch_shapes=list(scratch) + buffers,
        compiler_params=pltpu.CompilerParams(vmem_limit_bytes=limit * 2**20),
        name=kernel.__name__,
    )(*args)


def swap_groups(tiles):
    tiles = list(tiles)
    group = lax.broadcasted_iota(jnp.int32, tiles[0].shape, 1) // 16
    for bit in range(3):
        step = 1 << bit
        upper = (group & step) != 0
        for i in range(8):
            if i & step:
                continue
            low, high = tiles[i], tiles[i + step]
            tiles[i] = jnp.where(upper, pltpu.roll(high, 16 * step, 1), low)
            tiles[i + step] = jnp.where(upper, high, pltpu.roll(low, 128 - 16 * step, 1))
    return tiles


def lookup(tables, index):
    inner, outer = index & 127, index >> 7
    found = jnp.zeros((8, 128), F32)
    for part, table in enumerate(tables):
        row = jnp.broadcast_to(table, (8, 128))
        value = jnp.take_along_axis(row, inner, axis=1, mode="promise_in_bounds")
        found = jnp.where(outer == part, value, found)
    return found


def own_slots():
    slab = lax.broadcasted_iota(jnp.int32, (N_SLAB, SLOTS), 0)
    slot = lax.broadcasted_iota(jnp.int32, (N_SLAB, SLOTS), 1)
    return (slot >= slab * CAP) & (slot < slab * CAP + CAP)


def pack(slot_ref, spread_ref, lines_ref, pick_ref, other_pick_ref, weight_ref, strength_ref, out_ref):
    slots = jnp.broadcast_to(slot_ref[0], (N_SLAB, SLOTS)).astype(F32)
    by_slab = mm(jnp.where(own_slots(), slots, 0.0).astype(BF16), spread_ref[...])
    lane = lax.broadcasted_iota(jnp.int32, by_slab.shape, 1)
    by_slab = jnp.where(lane < CAP, by_slab, float(PAN_DEV))
    lines = mm(lines_ref[...], by_slab.astype(BF16))
    ones = jnp.ones((128, 128), BF16)
    panel = lax.broadcasted_iota(jnp.int32, (ROWS, 128), 1).astype(F32)
    hot = []
    for pick in (pick_ref, other_pick_ref):
        chosen = mm((lines * pick[...].astype(F32)).astype(BF16), ones)
        hot += [chosen == panel, chosen == panel + 128.0]
    hot = jnp.where(jnp.concatenate(hot, axis=1), 1.0, 0.0).astype(BF16)
    weight = weight_ref[...]
    empty = jnp.zeros_like(weight)
    values = jnp.concatenate(
        [jnp.concatenate([weight, empty], axis=1), jnp.concatenate([empty, weight], axis=1)], axis=0
    )
    high, low = split(values)
    out_ref[...] = mm_nt(hot, high) + mm_nt(hot, low)
    strength = strength_ref[...]
    tables = [strength[:, :128], strength[:, 128:]]
    index = by_slab.astype(jnp.int32)
    sent = jnp.concatenate([lookup(tables, index[i * 8 : i * 8 + 8]) for i in range(4)], axis=0)
    out_ref[pl.ds(12, N_SLAB, stride=13), :] = sent


def anchor_parts(anchor):
    return anchor >> 13, (anchor >> 8) & 31, anchor & 255


def z_hot(third, dz):
    z = lax.broadcasted_iota(jnp.int32, (GZ, SLOTS), 0)
    return jnp.where(z - dz == third, 1.0, 0.0).astype(BF16)


def y_place(second, y_ref):
    rel = lax.broadcasted_iota(jnp.int32, (PENCIL_ROWS, SLOTS), 0) - second
    y_ref[...] = jnp.where((rel >= 0) & (rel < EDGE), rel, EDGE)


def stencil_row(x, first, weight_ref):
    total = jnp.zeros((32, SLOTS), F32)
    for dx in range(EDGE):
        total = jnp.where(first == x - dx, weight_ref[dx * 32 : dx * 32 + 32, :], total)
    return total


def place_rows(rows, y_ref):
    out = []
    for block in range(PENCIL_ROWS // 8):
        pieces = []
        for lane in range(SLOTS // 128):
            at = slice(lane * 128, lane * 128 + 128)
            index = y_ref[block * 8 : block * 8 + 8, at]
            pieces.append(jnp.take_along_axis(rows[:, at], index, axis=0, mode="promise_in_bounds"))
        out.append(jnp.concatenate(pieces, axis=1))
    return jnp.concatenate(out, axis=0)


def project(arrived_ref, select_ref, spread_ref, order_ref, anchor_ref, zh_ref, zl_ref, out_ref, weight_ref, scaled_ref, y_ref, high_ref, low_ref):
    arrived = jnp.concatenate(split(arrived_ref[...]), axis=0)
    select = select_ref[...]
    total = jnp.zeros((256, SLOTS), F32)
    for half in range(2):
        turned = mm_nt(order_ref[half * 128 : half * 128 + 128, :], arrived).astype(BF16)
        turned = jnp.concatenate([turned[:, :ROWS], turned[:, ROWS:]], axis=0)
        total += mm(turned, select[half * ROWS : half * ROWS + ROWS])
    weights = total[:128] + total[128:]
    weight_ref[...] = weights
    high, low = split(arrived_ref[pl.ds(12, N_SLAB, stride=13), :])
    spread = spread_ref[...]
    strength = jnp.where(own_slots(), mm_nt(high, spread) + mm_nt(low, spread), 0.0)
    scaled_ref[...] = weights * jnp.sum(strength, axis=0, keepdims=True)
    first, second, third = anchor_parts(anchor_ref[0])
    y_place(second, y_ref)

    def step(x, carry):
        rows = stencil_row(x, first, scaled_ref)
        for dz in range(EDGE):
            high, low = split(place_rows(rows[dz * 8 : dz * 8 + 8], y_ref))
            at = pl.ds(pl.multiple_of(dz * 512 + x * PENCIL_ROWS, PENCIL_ROWS), PENCIL_ROWS)
            high_ref[at, :] = high
            low_ref[at, :] = low
        return carry

    lax.fori_loop(0, SLAB_ROWS, step, 0)
    hot = z_hot(third, 0)
    charge = jnp.zeros((512, GZ), F32)
    for dz in range(EDGE):
        at = slice(dz * 512, dz * 512 + 512)
        part = mm_nt(high_ref[at, :], hot) + mm_nt(low_ref[at, :], hot)
        charge += pltpu.roll(part, dz, 1) if dz else part
    after = mm3(split(charge), (zh_ref[...], zl_ref[...]))
    for half in range(2):
        for quarter in range(2):
            tiles = [
                after[x * 32 : x * 32 + 32, quarter * 128 : quarter * 128 + 128]
                for x in range(half * 8, half * 8 + 8)
            ]
            for g, tile in enumerate(swap_groups(tiles)):
                pencil, ri = quarter * 4 + g // 2, g % 2
                start = pencil * 128 + half * 64 + ri * 32
                out_ref[start : start + 32, :] = tile


def gathered(ref, count, rows):
    block = ref[...].reshape(count, 2, rows, 128)
    return jnp.concatenate([block[:, half].reshape(count * rows, 128) for half in range(2)], axis=1)


def scattered(value, ref, count, rows):
    for half in range(2):
        part = value[:, half * 128 : half * 128 + 128].reshape(count, rows, 128)
        for i in range(count):
            ref[(i * 2 + half) * rows : (i * 2 + half + 1) * rows, :] = part[i]


def shared_lane(shape):
    return lax.broadcasted_iota(jnp.int32, shape, 1) % KZ == 0


def y_stage(source, target):
    def kernel(flag_ref, in_ref, th_ref, tl_ref, sh_ref, sl_ref, out_ref, work_ref):
        data = split(gathered(in_ref, *source))
        work_ref[...] = mm3((th_ref[...], tl_ref[...]), data)

        @pl.when(flag_ref[0] == 1)
        def _():
            other = mm3((sh_ref[...], sl_ref[...]), data)
            work_ref[...] = jnp.where(shared_lane(other.shape), other, work_ref[...])

        scattered(work_ref[...], out_ref, *target)

    return kernel


def y_forward(*refs):
    y_stage((8, 64), (32, 16))(*refs)


def y_backward(*refs):
    y_stage((32, 16), (8, 64))(*refs)


def x_stage(flag_ref, in_ref, rh, rl, green_ref, other_ref, cos_ref, sin_ref, lh, ll, mh, ml, lbh, lbl, rbh, rbl, out_ref, re_ref, im_ref):
    data = gathered(in_ref, 32, 16)
    rows = mm3((rh[...], rl[...]), split(data)).reshape(32, 2, 8, 256)
    cosine, sine = cos_ref[...], sin_ref[...]
    lane_tables = (lh[...], ll[...])
    line_tables = (mh[...], ml[...])

    def lanes_of(re, im, cosine, sine):
        turned = jnp.concatenate([re * cosine + im * sine, im * cosine - re * sine], axis=1)
        return mm3(split(turned), lane_tables)

    full = lanes_of(rows[:, 0].reshape(256, 256), rows[:, 1].reshape(256, 256), cosine, sine)
    green = green_ref[...]
    for half in range(2):
        at = slice(half * 128, half * 128 + 128)
        re_ref[half] = full[:, at] * green[:, at]
        im_ref[half] = full[:, 256 + half * 128 : 384 + half * 128] * green[:, at]

    @pl.when(flag_ref[1] == 1)
    def _():
        line = jnp.concatenate(
            [
                jnp.concatenate([in_ref[pl.ds(half * 16 + ri * 8, 32, stride=32), :] for half in range(2)], axis=1)
                for ri in range(2)
            ],
            axis=0,
        )
        turned = mm3(line_tables, split(line))
        few = (cosine.reshape(32, 8, 256)[:, 0], sine.reshape(32, 8, 256)[:, 0])
        mirror = lanes_of(turned[:32], turned[32:], *few)
        other = other_ref[...]
        rows_at = pl.ds(0, 32, stride=8)
        for half in range(2):
            at = slice(half * 128, half * 128 + 128)
            re_ref[half, rows_at, :] += mirror[:, at] * other[:, at]
            im_ref[half, rows_at, :] += mirror[:, 256 + half * 128 : 384 + half * 128] * other[:, at]

    product = jnp.concatenate([re_ref[0], re_ref[1], im_ref[0], im_ref[1]], axis=1)
    back = mm3(split(product), (lbh[...], lbl[...]))
    re, im = back[:, :256], back[:, 256:]
    re, im = re * cosine - im * sine, im * cosine + re * sine
    rows = jnp.stack([re.reshape(32, 8, 256), im.reshape(32, 8, 256)], axis=1).reshape(512, 256)
    scattered(mm3((rbh[...], rbl[...]), split(rows)), out_ref, 32, 16)


def sample(in_ref, weight_ref, anchor_ref, zh_ref, zl_ref, spread_ref, out_ref, y_ref, after_ref, rows_ref, grid_ref):
    for half in range(2):
        for quarter in range(2):
            tiles = []
            for g in range(8):
                pencil, ri = quarter * 4 + g // 2, g % 2
                start = pencil * 128 + half * 64 + ri * 32
                tiles.append(in_ref[start : start + 32, :])
            for i, tile in enumerate(swap_groups(tiles)):
                x = half * 8 + i
                after_ref[x * 32 : x * 32 + 32, quarter * 128 : quarter * 128 + 128] = tile
    high, low = split(mm3(split(after_ref[...]), (zh_ref[...], zl_ref[...])))
    first, second, third = anchor_parts(anchor_ref[0])
    y_place(second, y_ref)

    def fill(x, carry):
        rows_ref[pl.ds(pl.multiple_of(x * 32, 32), 32), :] = stencil_row(x, first, weight_ref)
        return carry

    lax.fori_loop(0, SLAB_ROWS, fill, 0)
    total = jnp.zeros((8, SLOTS), F32)
    for dz in range(EDGE):
        hot = z_hot(third, dz)
        grid_ref[...] = mm(high, hot) + mm(low, hot)

        def step(x, total, dz=dz):
            rows = rows_ref[pl.ds(pl.multiple_of(x * 32 + dz * 8, 8), 8), :]
            cells = grid_ref[pl.ds(pl.multiple_of(x * 32, 32), 32), :] * place_rows(rows, y_ref)
            return total + jnp.sum(cells.reshape(4, 8, SLOTS), axis=0)

        total = lax.fori_loop(0, SLAB_ROWS, step, total)
    far = jnp.sum(total, axis=0, keepdims=True)
    high, low = split(jnp.where(own_slots(), jnp.broadcast_to(far, (N_SLAB, SLOTS)), 0.0))
    out_ref[...] = mm(high, spread_ref[...]) + mm(low, spread_ref[...])


def near(low_ref, own_ref, high_ref, index_ref, factor_ref, out_ref):
    table = jnp.concatenate([low_ref[...], own_ref[...], high_ref[...]], axis=1)
    tables = [table[:, part * 128 : part * 128 + 128] for part in range(6)]
    for lane in range(2):
        total = jnp.zeros((8, 128), F32)
        for block in range(4):
            at = (slice(block * 8, block * 8 + 8), slice(lane * 128, lane * 128 + 128))
            total += lookup(tables, index_ref[at]) * factor_ref[at]
        out_ref[:, lane * 128 : lane * 128 + 128] = jnp.sum(total, axis=0, keepdims=True)


def finish(far_ref, spread_ref, own_ref, slot_ref, near_ref, out_ref):
    high, low = split(far_ref[...])
    own = own_ref[...]
    rows = (mm(own, high) + mm(own, low)) * spread_ref[...].astype(F32)
    column = jnp.sum(rows, axis=1, keepdims=True)
    slots = jnp.transpose(jnp.broadcast_to(slot_ref[0], (128, SLOTS)))
    panel = lax.broadcasted_iota(jnp.int32, (SLOTS, 128), 1)
    for lane in range(2):
        part = jnp.where(slots == panel + lane * 128, column, 0.0)
        at = slice(lane * 128, lane * 128 + 128)
        out_ref[:, at] = jnp.sum(part, axis=0, keepdims=True) + near_ref[:, at]


def swap(value, axis, count):
    rows = value.shape[0]
    return lax.all_to_all(value.reshape(count, rows // count, 128), axis, 0, 0, tiled=True).reshape(rows, 128)


def arrange_green(green, slab, pencil):
    plane = lax.ppermute(green[:, 0, :], "pencil", [(4, 0)])
    chosen = jnp.where(pencil < 4, green[:, :KZ], jnp.flip(green[:, 1 : KZ + 1], axis=1))
    zero = chosen[:, 0, :]
    line = lax.broadcasted_iota(jnp.int32, zero.shape, 0) == 0
    ends = line & ((slab == 0) | (slab == 16))
    both = jnp.where(ends, 0.5 * (zero + plane), jnp.where(slab >= 16, plane, zero))
    both = jnp.where(pencil == 0, both, zero)
    differ = jnp.where(ends & (pencil == 0), 0.5 * (zero - plane), 0.0)
    place = lax.broadcasted_iota(jnp.int32, chosen.shape, 1) == 0
    chosen = jnp.where(place, both[:, None, :], chosen)
    chosen = chosen.reshape(8, KZ, 16, 32).transpose(3, 0, 2, 1).reshape(256, 256)
    first = lax.broadcasted_iota(jnp.int32, (32, 16, KZ), 2) == 0
    other = jnp.where(first, differ[0].reshape(16, 32).T[:, :, None], 0.0).reshape(32, 256)
    return chosen, other


def slot_tables():
    order = np.zeros((256, 128))
    for half in range(2):
        for dx in range(4):
            for dy in range(4):
                for dz in range(4):
                    order[half * 128 + dx * 32 + dz * 8 + dy, half * 64 + dx * 16 + dy * 4 + dz] = 1.0
    index = np.arange(SLOTS)
    spread = (index % CAP)[:, None] == np.arange(128)[None, :]
    own = (index // CAP)[:, None] == np.arange(N_SLAB)[None, :]
    line = np.arange(ROWS)
    slab, place = line // 13, line % 13
    lines = slab[:, None] == np.arange(N_SLAB)[None, :]
    lane = np.arange(128)[None, :]
    pick = lane == np.where(place < 12, place, CAP)[:, None]
    other_pick = lane == np.where(place < 12, place + 12, CAP)[:, None]
    target = slab * CAP + place
    select = np.concatenate(
        [(place[:, None] < 12) & (index[None, :] == (target + shift)[:, None]) for shift in (0, 12)]
    )
    return [jnp.asarray(t, BF16) for t in (order, spread, own, lines, pick, other_pick, select)]


def per_device(strength, stencil_weight, slot_panel, slot_anchor, green_spectrum, near_index, near_factor):
    slab = lax.axis_index("slab")
    pencil = lax.axis_index("pencil")
    flags = jnp.stack([pencil == 0, (pencil == 0) & ((slab == 0) | (slab == 16))]).astype(jnp.int32)
    row = strength.reshape(1, PAN_DEV)

    z_fwd, z_bwd = (pair(t) for t in z_tables())
    y_fwd, y_fwd_shared, y_bwd, y_bwd_shared = (pair(t) for t in y_tables())
    rows, rows_back, cosine, sine, lanes, lanes_back, line = x_tables()
    rows, rows_back, lanes, lanes_back, line = (pair(t) for t in (rows, rows_back, lanes, lanes_back, line))
    cosine, sine = jnp.asarray(cosine, F32), jnp.asarray(sine, F32)
    order, spread, own, lines, pick, other_pick, select = slot_tables()

    shape = jax.ShapeDtypeStruct
    payload = call(
        pack, shape((ROWS, 128), F32), slot_panel, spread, lines, pick, other_pick, stencil_weight, row,
        late=range(7), limit=8,
    )
    arrived = lax.all_to_all(payload.reshape(N_SLAB, 1, 13 * 128), "slab", 0, 0, tiled=True).reshape(ROWS, 128)
    after_z, weights = call(
        project, [shape((1024, 128), F32), shape((128, SLOTS), F32)], arrived, select, spread, order, slot_anchor, *z_fwd,
        scratch=[pltpu.VMEM((128, SLOTS), F32), pltpu.VMEM((PENCIL_ROWS, SLOTS), jnp.int32)]
        + [pltpu.VMEM((EDGE * 512, SLOTS), BF16)] * 2,
        late=(4, 5, 6), limit=24,
    )
    by_y = swap(after_z, "pencil", N_PENCIL)
    after_y = call(
        y_forward, shape((1024, 128), F32), flags, by_y, *y_fwd, *y_fwd_shared,
        scratch=[pltpu.VMEM((512, 256), F32)], smem=(0,), limit=12,
    )
    by_x = swap(after_y, "slab", N_SLAB)
    green, other = arrange_green(green_spectrum, slab, pencil)
    after_x = call(
        x_stage, shape((1024, 128), F32), flags, by_x, *rows, green, other, cosine, sine, *lanes, *line, *lanes_back, *rows_back,
        scratch=[pltpu.VMEM((2, 256, 128), F32)] * 2, smem=(0,), late=range(6, 16), limit=16,
    )
    forward = [(i, (i + 1) % N_SLAB) for i in range(N_SLAB)]
    backward = [(target, source) for source, target in forward]
    low = lax.ppermute(row, "slab", forward)
    high = lax.ppermute(row, "slab", backward)
    near_field = call(near, shape((1, PAN_DEV), F32), low, row, high, near_index, near_factor, limit=4)
    back_x = swap(after_x, "slab", N_SLAB)
    back_y = call(
        y_backward, shape((1024, 128), F32), flags, back_x, *y_bwd, *y_bwd_shared,
        scratch=[pltpu.VMEM((512, 256), F32)], smem=(0,), limit=12,
    )
    back_y, near_field = lax.optimization_barrier((back_y, near_field))
    by_z = swap(back_y, "pencil", N_PENCIL)
    sampled = call(
        sample, shape((N_SLAB, 128), F32), by_z, weights, slot_anchor, *z_bwd, spread,
        scratch=[pltpu.VMEM((PENCIL_ROWS, SLOTS), jnp.int32), pltpu.VMEM((512, 256), F32)]
        + [pltpu.VMEM((512, SLOTS), F32)] * 2,
        limit=20,
    )
    far = lax.all_to_all(sampled, "slab", 0, 0, tiled=True)
    return call(finish, shape((1, PAN_DEV), F32), far, spread, own, slot_panel, near_field, limit=4).reshape(PAN_DEV)


def solution(mesh):
    in_specs = (
        P(("slab", "pencil")),
        P(None, ("slab", "pencil")),
        P("slab", "pencil", None),
        P("slab", "pencil", None),
        P("slab", "pencil", None),
        P(None, ("slab", "pencil")),
        P(None, ("slab", "pencil")),
    )
    out_specs = P(("slab", "pencil"))
    return jax.shard_map(
        per_device, mesh=mesh, in_specs=in_specs, out_specs=out_specs, check_vma=False
    )
```

```python
import math

import jax
import jax.numpy as jnp
import numpy as np
from jax import lax
from jax.experimental import pallas as pl
from jax.experimental.pallas import tpu as pltpu
from jax.sharding import PartitionSpec as P

GX = 512
GY = 256
GZ = 256
EDGE = 4
PAN_DEV = 256
CAP = 24
N_SLAB = 32
N_PENCIL = 8
SLOTS = N_SLAB * CAP
SLAB_ROWS = 16
PENCIL_ROWS = 32
KZ = 16
ROWS = 13 * N_SLAB
F32 = jnp.float32
BF16 = jnp.bfloat16


def kz_of(pencil, place):
    return np.where(
        pencil < 4, 32 * pencil + place, -(32 * (7 - pencil) + 16 + place)
    )


def z_tables():
    pencil, ri, place = np.meshgrid(np.arange(8), np.arange(2), np.arange(KZ), indexing="ij")
    kz = kz_of(pencil, place).reshape(-1)
    ri = ri.reshape(-1)
    shared = (pencil.reshape(-1) == 0) & (place.reshape(-1) == 0)
    z = np.arange(GZ)
    theta = 2 * np.pi * ((z[:, None] * kz[None, :]) % GZ) / GZ
    sign = 1.0 - 2.0 * (z % 2)
    forward = np.where(ri == 0, np.cos(theta), -np.sin(theta))
    forward = np.where(shared & (ri == 1), sign[:, None], forward)
    scale = np.where(shared, 1.0, 2.0) / GZ
    backward = (forward * scale).T
    return forward, backward


def y_tables():
    slab, ro, k8 = (a.reshape(-1) for a in np.meshgrid(np.arange(32), np.arange(2), np.arange(8), indexing="ij"))
    pencil, ri, y32 = (a.reshape(-1) for a in np.meshgrid(np.arange(8), np.arange(2), np.arange(32), indexing="ij"))
    ky = (8 * slab + k8)[:, None]
    ro = ro[:, None]
    y = (32 * pencil + y32)[None, :]
    ri = ri[None, :]
    theta = 2 * np.pi * ((ky * y) % GY) / GY
    cosine, sine = np.cos(theta), np.sin(theta)
    forward = np.where(ro == ri, cosine, np.where(ro == 0, sine, -sine))
    backward = forward.T / GY
    low = (ky > 0) & (ky < 128)
    high = ky > 128
    ends = (ky == 0) | (ky == 128)
    part = np.where(ro == 0, cosine, -sine)
    shared = np.where(low & (ri == 0), part, 0.0)
    shared = np.where(high & (ri == 1), part, shared)
    shared = np.where(ends & (ro == ri), cosine, shared)
    shared_back = (shared * np.where(ends, 1.0, 2.0)).T / GY
    return forward, shared, backward, shared_back


def x_tables():
    k1, ro, ko = (a.reshape(-1)[:, None] for a in np.meshgrid(np.arange(32), np.arange(2), np.arange(8), indexing="ij"))
    slab, ri, ki = (a.reshape(-1)[None, :] for a in np.meshgrid(np.arange(32), np.arange(2), np.arange(8), indexing="ij"))
    theta = 2 * np.pi * ((k1 * slab) % 32) / 32
    rows = np.where(ro == ri, np.cos(theta), np.where(ro == 0, np.sin(theta), -np.sin(theta)))
    rows = rows * (ko == ki)
    x16 = np.arange(16)
    twist = 2 * np.pi * np.arange(32)[:, None] * x16[None, :] / GX
    twist = np.repeat(np.repeat(twist, 8, axis=0), KZ, axis=1)
    inner = 2 * np.pi * ((x16[:, None] * x16[None, :]) % 16) / 16
    eye = np.eye(KZ)
    cosine, sine = np.kron(np.cos(inner), eye), np.kron(np.sin(inner), eye)
    lanes = np.block([[cosine, -sine], [sine, cosine]])
    ro, k1 = (a.reshape(-1)[:, None] for a in np.meshgrid(np.arange(2), np.arange(32), indexing="ij"))
    ri, slab = (a.reshape(-1)[None, :] for a in np.meshgrid(np.arange(2), np.arange(32), indexing="ij"))
    theta = 2 * np.pi * ((k1 * slab) % 32) / 32
    line = np.where(ro == ri, np.cos(theta), np.where(ro == 0, np.sin(theta), -np.sin(theta)))
    line = line * np.where(ri == 1, -1.0, 1.0)
    return rows, np.cos(twist), np.sin(twist), lanes, line


def pair(table):
    high = np.asarray(table, np.float32).astype(jnp.bfloat16)
    low = (np.asarray(table, np.float64) - high.astype(np.float64)).astype(jnp.bfloat16)
    return jnp.asarray(np.stack([high, low]))


def split(value):
    high = value.astype(BF16)
    return high, (value - high.astype(F32)).astype(BF16)


def mm(left, right):
    return jnp.dot(left, right, preferred_element_type=F32)


def mm_nt(left, right):
    return lax.dot_general(left, right, (((1,), (1,)), ((), ())), preferred_element_type=F32)


def mm3(left, right):
    return mm(left[0], right[0]) + (mm(left[0], right[1]) + mm(left[1], right[0]))


class Late:
    def __init__(self, copy, buffer):
        self.copy, self.buffer, self.here = copy, buffer, False

    def __getitem__(self, index):
        if not self.here:
            self.copy.wait()
            self.here = True
        return self.buffer[index]


def call(kernel, out_shape, *args, scratch=(), smem=(), late=(), limit=20):
    spaces = {i: pltpu.SMEM for i in smem} | {i: pltpu.HBM for i in late}
    specs = [pl.BlockSpec(memory_space=spaces.get(i, pltpu.VMEM)) for i in range(len(args))]
    multi = isinstance(out_shape, list)
    out_spec = pl.BlockSpec(memory_space=pltpu.VMEM)
    buffers = [pltpu.VMEM(args[i].shape, args[i].dtype) for i in late]
    if late:
        buffers.append(pltpu.SemaphoreType.DMA((len(late),)))
    own = len(args) + (len(out_shape) if multi else 1) + len(scratch)

    def wrapped(*refs):
        ins = list(refs[: len(args)])
        for place, i in enumerate(late):
            copy = pltpu.make_async_copy(ins[i], refs[own + place], refs[-1].at[place])
            copy.start()
            ins[i] = Late(copy, refs[own + place])
        kernel(*ins, *refs[len(args) : own])

    return pl.pallas_call(
        wrapped,
        out_shape=out_shape,
        in_specs=specs,
        out_specs=[out_spec] * len(out_shape) if multi else out_spec,
        scratch_shapes=list(scratch) + buffers,
        compiler_params=pltpu.CompilerParams(vmem_limit_bytes=limit * 2**20),
        name=kernel.__name__,
    )(*args)


def swap_groups(tiles):
    tiles = list(tiles)
    group = lax.broadcasted_iota(jnp.int32, tiles[0].shape, 1) // 16
    for bit in range(3):
        step = 1 << bit
        upper = (group & step) != 0
        for i in range(8):
            if i & step:
                continue
            low, high = tiles[i], tiles[i + step]
            tiles[i] = jnp.where(upper, pltpu.roll(high, 16 * step, 1), low)
            tiles[i + step] = jnp.where(upper, high, pltpu.roll(low, 128 - 16 * step, 1))
    return tiles


def lookup(tables, index):
    inner, outer = index & 127, index >> 7
    found = jnp.zeros((8, 128), F32)
    for part, table in enumerate(tables):
        row = jnp.broadcast_to(table, (8, 128))
        value = jnp.take_along_axis(row, inner, axis=1, mode="promise_in_bounds")
        found = jnp.where(outer == part, value, found)
    return found


def quotient(value, divisor):
    return ((value.astype(F32) + 0.5) * (1.0 / divisor)).astype(jnp.int32)


def own_slots():
    slab = lax.broadcasted_iota(jnp.int32, (N_SLAB, SLOTS), 0)
    slot = lax.broadcasted_iota(jnp.int32, (N_SLAB, SLOTS), 1)
    return (slot >= slab * CAP) & (slot < slab * CAP + CAP)


def pack(slot_ref, weight_ref, strength_ref, out_ref):
    slots = jnp.broadcast_to(slot_ref[0], (N_SLAB, SLOTS)).astype(F32)
    index = lax.broadcasted_iota(jnp.int32, (SLOTS, 128), 0)
    lane = lax.broadcasted_iota(jnp.int32, (SLOTS, 128), 1)
    spread = jnp.where((lane < CAP) & (quotient(index, CAP) * CAP + lane == index), 1.0, 0.0)
    by_slab = mm(jnp.where(own_slots(), slots, 0.0).astype(BF16), spread.astype(BF16))
    lane = lax.broadcasted_iota(jnp.int32, by_slab.shape, 1)
    by_slab = jnp.where(lane < CAP, by_slab, float(PAN_DEV))
    line = lax.broadcasted_iota(jnp.int32, (ROWS, 128), 0)
    lane = lax.broadcasted_iota(jnp.int32, (ROWS, 128), 1)
    slab = quotient(line, 13)
    place = line - slab * 13
    mine = jnp.where(lane == slab, 1.0, 0.0).astype(BF16)[:, :N_SLAB]
    lines = mm(mine, by_slab.astype(BF16))
    ones = jnp.ones((128, 128), BF16)
    panel = lane.astype(F32)
    hot = []
    for shift in (0, 12):
        pick = lane == jnp.where(place < 12, place + shift, CAP)
        chosen = mm(jnp.where(pick, lines, 0.0).astype(BF16), ones)
        hot += [chosen == panel, chosen == panel + 128.0]
    hot = jnp.where(jnp.concatenate(hot, axis=1), 1.0, 0.0).astype(BF16)
    weight = weight_ref[...]
    empty = jnp.zeros_like(weight)
    values = jnp.concatenate(
        [jnp.concatenate([weight, empty], axis=1), jnp.concatenate([empty, weight], axis=1)], axis=0
    )
    high, low = split(values)
    out_ref[...] = mm_nt(hot, high) + mm_nt(hot, low)
    strength = strength_ref[...]
    tables = [strength[:, :128], strength[:, 128:]]
    index = by_slab.astype(jnp.int32)
    sent = jnp.concatenate([lookup(tables, index[i * 8 : i * 8 + 8]) for i in range(4)], axis=0)
    out_ref[pl.ds(12, N_SLAB, stride=13), :] = sent


def anchor_parts(anchor):
    return anchor >> 13, (anchor >> 8) & 31, anchor & 255


def z_hot(third, dz):
    z = lax.broadcasted_iota(jnp.int32, (GZ, SLOTS), 0)
    return jnp.where(z - dz == third, 1.0, 0.0).astype(BF16)


def y_place(second, y_ref):
    rel = lax.broadcasted_iota(jnp.int32, (PENCIL_ROWS, SLOTS), 0) - second
    y_ref[...] = jnp.where((rel >= 0) & (rel < EDGE), rel, EDGE)


def stencil_row(x, first, weight_ref):
    total = jnp.zeros((32, SLOTS), F32)
    for dx in range(EDGE):
        total = jnp.where(first == x - dx, weight_ref[dx * 32 : dx * 32 + 32, :], total)
    return total


def place_rows(rows, y_ref):
    out = []
    for block in range(PENCIL_ROWS // 8):
        pieces = []
        for lane in range(SLOTS // 128):
            at = slice(lane * 128, lane * 128 + 128)
            index = y_ref[block * 8 : block * 8 + 8, at]
            pieces.append(jnp.take_along_axis(rows[:, at], index, axis=0, mode="promise_in_bounds"))
        out.append(jnp.concatenate(pieces, axis=1))
    return jnp.concatenate(out, axis=0)


def project(arrived_ref, select_ref, spread_ref, order_ref, anchor_ref, z_ref, out_ref, weight_ref, scaled_ref, y_ref, high_ref, low_ref):
    arrived = jnp.concatenate(split(arrived_ref[...]), axis=0)
    select = select_ref[...]
    total = jnp.zeros((256, SLOTS), F32)
    for half in range(2):
        turned = mm_nt(order_ref[half * 128 : half * 128 + 128, :], arrived).astype(BF16)
        turned = jnp.concatenate([turned[:, :ROWS], turned[:, ROWS:]], axis=0)
        total += mm(turned, select[half * ROWS : half * ROWS + ROWS])
    weights = total[:128] + total[128:]
    weight_ref[...] = weights
    high, low = split(arrived_ref[pl.ds(12, N_SLAB, stride=13), :])
    spread = spread_ref[...]
    strength = jnp.where(own_slots(), mm_nt(high, spread) + mm_nt(low, spread), 0.0)
    scaled_ref[...] = weights * jnp.sum(strength, axis=0, keepdims=True)
    first, second, third = anchor_parts(anchor_ref[0])
    y_place(second, y_ref)

    def step(x, carry):
        rows = stencil_row(x, first, scaled_ref)
        for dz in range(EDGE):
            high, low = split(place_rows(rows[dz * 8 : dz * 8 + 8], y_ref))
            at = pl.ds(pl.multiple_of(dz * 512 + x * PENCIL_ROWS, PENCIL_ROWS), PENCIL_ROWS)
            high_ref[at, :] = high
            low_ref[at, :] = low
        return carry

    lax.fori_loop(0, SLAB_ROWS, step, 0)
    hot = z_hot(third, 0)
    charge = jnp.zeros((512, GZ), F32)
    for dz in range(EDGE):
        at = slice(dz * 512, dz * 512 + 512)
        part = mm_nt(high_ref[at, :], hot) + mm_nt(low_ref[at, :], hot)
        charge += pltpu.roll(part, dz, 1) if dz else part
    after = mm3(split(charge), z_ref[...])
    for half in range(2):
        for quarter in range(2):
            tiles = [
                after[x * 32 : x * 32 + 32, quarter * 128 : quarter * 128 + 128]
                for x in range(half * 8, half * 8 + 8)
            ]
            for g, tile in enumerate(swap_groups(tiles)):
                pencil, ri = quarter * 4 + g // 2, g % 2
                start = pencil * 128 + half * 64 + ri * 32
                out_ref[start : start + 32, :] = tile


def gathered(ref, count, rows):
    block = ref[...].reshape(count, 2, rows, 128)
    return jnp.concatenate([block[:, half].reshape(count * rows, 128) for half in range(2)], axis=1)


def scattered(value, ref, count, rows):
    for half in range(2):
        part = value[:, half * 128 : half * 128 + 128].reshape(count, rows, 128)
        for i in range(count):
            ref[(i * 2 + half) * rows : (i * 2 + half + 1) * rows, :] = part[i]


def shared_lane(shape):
    return lax.broadcasted_iota(jnp.int32, shape, 1) % KZ == 0


def y_stage(source, target):
    def kernel(flag_ref, in_ref, table_ref, shared_ref, out_ref, work_ref):
        data = split(gathered(in_ref, *source))
        work_ref[...] = mm3(table_ref[...], data)

        @pl.when(flag_ref[0] == 1)
        def _():
            other = mm3(shared_ref[...], data)
            work_ref[...] = jnp.where(shared_lane(other.shape), other, work_ref[...])

        scattered(work_ref[...], out_ref, *target)

    return kernel


def y_forward(*refs):
    y_stage((8, 64), (32, 16))(*refs)


def y_backward(*refs):
    y_stage((32, 16), (8, 64))(*refs)


def x_stage(flag_ref, in_ref, row_ref, green_ref, other_ref, cos_ref, sin_ref, lane_ref, line_ref, out_ref, re_ref, im_ref):
    row_tables = row_ref[...]
    rows = mm3(row_tables, split(gathered(in_ref, 32, 16))).reshape(32, 2, 8, 256)
    cosine, sine = cos_ref[...], sin_ref[...]
    lane_tables = lane_ref[...]
    line_tables = line_ref[...]

    def lanes_of(re, im, cosine, sine):
        turned = jnp.concatenate([re * cosine + im * sine, im * cosine - re * sine], axis=1)
        return mm3(split(turned), lane_tables)

    full = lanes_of(rows[:, 0].reshape(256, 256), rows[:, 1].reshape(256, 256), cosine, sine)
    green = green_ref[...]
    for half in range(2):
        at = slice(half * 128, half * 128 + 128)
        re_ref[half] = full[:, at] * green[:, at]
        im_ref[half] = full[:, 256 + half * 128 : 384 + half * 128] * green[:, at]

    @pl.when(flag_ref[1] == 1)
    def _():
        line = jnp.concatenate(
            [
                jnp.concatenate([in_ref[pl.ds(half * 16 + ri * 8, 32, stride=32), :] for half in range(2)], axis=1)
                for ri in range(2)
            ],
            axis=0,
        )
        turned = mm3(line_tables, split(line))
        few = (cosine.reshape(32, 8, 256)[:, 0], sine.reshape(32, 8, 256)[:, 0])
        mirror = lanes_of(turned[:32], turned[32:], *few)
        other = other_ref[...]
        rows_at = pl.ds(0, 32, stride=8)
        for half in range(2):
            at = slice(half * 128, half * 128 + 128)
            re_ref[half, rows_at, :] += mirror[:, at] * other[:, at]
            im_ref[half, rows_at, :] += mirror[:, 256 + half * 128 : 384 + half * 128] * other[:, at]

    product = jnp.concatenate([re_ref[0], re_ref[1], -im_ref[0], -im_ref[1]], axis=1)
    back = mm3(split(product), lane_tables)
    re, im = back[:, :256], back[:, 256:]
    re, im = re * cosine + im * sine, im * cosine - re * sine
    rows = jnp.stack([re.reshape(32, 8, 256), im.reshape(32, 8, 256)], axis=1).reshape(512, 256)
    rows = mm3(row_tables, split(rows)).reshape(32, 2, 8, 256) * (1.0 / GX)
    rows = jnp.stack([rows[:, 0], -rows[:, 1]], axis=1).reshape(512, 256)
    scattered(rows, out_ref, 32, 16)


def sample(in_ref, weight_ref, anchor_ref, z_ref, spread_ref, out_ref, y_ref, after_ref, rows_ref, grid_ref):
    for half in range(2):
        for quarter in range(2):
            tiles = []
            for g in range(8):
                pencil, ri = quarter * 4 + g // 2, g % 2
                start = pencil * 128 + half * 64 + ri * 32
                tiles.append(in_ref[start : start + 32, :])
            for i, tile in enumerate(swap_groups(tiles)):
                x = half * 8 + i
                after_ref[x * 32 : x * 32 + 32, quarter * 128 : quarter * 128 + 128] = tile
    high, low = split(mm3(split(after_ref[...]), z_ref[...]))
    first, second, third = anchor_parts(anchor_ref[0])
    y_place(second, y_ref)

    def fill(x, carry):
        rows_ref[pl.ds(pl.multiple_of(x * 32, 32), 32), :] = stencil_row(x, first, weight_ref)
        return carry

    lax.fori_loop(0, SLAB_ROWS, fill, 0)
    total = jnp.zeros((8, SLOTS), F32)
    for dz in range(EDGE):
        hot = z_hot(third, dz)
        grid_ref[...] = mm(high, hot) + mm(low, hot)

        def step(x, total, dz=dz):
            rows = rows_ref[pl.ds(pl.multiple_of(x * 32 + dz * 8, 8), 8), :]
            cells = grid_ref[pl.ds(pl.multiple_of(x * 32, 32), 32), :] * place_rows(rows, y_ref)
            return total + jnp.sum(cells.reshape(4, 8, SLOTS), axis=0)

        total = lax.fori_loop(0, SLAB_ROWS, step, total)
    far = jnp.sum(total, axis=0, keepdims=True)
    high, low = split(jnp.where(own_slots(), jnp.broadcast_to(far, (N_SLAB, SLOTS)), 0.0))
    out_ref[...] = mm(high, spread_ref[...]) + mm(low, spread_ref[...])


def near(low_ref, own_ref, high_ref, index_ref, factor_ref, out_ref):
    table = jnp.concatenate([low_ref[...], own_ref[...], high_ref[...]], axis=1)
    tables = [table[:, part * 128 : part * 128 + 128] for part in range(6)]
    for lane in range(2):
        total = jnp.zeros((8, 128), F32)
        for block in range(4):
            at = (slice(block * 8, block * 8 + 8), slice(lane * 128, lane * 128 + 128))
            total += lookup(tables, index_ref[at]) * factor_ref[at]
        out_ref[:, lane * 128 : lane * 128 + 128] = jnp.sum(total, axis=0, keepdims=True)


def finish(far_ref, spread_ref, own_ref, slot_ref, near_ref, out_ref):
    high, low = split(far_ref[...])
    own = own_ref[...]
    rows = (mm(own, high) + mm(own, low)) * spread_ref[...].astype(F32)
    column = jnp.sum(rows, axis=1, keepdims=True)
    slots = jnp.transpose(jnp.broadcast_to(slot_ref[0], (128, SLOTS)))
    panel = lax.broadcasted_iota(jnp.int32, (SLOTS, 128), 1)
    for lane in range(2):
        part = jnp.where(slots == panel + lane * 128, column, 0.0)
        at = slice(lane * 128, lane * 128 + 128)
        out_ref[:, at] = jnp.sum(part, axis=0, keepdims=True) + near_ref[:, at]


def swap(value, axis, count):
    rows = value.shape[0]
    return lax.all_to_all(value.reshape(count, rows // count, 128), axis, 0, 0, tiled=True).reshape(rows, 128)


def arrange_green(green, slab, pencil):
    plane = lax.ppermute(green[:, 0, :], "pencil", [(4, 0)])
    chosen = jnp.where(pencil < 4, green[:, :KZ], jnp.flip(green[:, 1 : KZ + 1], axis=1))
    zero = chosen[:, 0, :]
    line = lax.broadcasted_iota(jnp.int32, zero.shape, 0) == 0
    ends = line & ((slab == 0) | (slab == 16))
    both = jnp.where(ends, 0.5 * (zero + plane), jnp.where(slab >= 16, plane, zero))
    both = jnp.where(pencil == 0, both, zero)
    differ = jnp.where(ends & (pencil == 0), 0.5 * (zero - plane), 0.0)
    place = lax.broadcasted_iota(jnp.int32, chosen.shape, 1) == 0
    chosen = jnp.where(place, both[:, None, :], chosen)
    chosen = chosen.reshape(8, KZ, 16, 32).transpose(3, 0, 2, 1).reshape(256, 256)
    first = lax.broadcasted_iota(jnp.int32, (32, 16, KZ), 2) == 0
    other = jnp.where(first, differ[0].reshape(16, 32).T[:, :, None], 0.0).reshape(32, 256)
    return chosen, other


def slot_tables():
    order = np.zeros((256, 128))
    for half in range(2):
        for dx in range(4):
            for dy in range(4):
                for dz in range(4):
                    order[half * 128 + dx * 32 + dz * 8 + dy, half * 64 + dx * 16 + dy * 4 + dz] = 1.0
    index = np.arange(SLOTS)
    spread = (index % CAP)[:, None] == np.arange(128)[None, :]
    own = (index // CAP)[:, None] == np.arange(N_SLAB)[None, :]
    line = np.arange(ROWS)
    place, target = line % 13, line // 13 * CAP + line % 13
    select = np.concatenate(
        [(place[:, None] < 12) & (index[None, :] == (target + shift)[:, None]) for shift in (0, 12)]
    )
    return [jnp.asarray(t, BF16) for t in (order, spread, own, select)]


def per_device(strength, stencil_weight, slot_panel, slot_anchor, green_spectrum, near_index, near_factor):
    slab = lax.axis_index("slab")
    pencil = lax.axis_index("pencil")
    flags = jnp.stack([pencil == 0, (pencil == 0) & ((slab == 0) | (slab == 16))]).astype(jnp.int32)
    row = strength.reshape(1, PAN_DEV)

    z_fwd, z_bwd = (pair(t) for t in z_tables())
    y_fwd, y_fwd_shared, y_bwd, y_bwd_shared = (pair(t) for t in y_tables())
    rows, cosine, sine, lanes, line = x_tables()
    rows, lanes, line = (pair(t) for t in (rows, lanes, line))
    cosine, sine = jnp.asarray(cosine, F32), jnp.asarray(sine, F32)
    order, spread, own, select = slot_tables()

    shape = jax.ShapeDtypeStruct
    payload = call(
        pack, shape((ROWS, 128), F32), slot_panel, stencil_weight, row, limit=56)
    arrived = lax.all_to_all(payload.reshape(N_SLAB, 1, 13 * 128), "slab", 0, 0, tiled=True).reshape(ROWS, 128)
    after_z, weights = call(
        project, [shape((1024, 128), F32), shape((128, SLOTS), F32)], arrived, select, spread, order, slot_anchor, z_fwd,
        scratch=[pltpu.VMEM((128, SLOTS), F32), pltpu.VMEM((PENCIL_ROWS, SLOTS), jnp.int32)]
        + [pltpu.VMEM((EDGE * 512, SLOTS), BF16)] * 2,
        late=(5,), limit=54,
    )
    by_y = swap(after_z, "pencil", N_PENCIL)
    after_y = call(
        y_forward, shape((1024, 128), F32), flags, by_y, y_fwd, y_fwd_shared,
        scratch=[pltpu.VMEM((512, 256), F32)], smem=(0,), limit=40,
    )
    by_x = swap(after_y, "slab", N_SLAB)
    green, other = arrange_green(green_spectrum, slab, pencil)
    after_x = call(
        x_stage, shape((1024, 128), F32), flags, by_x, rows, green, other, cosine, sine, lanes, line,
        scratch=[pltpu.VMEM((2, 256, 128), F32)] * 2, smem=(0,), late=range(5, 9), limit=56,
    )
    forward = [(i, (i + 1) % N_SLAB) for i in range(N_SLAB)]
    backward = [(target, source) for source, target in forward]
    low = lax.ppermute(row, "slab", forward)
    high = lax.ppermute(row, "slab", backward)
    near_field = call(near, shape((1, PAN_DEV), F32), low, row, high, near_index, near_factor, limit=40)
    back_x = swap(after_x, "slab", N_SLAB)
    back_y = call(
        y_backward, shape((1024, 128), F32), flags, back_x, y_bwd, y_bwd_shared,
        scratch=[pltpu.VMEM((512, 256), F32)], smem=(0,), limit=40,
    )
    back_y, near_field = lax.optimization_barrier((back_y, near_field))
    by_z = swap(back_y, "pencil", N_PENCIL)
    sampled = call(
        sample, shape((N_SLAB, 128), F32), by_z, weights, slot_anchor, z_bwd, spread,
        scratch=[pltpu.VMEM((PENCIL_ROWS, SLOTS), jnp.int32), pltpu.VMEM((512, 256), F32)]
        + [pltpu.VMEM((512, SLOTS), F32)] * 2,
        limit=40,
    )
    far = lax.all_to_all(sampled, "slab", 0, 0, tiled=True)
    return call(finish, shape((1, PAN_DEV), F32), far, spread, own, slot_panel, near_field, limit=40).reshape(PAN_DEV)


def solution(mesh):
    in_specs = (
        P(("slab", "pencil")),
        P(None, ("slab", "pencil")),
        P("slab", "pencil", None),
        P("slab", "pencil", None),
        P("slab", "pencil", None),
        P(None, ("slab", "pencil")),
        P(None, ("slab", "pencil")),
    )
    out_specs = P(("slab", "pencil"))
    return jax.shard_map(
        per_device, mesh=mesh, in_specs=in_specs, out_specs=out_specs, check_vma=False
    )
```

```python
import math

import jax
import jax.numpy as jnp
import numpy as np
from jax import lax
from jax.experimental import pallas as pl
from jax.experimental.pallas import tpu as pltpu
from jax.sharding import PartitionSpec as P

GX = 512
GY = 256
GZ = 256
EDGE = 4
PAN_DEV = 256
CAP = 24
N_SLAB = 32
N_PENCIL = 8
SLOTS = N_SLAB * CAP
SLAB_ROWS = 16
PENCIL_ROWS = 32
KZ = 16
ROWS = 13 * N_SLAB
LIMIT_P, LIMIT_Y, LIMIT_X, LIMIT_S = 48, 40, 51, 40
LIMIT_N = 40
F32 = jnp.float32
BF16 = jnp.bfloat16


def kz_of(pencil, place):
    return np.where(
        pencil < 4, 32 * pencil + place, -(32 * (7 - pencil) + 16 + place)
    )


def z_tables():
    pencil, ri, place = np.meshgrid(np.arange(8), np.arange(2), np.arange(KZ), indexing="ij")
    kz = kz_of(pencil, place).reshape(-1)
    ri = ri.reshape(-1)
    shared = (pencil.reshape(-1) == 0) & (place.reshape(-1) == 0)
    z = np.arange(GZ)
    theta = 2 * np.pi * ((z[:, None] * kz[None, :]) % GZ) / GZ
    sign = 1.0 - 2.0 * (z % 2)
    forward = np.where(ri == 0, np.cos(theta), -np.sin(theta))
    forward = np.where(shared & (ri == 1), sign[:, None], forward)
    scale = np.where(shared, 1.0, 2.0) / GZ
    backward = (forward * scale).T
    return forward, backward


def y_tables():
    slab, ro, k8 = (a.reshape(-1) for a in np.meshgrid(np.arange(32), np.arange(2), np.arange(8), indexing="ij"))
    pencil, ri, y32 = (a.reshape(-1) for a in np.meshgrid(np.arange(8), np.arange(2), np.arange(32), indexing="ij"))
    ky = (8 * slab + k8)[:, None]
    ro = ro[:, None]
    y = (32 * pencil + y32)[None, :]
    ri = ri[None, :]
    theta = 2 * np.pi * ((ky * y) % GY) / GY
    cosine, sine = np.cos(theta), np.sin(theta)
    forward = np.where(ro == ri, cosine, np.where(ro == 0, sine, -sine))
    backward = forward.T / GY
    low = (ky > 0) & (ky < 128)
    high = ky > 128
    ends = (ky == 0) | (ky == 128)
    part = np.where(ro == 0, cosine, -sine)
    shared = np.where(low & (ri == 0), part, 0.0)
    shared = np.where(high & (ri == 1), part, shared)
    shared = np.where(ends & (ro == ri), cosine, shared)
    shared_back = (shared * np.where(ends, 1.0, 2.0)).T / GY
    return forward, shared, backward, shared_back


def x_tables():
    k1, ro, ko = (a.reshape(-1)[:, None] for a in np.meshgrid(np.arange(32), np.arange(2), np.arange(8), indexing="ij"))
    slab, ri, ki = (a.reshape(-1)[None, :] for a in np.meshgrid(np.arange(32), np.arange(2), np.arange(8), indexing="ij"))
    theta = 2 * np.pi * ((k1 * slab) % 32) / 32
    rows = np.where(ro == ri, np.cos(theta), np.where(ro == 0, np.sin(theta), -np.sin(theta)))
    rows = rows * (ko == ki)
    x16 = np.arange(16)
    twist = 2 * np.pi * np.arange(32)[:, None] * x16[None, :] / GX
    twist = np.repeat(twist, KZ, axis=1)
    inner = 2 * np.pi * ((x16[:, None] * x16[None, :]) % 16) / 16
    eye = np.eye(KZ)
    cosine, sine = np.kron(np.cos(inner), eye), np.kron(np.sin(inner), eye)
    lanes = np.block([[cosine, -sine], [sine, cosine]])
    ro, k1 = (a.reshape(-1)[:, None] for a in np.meshgrid(np.arange(2), np.arange(32), indexing="ij"))
    ri, slab = (a.reshape(-1)[None, :] for a in np.meshgrid(np.arange(2), np.arange(32), indexing="ij"))
    theta = 2 * np.pi * ((k1 * slab) % 32) / 32
    line = np.where(ro == ri, np.cos(theta), np.where(ro == 0, np.sin(theta), -np.sin(theta)))
    line = line * np.where(ri == 1, -1.0, 1.0)
    return rows, np.stack([np.cos(twist), np.sin(twist)]), lanes, line


def pair(table):
    high = np.asarray(table, np.float32).astype(jnp.bfloat16)
    low = (np.asarray(table, np.float64) - high.astype(np.float64)).astype(jnp.bfloat16)
    return jnp.asarray(np.stack([high, low]))


def split(value):
    high = value.astype(BF16)
    return high, (value - high.astype(F32)).astype(BF16)


def mm(left, right):
    return jnp.dot(left, right, preferred_element_type=F32)


def mm_nt(left, right):
    return lax.dot_general(left, right, (((1,), (1,)), ((), ())), preferred_element_type=F32)


def mm3(left, right):
    return mm(left[0], right[0]) + (mm(left[0], right[1]) + mm(left[1], right[0]))


class Late:
    def __init__(self, copy, buffer):
        self.copy, self.buffer, self.here = copy, buffer, False

    def __getitem__(self, index):
        if not self.here:
            self.copy.wait()
            self.here = True
        return self.buffer[index]


def call(kernel, out_shape, *args, scratch=(), smem=(), late=(), limit=20):
    spaces = {i: pltpu.SMEM for i in smem} | {i: pltpu.HBM for i in late}
    specs = [pl.BlockSpec(memory_space=spaces.get(i, pltpu.VMEM)) for i in range(len(args))]
    multi = isinstance(out_shape, list)
    out_spec = pl.BlockSpec(memory_space=pltpu.VMEM)
    buffers = [pltpu.VMEM(args[i].shape, args[i].dtype) for i in late]
    if late:
        buffers.append(pltpu.SemaphoreType.DMA((len(late),)))
    own = len(args) + (len(out_shape) if multi else 1) + len(scratch)

    def wrapped(*refs):
        ins = list(refs[: len(args)])
        for place, i in enumerate(late):
            copy = pltpu.make_async_copy(ins[i], refs[own + place], refs[-1].at[place])
            copy.start()
            ins[i] = Late(copy, refs[own + place])
        kernel(*ins, *refs[len(args) : own])

    return pl.pallas_call(
        wrapped,
        out_shape=out_shape,
        in_specs=specs,
        out_specs=[out_spec] * len(out_shape) if multi else out_spec,
        scratch_shapes=list(scratch) + buffers,
        compiler_params=pltpu.CompilerParams(vmem_limit_bytes=limit * 2**20),
        name=kernel.__name__,
    )(*args)


def swap_groups(tiles):
    tiles = list(tiles)
    group = lax.broadcasted_iota(jnp.int32, tiles[0].shape, 1) // 16
    for bit in range(3):
        step = 1 << bit
        upper = (group & step) != 0
        for i in range(8):
            if i & step:
                continue
            low, high = tiles[i], tiles[i + step]
            tiles[i] = jnp.where(upper, pltpu.roll(high, 16 * step, 1), low)
            tiles[i + step] = jnp.where(upper, high, pltpu.roll(low, 128 - 16 * step, 1))
    return tiles


def lookup(tables, index):
    inner, outer = index & 127, index >> 7
    found = jnp.zeros((8, 128), F32)
    for part, table in enumerate(tables):
        row = jnp.broadcast_to(table, (8, 128))
        value = jnp.take_along_axis(row, inner, axis=1, mode="promise_in_bounds")
        found = jnp.where(outer == part, value, found)
    return found


def quotient(value, divisor):
    return ((value.astype(F32) + 0.5) * (1.0 / divisor)).astype(jnp.int32)


def own_slots(width, slots):
    slab = lax.broadcasted_iota(jnp.int32, (N_SLAB, slots), 0)
    slot = lax.broadcasted_iota(jnp.int32, (N_SLAB, slots), 1)
    return (slot >= slab * width) & (slot < slab * width + width)


def received_slots():
    own = own_slots(CAP // 2, SLOTS // 2)
    return jnp.concatenate([own, own], axis=1)


def pack(slot_ref, weight_ref, strength_ref, out_ref):
    slots = jnp.broadcast_to(slot_ref[0], (N_SLAB, SLOTS)).astype(F32)
    index = lax.broadcasted_iota(jnp.int32, (SLOTS, 128), 0)
    lane = lax.broadcasted_iota(jnp.int32, (SLOTS, 128), 1)
    spread = jnp.where((lane < CAP) & (quotient(index, CAP) * CAP + lane == index), 1.0, 0.0)
    by_slab = mm(jnp.where(own_slots(CAP, SLOTS), slots, 0.0).astype(BF16), spread.astype(BF16))
    lane = lax.broadcasted_iota(jnp.int32, by_slab.shape, 1)
    by_slab = jnp.where(lane < CAP, by_slab, float(PAN_DEV))
    line = lax.broadcasted_iota(jnp.int32, (ROWS, 128), 0)
    lane = lax.broadcasted_iota(jnp.int32, (ROWS, 128), 1)
    slab = quotient(line, 13)
    place = line - slab * 13
    mine = jnp.where(lane == slab, 1.0, 0.0).astype(BF16)[:, :N_SLAB]
    lines = mm(mine, by_slab.astype(BF16))
    ones = jnp.ones((128, 128), BF16)
    panel = lane.astype(F32)
    hot = []
    for shift in (0, 12):
        pick = lane == jnp.where(place < 12, place + shift, CAP)
        chosen = mm(jnp.where(pick, lines, 0.0).astype(BF16), ones)
        hot += [chosen == panel, chosen == panel + 128.0]
    hot = jnp.where(jnp.concatenate(hot, axis=1), 1.0, 0.0).astype(BF16)
    weight = weight_ref[...]
    empty = jnp.zeros_like(weight)
    values = jnp.concatenate(
        [jnp.concatenate([weight, empty], axis=1), jnp.concatenate([empty, weight], axis=1)], axis=0
    )
    high, low = split(values)
    out_ref[...] = mm_nt(hot, high) + mm_nt(hot, low)
    strength = strength_ref[...]
    tables = [strength[:, :128], strength[:, 128:]]
    index = by_slab.astype(jnp.int32)
    sent = jnp.concatenate([lookup(tables, index[i * 8 : i * 8 + 8]) for i in range(4)], axis=0)
    out_ref[pl.ds(12, N_SLAB, stride=13), :] = sent


def anchor_parts(anchor):
    return anchor >> 13, (anchor >> 8) & 31, anchor & 255


def z_hot(third, dz):
    z = lax.broadcasted_iota(jnp.int32, (GZ, SLOTS), 0)
    return jnp.where(z - dz == third, 1.0, 0.0).astype(BF16)


def y_place(second, y_ref):
    rel = lax.broadcasted_iota(jnp.int32, (PENCIL_ROWS, SLOTS), 0) - second
    y_ref[...] = jnp.where((rel >= 0) & (rel < EDGE), rel, EDGE)


def stencil_row(x, first, weight_ref):
    total = jnp.zeros((32, SLOTS), F32)
    for dx in range(EDGE):
        total = jnp.where(first == x - dx, weight_ref[dx * 32 : dx * 32 + 32, :], total)
    return total


def place_rows(rows, y_ref):
    out = []
    for block in range(PENCIL_ROWS // 8):
        pieces = []
        for lane in range(SLOTS // 128):
            at = slice(lane * 128, lane * 128 + 128)
            index = y_ref[block * 8 : block * 8 + 8, at]
            pieces.append(jnp.take_along_axis(rows[:, at], index, axis=0, mode="promise_in_bounds"))
        out.append(jnp.concatenate(pieces, axis=1))
    return jnp.concatenate(out, axis=0)


def fill_rows(rows_ref, first, weight_ref):
    def step(x, carry):
        rows_ref[pl.ds(pl.multiple_of(x * 32, 32), 32), :] = stencil_row(x, first, weight_ref)
        return carry

    lax.fori_loop(0, SLAB_ROWS, step, 0)


def slot_order():
    row = lax.broadcasted_iota(jnp.int32, (256, 128), 0)
    lane = lax.broadcasted_iota(jnp.int32, (256, 128), 1)
    dy = row & 7
    picked = ((row >> 5) << 4) + (dy << 2) + ((row >> 3) & 3)
    return jnp.where((lane == picked) & (dy < EDGE), 1.0, 0.0).astype(BF16)


def project(arrived_ref, spread_ref, anchor_ref, z_ref, out_ref, weight_ref, scaled_ref, y_ref, rows_ref, packed_ref, high_ref, low_ref):
    for s in range(N_SLAB):
        packed_ref[s * 12 : s * 12 + 12, :] = arrived_ref[s * 13 : s * 13 + 12, :]
    packed = jnp.concatenate(split(packed_ref[...]), axis=0)
    order = slot_order()
    turned = [mm_nt(order[half * 128 : half * 128 + 128, :], packed) for half in range(2)]
    turned = [part[:, : SLOTS // 2] + part[:, SLOTS // 2 :] for part in turned]
    weights = jnp.concatenate(turned, axis=1)
    weight_ref[...] = weights
    high, low = split(arrived_ref[pl.ds(12, N_SLAB, stride=13), :])
    spread = spread_ref[...]
    strength = jnp.where(received_slots(), mm_nt(high, spread) + mm_nt(low, spread), 0.0)
    scaled_ref[...] = weights * jnp.sum(strength, axis=0, keepdims=True)
    first, second, third = anchor_parts(anchor_ref[0])
    y_place(second, y_ref)
    fill_rows(rows_ref, first, scaled_ref)
    hot = z_hot(third, 0)
    charge = jnp.zeros((512, GZ), F32)
    for dz in range(EDGE):
        for x in range(SLAB_ROWS):
            at = slice(x * PENCIL_ROWS, x * PENCIL_ROWS + PENCIL_ROWS)
            high, low = split(place_rows(rows_ref[x * 32 + dz * 8 : x * 32 + dz * 8 + 8, :], y_ref))
            high_ref[dz, at, :] = high
            low_ref[dz, at, :] = low
        part = mm_nt(high_ref[dz], hot) + mm_nt(low_ref[dz], hot)
        charge += pltpu.roll(part, dz, 1) if dz else part
    after = mm3(split(charge), z_ref[...])
    for half in range(2):
        for quarter in range(2):
            tiles = [
                after[x * 32 : x * 32 + 32, quarter * 128 : quarter * 128 + 128]
                for x in range(half * 8, half * 8 + 8)
            ]
            for g, tile in enumerate(swap_groups(tiles)):
                pencil, ri = quarter * 4 + g // 2, g % 2
                start = pencil * 128 + half * 64 + ri * 32
                out_ref[start : start + 32, :] = tile


def gathered(ref, count, rows):
    block = ref[...].reshape(count, 2, rows, 128)
    return jnp.concatenate([block[:, half].reshape(count * rows, 128) for half in range(2)], axis=1)


def scattered(value, ref, count, rows):
    for half in range(2):
        part = value[:, half * 128 : half * 128 + 128].reshape(count, rows, 128)
        for i in range(count):
            ref[(i * 2 + half) * rows : (i * 2 + half + 1) * rows, :] = part[i]


def shared_lane(shape):
    return lax.broadcasted_iota(jnp.int32, shape, 1) % KZ == 0


def y_stage(source, target):
    def kernel(flag_ref, in_ref, table_ref, shared_ref, out_ref, work_ref):
        data = split(gathered(in_ref, *source))
        work_ref[...] = mm3(table_ref[...], data)

        @pl.when(flag_ref[0] == 1)
        def _():
            other = mm3(shared_ref[...], data)
            work_ref[...] = jnp.where(shared_lane(other.shape), other, work_ref[...])

        scattered(work_ref[...], out_ref, *target)

    return kernel


def y_forward(*refs):
    y_stage((8, 64), (32, 16))(*refs)


def y_backward(*refs):
    y_stage((32, 16), (8, 64))(*refs)


def x_stage(flag_ref, in_ref, row_ref, green_ref, other_ref, twist_ref, lane_ref, line_ref, out_ref, re_ref, im_ref):
    row_tables = row_ref[...]
    rows = mm3(row_tables, split(gathered(in_ref, 32, 16))).reshape(32, 2, 8, 256)
    few = twist_ref[0], twist_ref[1]
    cosine, sine = (
        jnp.concatenate([jnp.broadcast_to(part[k : k + 1], (8, 256)) for k in range(32)], axis=0) for part in few
    )
    lane_tables = lane_ref[...]
    line_tables = line_ref[...]

    def lanes_of(re, im, cosine, sine):
        turned = jnp.concatenate([re * cosine + im * sine, im * cosine - re * sine], axis=1)
        return mm3(split(turned), lane_tables)

    full = lanes_of(rows[:, 0].reshape(256, 256), rows[:, 1].reshape(256, 256), cosine, sine)
    green = green_ref[...]
    for half in range(2):
        at = slice(half * 128, half * 128 + 128)
        re_ref[half] = full[:, at] * green[:, at]
        im_ref[half] = full[:, 256 + half * 128 : 384 + half * 128] * green[:, at]

    @pl.when(flag_ref[1] == 1)
    def _():
        line = jnp.concatenate(
            [
                jnp.concatenate([in_ref[pl.ds(half * 16 + ri * 8, 32, stride=32), :] for half in range(2)], axis=1)
                for ri in range(2)
            ],
            axis=0,
        )
        turned = mm3(line_tables, split(line))
        mirror = lanes_of(turned[:32], turned[32:], *few)
        other = other_ref[...]
        rows_at = pl.ds(0, 32, stride=8)
        for half in range(2):
            at = slice(half * 128, half * 128 + 128)
            re_ref[half, rows_at, :] += mirror[:, at] * other[:, at]
            im_ref[half, rows_at, :] += mirror[:, 256 + half * 128 : 384 + half * 128] * other[:, at]

    product = jnp.concatenate([re_ref[0], re_ref[1], -im_ref[0], -im_ref[1]], axis=1)
    back = mm3(split(product), lane_tables)
    re, im = back[:, :256], back[:, 256:]
    re, im = re * cosine + im * sine, im * cosine - re * sine
    rows = jnp.stack([re.reshape(32, 8, 256), im.reshape(32, 8, 256)], axis=1).reshape(512, 256)
    rows = mm3(row_tables, split(rows)).reshape(32, 2, 8, 256) * (1.0 / GX)
    rows = jnp.stack([rows[:, 0], -rows[:, 1]], axis=1).reshape(512, 256)
    scattered(rows, out_ref, 32, 16)


def sample(in_ref, weight_ref, anchor_ref, z_ref, spread_ref, out_ref, y_ref, after_ref, rows_ref, grid_ref):
    for half in range(2):
        for quarter in range(2):
            tiles = []
            for g in range(8):
                pencil, ri = quarter * 4 + g // 2, g % 2
                start = pencil * 128 + half * 64 + ri * 32
                tiles.append(in_ref[start : start + 32, :])
            for i, tile in enumerate(swap_groups(tiles)):
                x = half * 8 + i
                after_ref[x * 32 : x * 32 + 32, quarter * 128 : quarter * 128 + 128] = tile
    high, low = split(mm3(split(after_ref[...]), z_ref[...]))
    first, second, third = anchor_parts(anchor_ref[0])
    y_place(second, y_ref)

    fill_rows(rows_ref, first, weight_ref)
    total = jnp.zeros((8, SLOTS), F32)
    for dz in range(EDGE):
        hot = z_hot(third, dz)
        grid_ref[dz] = mm(high, hot) + mm(low, hot)
        for x in range(SLAB_ROWS):
            rows = rows_ref[x * 32 + dz * 8 : x * 32 + dz * 8 + 8, :]
            cells = grid_ref[dz, x * 32 : x * 32 + 32, :] * place_rows(rows, y_ref)
            total += jnp.sum(cells.reshape(4, 8, SLOTS), axis=0)
    far = jnp.sum(total, axis=0, keepdims=True)
    high, low = split(jnp.where(received_slots(), jnp.broadcast_to(far, (N_SLAB, SLOTS)), 0.0))
    out_ref[...] = mm(high, spread_ref[...]) + mm(low, spread_ref[...])


def near(low_ref, own_ref, high_ref, index_ref, factor_ref, out_ref):
    table = jnp.concatenate([low_ref[...], own_ref[...], high_ref[...]], axis=1)
    tables = [table[:, part * 128 : part * 128 + 128] for part in range(6)]
    for lane in range(2):
        total = jnp.zeros((8, 128), F32)
        for block in range(4):
            at = (slice(block * 8, block * 8 + 8), slice(lane * 128, lane * 128 + 128))
            total += lookup(tables, index_ref[at]) * factor_ref[at]
        out_ref[:, lane * 128 : lane * 128 + 128] = jnp.sum(total, axis=0, keepdims=True)


def finish(far_ref, spread_ref, own_ref, slot_ref, near_ref, out_ref):
    high, low = split(far_ref[...])
    own = own_ref[...]
    rows = (mm(own, high) + mm(own, low)) * spread_ref[...].astype(F32)
    column = jnp.sum(rows, axis=1, keepdims=True)
    slots = jnp.transpose(jnp.broadcast_to(slot_ref[0], (128, SLOTS)))
    panel = lax.broadcasted_iota(jnp.int32, (SLOTS, 128), 1)
    for lane in range(2):
        part = jnp.where(slots == panel + lane * 128, column, 0.0)
        at = slice(lane * 128, lane * 128 + 128)
        out_ref[:, at] = jnp.sum(part, axis=0, keepdims=True) + near_ref[:, at]


def swap(value, axis, count):
    rows = value.shape[0]
    return lax.all_to_all(value.reshape(count, rows // count, 128), axis, 0, 0, tiled=True).reshape(rows, 128)


def arrange_green(green, plane, slab, pencil):
    chosen = jnp.where(pencil < 4, green[:, :KZ], jnp.flip(green[:, 1 : KZ + 1], axis=1))
    zero = chosen[:, 0, :]
    line = np.tile(np.arange(8)[:, None] == 0, (1, GX))
    ends = line & ((slab == 0) | (slab == 16))
    both = jnp.where(ends, 0.5 * (zero + plane), jnp.where(slab >= 16, plane, zero))
    both = jnp.where(pencil == 0, both, zero)
    differ = jnp.where(ends & (pencil == 0), 0.5 * (zero - plane), 0.0)
    place = np.tile(np.arange(KZ)[None, :, None] == 0, (8, 1, GX))
    chosen = jnp.where(place, both[:, None, :], chosen)
    chosen = chosen.reshape(8, KZ, 16, 32).transpose(3, 0, 2, 1).reshape(256, 256)
    first = np.tile(np.arange(KZ)[None, None, :] == 0, (32, 16, 1))
    other = jnp.where(first, differ[0].reshape(16, 32).T[:, :, None], 0.0).reshape(32, 256)
    return chosen, other


def slot_tables():
    index = np.arange(SLOTS)
    lane = np.arange(128)[None, :]
    spread = (index % CAP)[:, None] == lane
    own = (index // CAP)[:, None] == np.arange(N_SLAB)[None, :]
    received = (index // (SLOTS // 2) * 12 + index % 12)[:, None] == lane
    return [jnp.asarray(t, BF16) for t in (spread, own, received)]


def per_device(strength, stencil_weight, slot_panel, slot_anchor, green_spectrum, near_index, near_factor):
    slab = lax.axis_index("slab")
    pencil = lax.axis_index("pencil")
    flags = jnp.stack([pencil == 0, (pencil == 0) & ((slab == 0) | (slab == 16))]).astype(jnp.int32)
    row = strength.reshape(1, PAN_DEV)

    z_fwd, z_bwd = (pair(t) for t in z_tables())
    y_fwd, y_fwd_shared, y_bwd, y_bwd_shared = (pair(t) for t in y_tables())
    rows, twist, lanes, line = x_tables()
    rows, lanes, line = (pair(t) for t in (rows, lanes, line))
    twist = jnp.asarray(twist, F32)
    spread, own, received = slot_tables()

    anchor = slot_anchor.reshape(N_SLAB, 2, 12).transpose(1, 0, 2).reshape(1, 1, SLOTS)

    shape = jax.ShapeDtypeStruct
    payload = call(
        pack, shape((ROWS, 128), F32), slot_panel, stencil_weight, row, limit=56)

    payload, spectrum = lax.optimization_barrier((payload, green_spectrum))
    plane = lax.ppermute(spectrum[:, 0, :], "pencil", [(4, 0)])
    arrived = lax.all_to_all(payload.reshape(N_SLAB, 1, 13 * 128), "slab", 0, 0, tiled=True).reshape(ROWS, 128)
    arrived, plane, flags, anchor = lax.optimization_barrier((arrived, plane, flags, anchor))
    after_z, weights = call(
        project, [shape((1024, 128), F32), shape((128, SLOTS), F32)], arrived, received, anchor, z_fwd,
        scratch=[pltpu.VMEM((128, SLOTS), F32), pltpu.VMEM((PENCIL_ROWS, SLOTS), jnp.int32)]
        + [pltpu.VMEM((512, SLOTS), F32), pltpu.VMEM((SLOTS // 2, 128), F32)]
        + [pltpu.VMEM((EDGE, 512, SLOTS), BF16)] * 2,
        late=(3,), limit=LIMIT_P,
    )
    by_y = swap(after_z, "pencil", N_PENCIL)
    after_y = call(
        y_forward, shape((1024, 128), F32), flags, by_y, y_fwd, y_fwd_shared,
        scratch=[pltpu.VMEM((512, 256), F32)], smem=(0,), limit=LIMIT_Y,
    )
    by_x = swap(after_y, "slab", N_SLAB)
    after_y, green_spectrum, slab, pencil = lax.optimization_barrier((after_y, green_spectrum, slab, pencil))
    green, other = arrange_green(green_spectrum, plane, slab, pencil)
    green, strengths = lax.optimization_barrier((green, row))
    forward = [(i, (i + 1) % N_SLAB) for i in range(N_SLAB)]
    backward = [(target, source) for source, target in forward]
    low = lax.ppermute(strengths, "slab", forward)
    high = lax.ppermute(strengths, "slab", backward)
    near_field = call(near, shape((1, PAN_DEV), F32), low, row, high, near_index, near_factor, limit=LIMIT_N)
    by_x, near_field = lax.optimization_barrier((by_x, near_field))
    after_x = call(
        x_stage, shape((1024, 128), F32), flags, by_x, rows, green, other, twist, lanes, line,
        scratch=[pltpu.VMEM((2, 256, 128), F32)] * 2, smem=(0,), late=range(5, 8), limit=LIMIT_X,
    )
    back_x = swap(after_x, "slab", N_SLAB)
    back_y = call(
        y_backward, shape((1024, 128), F32), flags, back_x, y_bwd, y_bwd_shared,
        scratch=[pltpu.VMEM((512, 256), F32)], smem=(0,), limit=LIMIT_Y,
    )
    by_z = swap(back_y, "pencil", N_PENCIL)
    sampled = call(
        sample, shape((N_SLAB, 128), F32), by_z, weights, anchor, z_bwd, received,
        scratch=[pltpu.VMEM((PENCIL_ROWS, SLOTS), jnp.int32), pltpu.VMEM((512, 256), F32)]
        + [pltpu.VMEM((512, SLOTS), F32), pltpu.VMEM((EDGE, 512, SLOTS), F32)],
        limit=LIMIT_S,
    )
    far = lax.all_to_all(sampled, "slab", 0, 0, tiled=True)
    return call(finish, shape((1, PAN_DEV), F32), far, spread, own, slot_panel, near_field, limit=40).reshape(PAN_DEV)


def solution(mesh):
    in_specs = (
        P(("slab", "pencil")),
        P(None, ("slab", "pencil")),
        P("slab", "pencil", None),
        P("slab", "pencil", None),
        P("slab", "pencil", None),
        P(None, ("slab", "pencil")),
        P(None, ("slab", "pencil")),
    )
    out_specs = P(("slab", "pencil"))
    return jax.shard_map(
        per_device, mesh=mesh, in_specs=in_specs, out_specs=out_specs, check_vma=False
    )
```

```python
import math

import jax
import jax.numpy as jnp
import numpy as np
from jax import lax
from jax.experimental import pallas as pl
from jax.experimental.pallas import tpu as pltpu
from jax.sharding import PartitionSpec as P

GX = 512
GY = 256
GZ = 256
EDGE = 4
PAN_DEV = 256
CAP = 24
N_SLAB = 32
N_PENCIL = 8
SLOTS = N_SLAB * CAP
SLAB_ROWS = 16
PENCIL_ROWS = 32
KZ = 16
LINES = 15
ROWS = LINES * N_SLAB
LIMIT_P, LIMIT_Y, LIMIT_X, LIMIT_S = 48, 40, 51, 40
LIMIT_N = 40
F32 = jnp.float32
BF16 = jnp.bfloat16


def kz_of(pencil, place):
    return np.where(
        pencil < 4, 32 * pencil + place, -(32 * (7 - pencil) + 16 + place)
    )


def z_tables():
    pencil, ri, place = np.meshgrid(np.arange(8), np.arange(2), np.arange(KZ), indexing="ij")
    kz = kz_of(pencil, place).reshape(-1)
    ri = ri.reshape(-1)
    shared = (pencil.reshape(-1) == 0) & (place.reshape(-1) == 0)
    z = np.arange(GZ)
    theta = 2 * np.pi * ((z[:, None] * kz[None, :]) % GZ) / GZ
    sign = 1.0 - 2.0 * (z % 2)
    forward = np.where(ri == 0, np.cos(theta), -np.sin(theta))
    forward = np.where(shared & (ri == 1), sign[:, None], forward)
    scale = np.where(shared, 1.0, 2.0) / GZ
    backward = (forward * scale).T
    return forward, backward


def y_tables():
    slab, ro, k8 = (a.reshape(-1) for a in np.meshgrid(np.arange(32), np.arange(2), np.arange(8), indexing="ij"))
    pencil, ri, y32 = (a.reshape(-1) for a in np.meshgrid(np.arange(8), np.arange(2), np.arange(32), indexing="ij"))
    ky = (8 * slab + k8)[:, None]
    ro = ro[:, None]
    y = (32 * pencil + y32)[None, :]
    ri = ri[None, :]
    theta = 2 * np.pi * ((ky * y) % GY) / GY
    cosine, sine = np.cos(theta), np.sin(theta)
    forward = np.where(ro == ri, cosine, np.where(ro == 0, sine, -sine))
    backward = forward.T / GY
    low = (ky > 0) & (ky < 128)
    high = ky > 128
    ends = (ky == 0) | (ky == 128)
    part = np.where(ro == 0, cosine, -sine)
    shared = np.where(low & (ri == 0), part, 0.0)
    shared = np.where(high & (ri == 1), part, shared)
    shared = np.where(ends & (ro == ri), cosine, shared)
    shared_back = (shared * np.where(ends, 1.0, 2.0)).T / GY
    return forward, shared, backward, shared_back


def x_tables():
    k1, ro, ko = (a.reshape(-1)[:, None] for a in np.meshgrid(np.arange(32), np.arange(2), np.arange(8), indexing="ij"))
    slab, ri, ki = (a.reshape(-1)[None, :] for a in np.meshgrid(np.arange(32), np.arange(2), np.arange(8), indexing="ij"))
    theta = 2 * np.pi * ((k1 * slab) % 32) / 32
    rows = np.where(ro == ri, np.cos(theta), np.where(ro == 0, np.sin(theta), -np.sin(theta)))
    rows = rows * (ko == ki)
    x16 = np.arange(16)
    twist = 2 * np.pi * np.arange(32)[:, None] * x16[None, :] / GX
    twist = np.repeat(twist, KZ, axis=1)
    inner = 2 * np.pi * ((x16[:, None] * x16[None, :]) % 16) / 16
    eye = np.eye(KZ)
    cosine, sine = np.kron(np.cos(inner), eye), np.kron(np.sin(inner), eye)
    lanes = np.block([[cosine, -sine], [sine, cosine]])
    ro, k1 = (a.reshape(-1)[:, None] for a in np.meshgrid(np.arange(2), np.arange(32), indexing="ij"))
    ri, slab = (a.reshape(-1)[None, :] for a in np.meshgrid(np.arange(2), np.arange(32), indexing="ij"))
    theta = 2 * np.pi * ((k1 * slab) % 32) / 32
    line = np.where(ro == ri, np.cos(theta), np.where(ro == 0, np.sin(theta), -np.sin(theta)))
    line = line * np.where(ri == 1, -1.0, 1.0)
    return rows, np.stack([np.cos(twist), np.sin(twist)]), lanes, line


def pair(table):
    high = np.asarray(table, np.float32).astype(jnp.bfloat16)
    low = (np.asarray(table, np.float64) - high.astype(np.float64)).astype(jnp.bfloat16)
    return jnp.asarray(np.stack([high, low]))


def split(value):
    high = value.astype(BF16)
    return high, (value - high.astype(F32)).astype(BF16)


def mm(left, right):
    return jnp.dot(left, right, preferred_element_type=F32)


def mm_nt(left, right):
    return lax.dot_general(left, right, (((1,), (1,)), ((), ())), preferred_element_type=F32)


def mm3(left, right):
    return mm(left[0], right[0]) + (mm(left[0], right[1]) + mm(left[1], right[0]))


class Late:
    def __init__(self, copy, buffer):
        self.copy, self.buffer, self.here = copy, buffer, False

    def __getitem__(self, index):
        if not self.here:
            self.copy.wait()
            self.here = True
        return self.buffer[index]


def call(kernel, out_shape, *args, scratch=(), smem=(), late=(), limit=20):
    spaces = {i: pltpu.SMEM for i in smem} | {i: pltpu.HBM for i in late}
    specs = [pl.BlockSpec(memory_space=spaces.get(i, pltpu.VMEM)) for i in range(len(args))]
    multi = isinstance(out_shape, list)
    out_spec = pl.BlockSpec(memory_space=pltpu.VMEM)
    buffers = [pltpu.VMEM(args[i].shape, args[i].dtype) for i in late]
    if late:
        buffers.append(pltpu.SemaphoreType.DMA((len(late),)))
    own = len(args) + (len(out_shape) if multi else 1) + len(scratch)

    def wrapped(*refs):
        ins = list(refs[: len(args)])
        for place, i in enumerate(late):
            copy = pltpu.make_async_copy(ins[i], refs[own + place], refs[-1].at[place])
            copy.start()
            ins[i] = Late(copy, refs[own + place])
        kernel(*ins, *refs[len(args) : own])

    return pl.pallas_call(
        wrapped,
        out_shape=out_shape,
        in_specs=specs,
        out_specs=[out_spec] * len(out_shape) if multi else out_spec,
        scratch_shapes=list(scratch) + buffers,
        compiler_params=pltpu.CompilerParams(vmem_limit_bytes=limit * 2**20),
        name=kernel.__name__,
    )(*args)


def swap_groups(tiles):
    tiles = list(tiles)
    group = lax.broadcasted_iota(jnp.int32, tiles[0].shape, 1) // 16
    for bit in range(3):
        step = 1 << bit
        upper = (group & step) != 0
        for i in range(8):
            if i & step:
                continue
            low, high = tiles[i], tiles[i + step]
            tiles[i] = jnp.where(upper, pltpu.roll(high, 16 * step, 1), low)
            tiles[i + step] = jnp.where(upper, high, pltpu.roll(low, 128 - 16 * step, 1))
    return tiles


def lookup(tables, index):
    inner, outer = index & 127, index >> 7
    found = jnp.zeros((8, 128), F32)
    for part, table in enumerate(tables):
        row = jnp.broadcast_to(table, (8, 128))
        value = jnp.take_along_axis(row, inner, axis=1, mode="promise_in_bounds")
        found = jnp.where(outer == part, value, found)
    return found


def quotient(value, divisor):
    return ((value.astype(F32) + 0.5) * (1.0 / divisor)).astype(jnp.int32)


def own_slots(width, slots):
    slab = lax.broadcasted_iota(jnp.int32, (N_SLAB, slots), 0)
    slot = lax.broadcasted_iota(jnp.int32, (N_SLAB, slots), 1)
    return (slot >= slab * width) & (slot < slab * width + width)


def received_slots():
    own = own_slots(CAP // 2, SLOTS // 2)
    return jnp.concatenate([own, own], axis=1)


def pack(slot_ref, weight_ref, strength_ref, out_ref):
    slots = jnp.broadcast_to(slot_ref[0], (N_SLAB, SLOTS)).astype(F32)
    index = lax.broadcasted_iota(jnp.int32, (SLOTS, 128), 0)
    lane = lax.broadcasted_iota(jnp.int32, (SLOTS, 128), 1)
    spread = jnp.where((lane < CAP) & (quotient(index, CAP) * CAP + lane == index), 1.0, 0.0)
    by_slab = mm(jnp.where(own_slots(CAP, SLOTS), slots, 0.0).astype(BF16), spread.astype(BF16))
    lane = lax.broadcasted_iota(jnp.int32, by_slab.shape, 1)
    by_slab = jnp.where(lane < CAP, by_slab, float(PAN_DEV))
    line = lax.broadcasted_iota(jnp.int32, (ROWS, 128), 0)
    lane = lax.broadcasted_iota(jnp.int32, (ROWS, 128), 1)
    slab = quotient(line, LINES)
    place = line - slab * LINES
    mine = jnp.where(lane == slab, 1.0, 0.0).astype(BF16)[:, :N_SLAB]
    lines = mm(mine, by_slab.astype(BF16))
    ones = jnp.ones((128, 128), BF16)
    panel = lane.astype(F32)
    hot = []
    for shift in (0, 12):
        pick = lane == jnp.where(place < 12, place + shift, CAP)
        chosen = mm(jnp.where(pick, lines, 0.0).astype(BF16), ones)
        hot += [chosen == panel, chosen == panel + 128.0]
    hot = jnp.where(jnp.concatenate(hot, axis=1), 1.0, 0.0).astype(BF16)
    weight = weight_ref[...]
    empty = jnp.zeros_like(weight)
    values = jnp.concatenate(
        [jnp.concatenate([weight, empty], axis=1), jnp.concatenate([empty, weight], axis=1)], axis=0
    )
    high, low = split(values)
    out_ref[...] = mm_nt(hot, high) + mm_nt(hot, low)
    strength = strength_ref[...]
    tables = [strength[:, :128], strength[:, 128:]]
    index = by_slab.astype(jnp.int32)
    sent = jnp.concatenate([lookup(tables, index[i * 8 : i * 8 + 8]) for i in range(4)], axis=0)
    out_ref[pl.ds(12, N_SLAB, stride=LINES), :] = sent
    for half in range(2):
        out_ref[pl.ds(13 + half, N_SLAB, stride=LINES), :] = jnp.broadcast_to(tables[half], (N_SLAB, 128))


def anchor_parts(anchor):
    return anchor >> 13, (anchor >> 8) & 31, anchor & 255


def z_hot(third, dz):
    z = lax.broadcasted_iota(jnp.int32, (GZ, SLOTS), 0)
    return jnp.where(z - dz == third, 1.0, 0.0).astype(BF16)


def y_place(second, y_ref):
    rel = lax.broadcasted_iota(jnp.int32, (PENCIL_ROWS, SLOTS), 0) - second
    y_ref[...] = jnp.where((rel >= 0) & (rel < EDGE), rel, EDGE)


def stencil_row(x, first, weight_ref):
    total = jnp.zeros((32, SLOTS), F32)
    for dx in range(EDGE):
        total = jnp.where(first == x - dx, weight_ref[dx * 32 : dx * 32 + 32, :], total)
    return total


def place_rows(rows, y_ref):
    out = []
    for block in range(PENCIL_ROWS // 8):
        pieces = []
        for lane in range(SLOTS // 128):
            at = slice(lane * 128, lane * 128 + 128)
            index = y_ref[block * 8 : block * 8 + 8, at]
            pieces.append(jnp.take_along_axis(rows[:, at], index, axis=0, mode="promise_in_bounds"))
        out.append(jnp.concatenate(pieces, axis=1))
    return jnp.concatenate(out, axis=0)


def fill_rows(rows_ref, first, weight_ref):
    def step(x, carry):
        rows_ref[pl.ds(pl.multiple_of(x * 32, 32), 32), :] = stencil_row(x, first, weight_ref)
        return carry

    lax.fori_loop(0, SLAB_ROWS, step, 0)


def slot_order():
    row = lax.broadcasted_iota(jnp.int32, (256, 128), 0)
    lane = lax.broadcasted_iota(jnp.int32, (256, 128), 1)
    dy = row & 7
    picked = ((row >> 5) << 4) + (dy << 2) + ((row >> 3) & 3)
    return jnp.where((lane == picked) & (dy < EDGE), 1.0, 0.0).astype(BF16)


def project(arrived_ref, spread_ref, anchor_ref, z_ref, out_ref, weight_ref, scaled_ref, y_ref, rows_ref, packed_ref, high_ref, low_ref):
    for s in range(N_SLAB):
        packed_ref[s * 12 : s * 12 + 12, :] = arrived_ref[s * LINES : s * LINES + 12, :]
    packed = jnp.concatenate(split(packed_ref[...]), axis=0)
    order = slot_order()
    turned = [mm_nt(order[half * 128 : half * 128 + 128, :], packed) for half in range(2)]
    turned = [part[:, : SLOTS // 2] + part[:, SLOTS // 2 :] for part in turned]
    weights = jnp.concatenate(turned, axis=1)
    weight_ref[...] = weights
    high, low = split(arrived_ref[pl.ds(12, N_SLAB, stride=LINES), :])
    spread = spread_ref[...]
    strength = jnp.where(received_slots(), mm_nt(high, spread) + mm_nt(low, spread), 0.0)
    scaled_ref[...] = weights * jnp.sum(strength, axis=0, keepdims=True)
    first, second, third = anchor_parts(anchor_ref[0])
    y_place(second, y_ref)
    fill_rows(rows_ref, first, scaled_ref)
    hot = z_hot(third, 0)
    charge = jnp.zeros((512, GZ), F32)
    for dz in range(EDGE):
        for x in range(SLAB_ROWS):
            at = slice(x * PENCIL_ROWS, x * PENCIL_ROWS + PENCIL_ROWS)
            high, low = split(place_rows(rows_ref[x * 32 + dz * 8 : x * 32 + dz * 8 + 8, :], y_ref))
            high_ref[dz, at, :] = high
            low_ref[dz, at, :] = low
        part = mm_nt(high_ref[dz], hot) + mm_nt(low_ref[dz], hot)
        charge += pltpu.roll(part, dz, 1) if dz else part
    after = mm3(split(charge), z_ref[...])
    for half in range(2):
        for quarter in range(2):
            tiles = [
                after[x * 32 : x * 32 + 32, quarter * 128 : quarter * 128 + 128]
                for x in range(half * 8, half * 8 + 8)
            ]
            for g, tile in enumerate(swap_groups(tiles)):
                pencil, ri = quarter * 4 + g // 2, g % 2
                start = pencil * 128 + half * 64 + ri * 32
                out_ref[start : start + 32, :] = tile


def gathered(ref, count, rows):
    block = ref[...].reshape(count, 2, rows, 128)
    return jnp.concatenate([block[:, half].reshape(count * rows, 128) for half in range(2)], axis=1)


def scattered(value, ref, count, rows):
    for half in range(2):
        part = value[:, half * 128 : half * 128 + 128].reshape(count, rows, 128)
        for i in range(count):
            ref[(i * 2 + half) * rows : (i * 2 + half + 1) * rows, :] = part[i]


def shared_lane(shape):
    return lax.broadcasted_iota(jnp.int32, shape, 1) % KZ == 0


def y_stage(source, target):
    def kernel(flag_ref, in_ref, table_ref, shared_ref, out_ref, work_ref):
        data = split(gathered(in_ref, *source))
        work_ref[...] = mm3(table_ref[...], data)

        @pl.when(flag_ref[0] == 1)
        def _():
            other = mm3(shared_ref[...], data)
            work_ref[...] = jnp.where(shared_lane(other.shape), other, work_ref[...])

        scattered(work_ref[...], out_ref, *target)

    return kernel


def y_forward(*refs):
    y_stage((8, 64), (32, 16))(*refs)


def y_backward(*refs):
    y_stage((32, 16), (8, 64))(*refs)


def x_stage(flag_ref, in_ref, row_ref, green_ref, other_ref, twist_ref, lane_ref, line_ref, out_ref, re_ref, im_ref):
    row_tables = row_ref[...]
    rows = mm3(row_tables, split(gathered(in_ref, 32, 16))).reshape(32, 2, 8, 256)
    few = twist_ref[0], twist_ref[1]
    cosine, sine = (
        jnp.concatenate([jnp.broadcast_to(part[k : k + 1], (8, 256)) for k in range(32)], axis=0) for part in few
    )
    lane_tables = lane_ref[...]
    line_tables = line_ref[...]

    def lanes_of(re, im, cosine, sine):
        turned = jnp.concatenate([re * cosine + im * sine, im * cosine - re * sine], axis=1)
        return mm3(split(turned), lane_tables)

    full = lanes_of(rows[:, 0].reshape(256, 256), rows[:, 1].reshape(256, 256), cosine, sine)
    for half in range(2):
        at = slice(half * 128, half * 128 + 128)
        green = green_ref[half]
        re_ref[half] = full[:, at] * green
        im_ref[half] = full[:, 256 + half * 128 : 384 + half * 128] * green

    @pl.when(flag_ref[1] == 1)
    def _():
        line = jnp.concatenate(
            [
                jnp.concatenate([in_ref[pl.ds(half * 16 + ri * 8, 32, stride=32), :] for half in range(2)], axis=1)
                for ri in range(2)
            ],
            axis=0,
        )
        turned = mm3(line_tables, split(line))
        mirror = lanes_of(turned[:32], turned[32:], *few)
        other = other_ref[...]
        rows_at = pl.ds(0, 32, stride=8)
        for half in range(2):
            at = slice(half * 128, half * 128 + 128)
            re_ref[half, rows_at, :] += mirror[:, at] * other[:, at]
            im_ref[half, rows_at, :] += mirror[:, 256 + half * 128 : 384 + half * 128] * other[:, at]

    product = jnp.concatenate([re_ref[0], re_ref[1], -im_ref[0], -im_ref[1]], axis=1)
    back = mm3(split(product), lane_tables)
    re, im = back[:, :256], back[:, 256:]
    re, im = re * cosine + im * sine, im * cosine - re * sine
    rows = jnp.stack([re.reshape(32, 8, 256), im.reshape(32, 8, 256)], axis=1).reshape(512, 256)
    rows = mm3(row_tables, split(rows)).reshape(32, 2, 8, 256) * (1.0 / GX)
    rows = jnp.stack([rows[:, 0], -rows[:, 1]], axis=1).reshape(512, 256)
    scattered(rows, out_ref, 32, 16)


def sample(in_ref, weight_ref, anchor_ref, z_ref, spread_ref, out_ref, y_ref, after_ref, rows_ref, grid_ref):
    for half in range(2):
        for quarter in range(2):
            tiles = []
            for g in range(8):
                pencil, ri = quarter * 4 + g // 2, g % 2
                start = pencil * 128 + half * 64 + ri * 32
                tiles.append(in_ref[start : start + 32, :])
            for i, tile in enumerate(swap_groups(tiles)):
                x = half * 8 + i
                after_ref[x * 32 : x * 32 + 32, quarter * 128 : quarter * 128 + 128] = tile
    high, low = split(mm3(split(after_ref[...]), z_ref[...]))
    first, second, third = anchor_parts(anchor_ref[0])
    y_place(second, y_ref)

    fill_rows(rows_ref, first, weight_ref)
    total = jnp.zeros((8, SLOTS), F32)
    for dz in range(EDGE):
        hot = z_hot(third, dz)
        grid_ref[dz] = mm(high, hot) + mm(low, hot)
        for x in range(SLAB_ROWS):
            rows = rows_ref[x * 32 + dz * 8 : x * 32 + dz * 8 + 8, :]
            cells = grid_ref[dz, x * 32 : x * 32 + 32, :] * place_rows(rows, y_ref)
            total += jnp.sum(cells.reshape(4, 8, SLOTS), axis=0)
    far = jnp.sum(total, axis=0, keepdims=True)
    high, low = split(jnp.where(received_slots(), jnp.broadcast_to(far, (N_SLAB, SLOTS)), 0.0))
    out_ref[...] = mm(high, spread_ref[...]) + mm(low, spread_ref[...])


def near(flag_ref, arrived_ref, own_ref, index_ref, factor_ref, out_ref):
    before = [arrived_ref[pl.ds(flag_ref[4] + half, 1), :] for half in range(2)]
    after = [arrived_ref[pl.ds(flag_ref[5] + half, 1), :] for half in range(2)]
    tables = before + [own_ref[:, :128], own_ref[:, 128:]] + after
    for lane in range(2):
        total = jnp.zeros((8, 128), F32)
        for block in range(4):
            at = (slice(block * 8, block * 8 + 8), slice(lane * 128, lane * 128 + 128))
            total += lookup(tables, index_ref[at]) * factor_ref[at]
        out_ref[:, lane * 128 : lane * 128 + 128] = jnp.sum(total, axis=0, keepdims=True)


def finish(far_ref, spread_ref, own_ref, slot_ref, near_ref, out_ref):
    high, low = split(far_ref[...])
    own = own_ref[...]
    rows = (mm(own, high) + mm(own, low)) * spread_ref[...].astype(F32)
    column = jnp.sum(rows, axis=1, keepdims=True)
    slots = jnp.transpose(jnp.broadcast_to(slot_ref[0], (128, SLOTS)))
    panel = lax.broadcasted_iota(jnp.int32, (SLOTS, 128), 1)
    for lane in range(2):
        part = jnp.where(slots == panel + lane * 128, column, 0.0)
        at = slice(lane * 128, lane * 128 + 128)
        out_ref[:, at] = jnp.sum(part, axis=0, keepdims=True) + near_ref[:, at]


def swap(value, axis, count):
    rows = value.shape[0]
    return lax.all_to_all(value.reshape(count, rows // count, 128), axis, 0, 0, tiled=True).reshape(rows, 128)


def arrange_green(flag_ref, green_ref, plane_ref, out_ref, other_ref):
    shared, ends, upper, straight = (flag_ref[i] == 1 for i in range(4))
    place = lax.broadcasted_iota(jnp.int32, (KZ, GX), 0) == 0
    group = lax.broadcasted_iota(jnp.int32, (32, 128), 1) // KZ

    def lay(rows):
        turned = jnp.transpose(jnp.concatenate([rows] * 8, axis=0))
        halves = []
        for half in range(2):
            total = jnp.zeros((32, 128), F32)
            for k2 in range(8):
                start = (half * 8 + k2) * 32
                total = jnp.where(group == k2, turned[start : start + 32], total)
            halves.append(total)
        return jnp.concatenate(halves, axis=1)

    for k in range(8):
        up = green_ref[k, :KZ, :]
        down = jnp.concatenate([green_ref[k, KZ - i : KZ - i + 1, :] for i in range(KZ)], axis=0)
        rows = jnp.where(straight, up, down)
        zero, plane = rows[0:1], plane_ref[k : k + 1, :]
        line = jnp.where(upper, plane, zero)
        if k == 0:
            line = jnp.where(ends, 0.5 * (zero + plane), line)
            differ = jnp.where(ends, 0.5 * (zero - plane), 0.0)
            other_ref[...] = lay(jnp.where(place, differ, 0.0))
        rows = jnp.where(place & shared, line, rows)
        laid = lay(rows)
        for half in range(2):
            out_ref[half, pl.ds(k, 32, stride=8), :] = laid[:, half * 128 : half * 128 + 128]


def slot_tables():
    index = np.arange(SLOTS)
    lane = np.arange(128)[None, :]
    spread = (index % CAP)[:, None] == lane
    own = (index // CAP)[:, None] == np.arange(N_SLAB)[None, :]
    received = (index // (SLOTS // 2) * 12 + index % 12)[:, None] == lane
    return [jnp.asarray(t, BF16) for t in (spread, own, received)]


def per_device(strength, stencil_weight, slot_panel, slot_anchor, green_spectrum, near_index, near_factor):
    slab = lax.axis_index("slab")
    pencil = lax.axis_index("pencil")
    ends = (pencil == 0) & ((slab == 0) | (slab == 16))
    flags = jnp.stack([pencil == 0, ends, slab >= 16, pencil < 4]).astype(jnp.int32)
    around = jnp.stack([(slab + N_SLAB - 1) % N_SLAB, (slab + 1) % N_SLAB])
    flags = jnp.concatenate([flags, around.astype(jnp.int32) * LINES + 13])
    row = strength.reshape(1, PAN_DEV)

    z_fwd, z_bwd = (pair(t) for t in z_tables())
    y_fwd, y_fwd_shared, y_bwd, y_bwd_shared = (pair(t) for t in y_tables())
    rows, twist, lanes, line = x_tables()
    rows, lanes, line = (pair(t) for t in (rows, lanes, line))
    twist = jnp.asarray(twist, F32)
    spread, own, received = slot_tables()

    anchor = slot_anchor.reshape(N_SLAB, 2, 12).transpose(1, 0, 2).reshape(1, 1, SLOTS)

    shape = jax.ShapeDtypeStruct
    payload = call(
        pack, shape((ROWS, 128), F32), slot_panel, stencil_weight, row, limit=56)

    payload, spectrum = lax.optimization_barrier((payload, green_spectrum))
    plane = lax.ppermute(spectrum[:, 0, :], "pencil", [(4, 0)])
    arrived = lax.all_to_all(payload.reshape(N_SLAB, 1, LINES * 128), "slab", 0, 0, tiled=True).reshape(ROWS, 128)
    green, other = call(
        arrange_green, [shape((2, 256, 128), F32), shape((32, 256), F32)], flags, spectrum, plane, smem=(0,), limit=LIMIT_N
    )
    arrived, green, other, flags, anchor = lax.optimization_barrier((arrived, green, other, flags, anchor))
    near_field = call(near, shape((1, PAN_DEV), F32), flags, arrived, row, near_index, near_factor, smem=(0,), limit=LIMIT_N)
    after_z, weights = call(
        project, [shape((1024, 128), F32), shape((128, SLOTS), F32)], arrived, received, anchor, z_fwd,
        scratch=[pltpu.VMEM((128, SLOTS), F32), pltpu.VMEM((PENCIL_ROWS, SLOTS), jnp.int32)]
        + [pltpu.VMEM((512, SLOTS), F32), pltpu.VMEM((SLOTS // 2, 128), F32)]
        + [pltpu.VMEM((EDGE, 512, SLOTS), BF16)] * 2,
        late=(3,), limit=LIMIT_P,
    )
    by_y = swap(after_z, "pencil", N_PENCIL)
    after_y = call(
        y_forward, shape((1024, 128), F32), flags, by_y, y_fwd, y_fwd_shared,
        scratch=[pltpu.VMEM((512, 256), F32)], smem=(0,), limit=LIMIT_Y,
    )
    by_x = swap(after_y, "slab", N_SLAB)
    after_x = call(
        x_stage, shape((1024, 128), F32), flags, by_x, rows, green, other, twist, lanes, line,
        scratch=[pltpu.VMEM((2, 256, 128), F32)] * 2, smem=(0,), late=range(5, 8), limit=LIMIT_X,
    )
    back_x = swap(after_x, "slab", N_SLAB)
    back_y = call(
        y_backward, shape((1024, 128), F32), flags, back_x, y_bwd, y_bwd_shared,
        scratch=[pltpu.VMEM((512, 256), F32)], smem=(0,), limit=LIMIT_Y,
    )
    by_z = swap(back_y, "pencil", N_PENCIL)
    sampled = call(
        sample, shape((N_SLAB, 128), F32), by_z, weights, anchor, z_bwd, received,
        scratch=[pltpu.VMEM((PENCIL_ROWS, SLOTS), jnp.int32), pltpu.VMEM((512, 256), F32)]
        + [pltpu.VMEM((512, SLOTS), F32), pltpu.VMEM((EDGE, 512, SLOTS), F32)],
        limit=LIMIT_S,
    )
    far = lax.all_to_all(sampled, "slab", 0, 0, tiled=True)
    return call(finish, shape((1, PAN_DEV), F32), far, spread, own, slot_panel, near_field, limit=40).reshape(PAN_DEV)


def solution(mesh):
    in_specs = (
        P(("slab", "pencil")),
        P(None, ("slab", "pencil")),
        P("slab", "pencil", None),
        P("slab", "pencil", None),
        P("slab", "pencil", None),
        P(None, ("slab", "pencil")),
        P(None, ("slab", "pencil")),
    )
    out_specs = P(("slab", "pencil"))
    return jax.shard_map(
        per_device, mesh=mesh, in_specs=in_specs, out_specs=out_specs, check_vma=False
    )
```

```python
import math

import jax
import jax.numpy as jnp
import numpy as np
from jax import lax
from jax.experimental import pallas as pl
from jax.experimental.pallas import tpu as pltpu
from jax.sharding import PartitionSpec as P

GX = 512
GY = 256
GZ = 256
EDGE = 4
PAN_DEV = 256
CAP = 24
N_SLAB = 32
N_PENCIL = 8
SLOTS = N_SLAB * CAP
SLAB_ROWS = 16
PENCIL_ROWS = 32
KZ = 16
LINES = 15
ROWS = LINES * N_SLAB
LIMIT_P, LIMIT_Y, LIMIT_X, LIMIT_S = 48, 40, 51, 40
LIMIT_N = 40
F32 = jnp.float32
BF16 = jnp.bfloat16


def kz_of(pencil, place):
    return np.where(
        pencil < 4, 32 * pencil + place, -(32 * (7 - pencil) + 16 + place)
    )


def z_tables():
    pencil, ri, place = np.meshgrid(np.arange(8), np.arange(2), np.arange(KZ), indexing="ij")
    kz = kz_of(pencil, place).reshape(-1)
    ri = ri.reshape(-1)
    shared = (pencil.reshape(-1) == 0) & (place.reshape(-1) == 0)
    z = np.arange(GZ)
    theta = 2 * np.pi * ((z[:, None] * kz[None, :]) % GZ) / GZ
    sign = 1.0 - 2.0 * (z % 2)
    forward = np.where(ri == 0, np.cos(theta), -np.sin(theta))
    forward = np.where(shared & (ri == 1), sign[:, None], forward)
    scale = np.where(shared, 1.0, 2.0) / GZ
    backward = (forward * scale).T
    return forward, backward


def y_tables():
    slab, ro, k8 = (a.reshape(-1) for a in np.meshgrid(np.arange(32), np.arange(2), np.arange(8), indexing="ij"))
    pencil, ri, y32 = (a.reshape(-1) for a in np.meshgrid(np.arange(8), np.arange(2), np.arange(32), indexing="ij"))
    ky = (8 * slab + k8)[:, None]
    ro = ro[:, None]
    y = (32 * pencil + y32)[None, :]
    ri = ri[None, :]
    theta = 2 * np.pi * ((ky * y) % GY) / GY
    cosine, sine = np.cos(theta), np.sin(theta)
    forward = np.where(ro == ri, cosine, np.where(ro == 0, sine, -sine))
    backward = forward.T / GY
    low = (ky > 0) & (ky < 128)
    high = ky > 128
    ends = (ky == 0) | (ky == 128)
    part = np.where(ro == 0, cosine, -sine)
    shared = np.where(low & (ri == 0), part, 0.0)
    shared = np.where(high & (ri == 1), part, shared)
    shared = np.where(ends & (ro == ri), cosine, shared)
    shared_back = (shared * np.where(ends, 1.0, 2.0)).T / GY
    return forward, shared, backward, shared_back


def x_tables():
    k1, ro, ko = (a.reshape(-1)[:, None] for a in np.meshgrid(np.arange(32), np.arange(2), np.arange(8), indexing="ij"))
    slab, ri, ki = (a.reshape(-1)[None, :] for a in np.meshgrid(np.arange(32), np.arange(2), np.arange(8), indexing="ij"))
    theta = 2 * np.pi * ((k1 * slab) % 32) / 32
    rows = np.where(ro == ri, np.cos(theta), np.where(ro == 0, np.sin(theta), -np.sin(theta)))
    rows = rows * (ko == ki)
    x16 = np.arange(16)
    twist = 2 * np.pi * np.arange(32)[:, None] * x16[None, :] / GX
    twist = np.repeat(twist, KZ, axis=1)
    inner = 2 * np.pi * ((x16[:, None] * x16[None, :]) % 16) / 16
    eye = np.eye(KZ)
    cosine, sine = np.kron(np.cos(inner), eye), np.kron(np.sin(inner), eye)
    lanes = np.block([[cosine, -sine], [sine, cosine]])
    ro, k1 = (a.reshape(-1)[:, None] for a in np.meshgrid(np.arange(2), np.arange(32), indexing="ij"))
    ri, slab = (a.reshape(-1)[None, :] for a in np.meshgrid(np.arange(2), np.arange(32), indexing="ij"))
    theta = 2 * np.pi * ((k1 * slab) % 32) / 32
    line = np.where(ro == ri, np.cos(theta), np.where(ro == 0, np.sin(theta), -np.sin(theta)))
    line = line * np.where(ri == 1, -1.0, 1.0)
    return rows, np.stack([np.cos(twist), np.sin(twist)]), lanes, line


def pair(table):
    high = np.asarray(table, np.float32).astype(jnp.bfloat16)
    low = (np.asarray(table, np.float64) - high.astype(np.float64)).astype(jnp.bfloat16)
    return jnp.asarray(np.stack([high, low]))


def split(value):
    high = value.astype(BF16)
    return high, (value - high.astype(F32)).astype(BF16)


def mm(left, right):
    return jnp.dot(left, right, preferred_element_type=F32)


def mm_nt(left, right):
    return lax.dot_general(left, right, (((1,), (1,)), ((), ())), preferred_element_type=F32)


def mm3(left, right):
    return mm(left[0], right[0]) + (mm(left[0], right[1]) + mm(left[1], right[0]))


def call(kernel, out_shape, *args, scratch=(), smem=(), limit):
    space = {i: pltpu.SMEM for i in smem}
    out_spec = pl.BlockSpec(memory_space=pltpu.VMEM)
    return pl.pallas_call(
        kernel,
        out_shape=out_shape,
        in_specs=[pl.BlockSpec(memory_space=space.get(i, pltpu.VMEM)) for i in range(len(args))],
        out_specs=[out_spec] * len(out_shape) if isinstance(out_shape, list) else out_spec,
        scratch_shapes=list(scratch),
        compiler_params=pltpu.CompilerParams(vmem_limit_bytes=limit * 2**20),
        name=kernel.__name__,
    )(*args)


def swap_groups(tiles):
    tiles = list(tiles)
    group = lax.broadcasted_iota(jnp.int32, tiles[0].shape, 1) // 16
    for bit in range(3):
        step = 1 << bit
        upper = (group & step) != 0
        for i in range(8):
            if i & step:
                continue
            low, high = tiles[i], tiles[i + step]
            tiles[i] = jnp.where(upper, pltpu.roll(high, 16 * step, 1), low)
            tiles[i + step] = jnp.where(upper, high, pltpu.roll(low, 128 - 16 * step, 1))
    return tiles


def lookup(tables, index):
    inner, outer = index & 127, index >> 7
    found = jnp.zeros((8, 128), F32)
    for part, table in enumerate(tables):
        row = jnp.broadcast_to(table, (8, 128))
        value = jnp.take_along_axis(row, inner, axis=1, mode="promise_in_bounds")
        found = jnp.where(outer == part, value, found)
    return found


def quotient(value, divisor):
    return ((value.astype(F32) + 0.5) * (1.0 / divisor)).astype(jnp.int32)


def own_slots(width, slots):
    slab = lax.broadcasted_iota(jnp.int32, (N_SLAB, slots), 0)
    slot = lax.broadcasted_iota(jnp.int32, (N_SLAB, slots), 1)
    return (slot >= slab * width) & (slot < slab * width + width)


def received_place():
    slot = lax.broadcasted_iota(jnp.int32, (SLOTS, 128), 0)
    lane = lax.broadcasted_iota(jnp.int32, (SLOTS, 128), 1)
    twelfth = quotient(slot, 12)
    place = slot - twelfth * 12 + jnp.where(slot >= SLOTS // 2, 12, 0)
    return jnp.where(lane == place, 1.0, 0.0).astype(BF16)


def received_slots():
    own = own_slots(CAP // 2, SLOTS // 2)
    return jnp.concatenate([own, own], axis=1)


def pack(slot_ref, weight_ref, strength_ref, out_ref):
    line = lax.broadcasted_iota(jnp.int32, (ROWS, 128), 0)
    lane = lax.broadcasted_iota(jnp.int32, (ROWS, 128), 1)
    slab = quotient(line, LINES)
    place = line - slab * LINES
    target = jnp.where(place < 12, slab * CAP + place, -CAP)
    picks = []
    for shift in (0, 12):
        tiles = [jnp.where(lane + part * 128 == target + shift, 1.0, 0.0) for part in range(SLOTS // 128)]
        picks.append(jnp.concatenate(tiles, axis=1).astype(BF16))
    slots = (slot_ref[0].astype(F32) + 1.0) * jnp.where(slot_ref[0] < PAN_DEV, 1.0, 0.0)
    rows = jnp.broadcast_to(slots, (128, SLOTS)).astype(BF16)
    chosen = mm_nt(jnp.concatenate(picks, axis=0), rows)
    panel = lane.astype(F32) + 1.0
    hot = []
    for half in range(2):
        part = chosen[half * ROWS : half * ROWS + ROWS]
        hot += [part == panel, part == panel + 128.0]
    hot = jnp.where(jnp.concatenate(hot, axis=1), 1.0, 0.0).astype(BF16)
    weight = weight_ref[...]
    empty = jnp.zeros_like(weight)
    values = jnp.concatenate(
        [jnp.concatenate([weight, empty], axis=1), jnp.concatenate([empty, weight], axis=1)], axis=0
    )
    high, low = split(values)
    out_ref[...] = mm_nt(hot, high) + mm_nt(hot, low)
    index = lax.broadcasted_iota(jnp.int32, (SLOTS, 128), 0)
    lane = lax.broadcasted_iota(jnp.int32, (SLOTS, 128), 1)
    spread = jnp.where((lane < CAP) & (quotient(index, CAP) * CAP + lane == index), 1.0, 0.0)
    own = own_slots(CAP, SLOTS)
    by_slab = mm(jnp.where(own, jnp.broadcast_to(slots, own.shape), 0.0).astype(BF16), spread.astype(BF16))
    strength = strength_ref[...]
    tables = [strength[:, :128], strength[:, 128:]]
    index = by_slab.astype(jnp.int32)
    index = jnp.where(index > 0, index - 1, PAN_DEV)
    sent = jnp.concatenate([lookup(tables, index[i * 8 : i * 8 + 8]) for i in range(4)], axis=0)
    out_ref[pl.ds(12, N_SLAB, stride=LINES), :] = sent
    for half in range(2):
        out_ref[pl.ds(13 + half, N_SLAB, stride=LINES), :] = jnp.broadcast_to(tables[half], (N_SLAB, 128))


def anchor_parts(anchor):
    return anchor >> 13, (anchor >> 8) & 31, anchor & 255


def z_hot(third, dz):
    z = lax.broadcasted_iota(jnp.int32, (GZ, SLOTS), 0)
    return jnp.where(z - dz == third, 1.0, 0.0).astype(BF16)


def y_place(second, y_ref):
    rel = lax.broadcasted_iota(jnp.int32, (PENCIL_ROWS, SLOTS), 0) - second
    y_ref[...] = jnp.where((rel >= 0) & (rel < EDGE), rel, EDGE)


def stencil_row(x, first, weight_ref):
    total = jnp.zeros((32, SLOTS), F32)
    for dx in range(EDGE):
        total = jnp.where(first == x - dx, weight_ref[dx * 32 : dx * 32 + 32, :], total)
    return total


def place_rows(rows, y_ref):
    out = []
    for block in range(PENCIL_ROWS // 8):
        pieces = []
        for lane in range(SLOTS // 128):
            at = slice(lane * 128, lane * 128 + 128)
            index = y_ref[block * 8 : block * 8 + 8, at]
            pieces.append(jnp.take_along_axis(rows[:, at], index, axis=0, mode="promise_in_bounds"))
        out.append(jnp.concatenate(pieces, axis=1))
    return jnp.concatenate(out, axis=0)


def fill_rows(rows_ref, first, weight_ref):
    def step(x, carry):
        rows_ref[pl.ds(pl.multiple_of(x * 32, 32), 32), :] = stencil_row(x, first, weight_ref)
        return carry

    lax.fori_loop(0, SLAB_ROWS, step, 0)


def slot_order():
    row = lax.broadcasted_iota(jnp.int32, (256, 128), 0)
    lane = lax.broadcasted_iota(jnp.int32, (256, 128), 1)
    dy = row & 7
    picked = ((row >> 5) << 4) + (dy << 2) + ((row >> 3) & 3)
    return jnp.where((lane == picked) & (dy < EDGE), 1.0, 0.0).astype(BF16)


def project(arrived_ref, anchor_ref, z_ref, out_ref, weight_ref, scaled_ref, y_ref, rows_ref, packed_ref, high_ref, low_ref):
    for s in range(N_SLAB):
        packed_ref[s * 12 : s * 12 + 12, :] = arrived_ref[s * LINES : s * LINES + 12, :]
    packed = jnp.concatenate(split(packed_ref[...]), axis=0)
    order = slot_order()
    turned = [mm_nt(order[half * 128 : half * 128 + 128, :], packed) for half in range(2)]
    turned = [part[:, : SLOTS // 2] + part[:, SLOTS // 2 :] for part in turned]
    weights = jnp.concatenate(turned, axis=1)
    weight_ref[...] = weights
    high, low = split(arrived_ref[pl.ds(12, N_SLAB, stride=LINES), :])
    spread = received_place()
    strength = jnp.where(received_slots(), mm_nt(high, spread) + mm_nt(low, spread), 0.0)
    scaled_ref[...] = weights * jnp.sum(strength, axis=0, keepdims=True)
    first, second, third = anchor_parts(anchor_ref[0])
    y_place(second, y_ref)
    fill_rows(rows_ref, first, scaled_ref)
    hot = z_hot(third, 0)
    charge = jnp.zeros((512, GZ), F32)
    for dz in range(EDGE):
        for x in range(SLAB_ROWS):
            at = slice(x * PENCIL_ROWS, x * PENCIL_ROWS + PENCIL_ROWS)
            high, low = split(place_rows(rows_ref[x * 32 + dz * 8 : x * 32 + dz * 8 + 8, :], y_ref))
            high_ref[dz, at, :] = high
            low_ref[dz, at, :] = low
        part = mm_nt(high_ref[dz], hot) + mm_nt(low_ref[dz], hot)
        charge += pltpu.roll(part, dz, 1) if dz else part
    after = mm3(split(charge), z_ref[...])
    for half in range(2):
        for quarter in range(2):
            tiles = [
                after[x * 32 : x * 32 + 32, quarter * 128 : quarter * 128 + 128]
                for x in range(half * 8, half * 8 + 8)
            ]
            for g, tile in enumerate(swap_groups(tiles)):
                pencil, ri = quarter * 4 + g // 2, g % 2
                start = pencil * 128 + half * 64 + ri * 32
                out_ref[start : start + 32, :] = tile


def gathered(ref, count, rows):
    block = ref[...].reshape(count, 2, rows, 128)
    return jnp.concatenate([block[:, half].reshape(count * rows, 128) for half in range(2)], axis=1)


def scattered(value, ref, count, rows):
    for half in range(2):
        part = value[:, half * 128 : half * 128 + 128].reshape(count, rows, 128)
        for i in range(count):
            ref[(i * 2 + half) * rows : (i * 2 + half + 1) * rows, :] = part[i]


def shared_lane(shape):
    return lax.broadcasted_iota(jnp.int32, shape, 1) % KZ == 0


def y_stage(source, target):
    def kernel(flag_ref, in_ref, table_ref, shared_ref, out_ref, work_ref):
        data = split(gathered(in_ref, *source))
        work_ref[...] = mm3(table_ref[...], data)

        @pl.when(flag_ref[0] == 1)
        def _():
            other = mm3(shared_ref[...], data)
            work_ref[...] = jnp.where(shared_lane(other.shape), other, work_ref[...])

        scattered(work_ref[...], out_ref, *target)

    return kernel


def y_forward(*refs):
    y_stage((8, 64), (32, 16))(*refs)


def y_backward(*refs):
    y_stage((32, 16), (8, 64))(*refs)


def x_stage(flag_ref, in_ref, row_ref, green_ref, other_ref, twist_ref, lane_ref, line_ref, out_ref, re_ref, im_ref):
    row_tables = row_ref[...]
    rows = mm3(row_tables, split(gathered(in_ref, 32, 16))).reshape(32, 2, 8, 256)
    few = twist_ref[0], twist_ref[1]
    cosine, sine = (
        jnp.concatenate([jnp.broadcast_to(part[k : k + 1], (8, 256)) for k in range(32)], axis=0) for part in few
    )
    lane_tables = lane_ref[...]
    line_tables = line_ref[...]

    def lanes_of(re, im, cosine, sine):
        turned = jnp.concatenate([re * cosine + im * sine, im * cosine - re * sine], axis=1)
        return mm3(split(turned), lane_tables)

    full = lanes_of(rows[:, 0].reshape(256, 256), rows[:, 1].reshape(256, 256), cosine, sine)
    for half in range(2):
        at = slice(half * 128, half * 128 + 128)
        green = green_ref[half]
        re_ref[half] = full[:, at] * green
        im_ref[half] = full[:, 256 + half * 128 : 384 + half * 128] * green

    @pl.when(flag_ref[1] == 1)
    def _():
        line = jnp.concatenate(
            [
                jnp.concatenate([in_ref[pl.ds(half * 16 + ri * 8, 32, stride=32), :] for half in range(2)], axis=1)
                for ri in range(2)
            ],
            axis=0,
        )
        turned = mm3(line_tables, split(line))
        mirror = lanes_of(turned[:32], turned[32:], *few)
        other = other_ref[...]
        rows_at = pl.ds(0, 32, stride=8)
        for half in range(2):
            at = slice(half * 128, half * 128 + 128)
            re_ref[half, rows_at, :] += mirror[:, at] * other[:, at]
            im_ref[half, rows_at, :] += mirror[:, 256 + half * 128 : 384 + half * 128] * other[:, at]

    product = jnp.concatenate([re_ref[0], re_ref[1], -im_ref[0], -im_ref[1]], axis=1)
    back = mm3(split(product), lane_tables)
    re, im = back[:, :256], back[:, 256:]
    re, im = re * cosine + im * sine, im * cosine - re * sine
    rows = jnp.stack([re.reshape(32, 8, 256), im.reshape(32, 8, 256)], axis=1).reshape(512, 256)
    rows = mm3(row_tables, split(rows)).reshape(32, 2, 8, 256) * (1.0 / GX)
    rows = jnp.stack([rows[:, 0], -rows[:, 1]], axis=1).reshape(512, 256)
    scattered(rows, out_ref, 32, 16)


def sample(in_ref, weight_ref, anchor_ref, z_ref, out_ref, y_ref, after_ref, rows_ref, grid_ref):
    for half in range(2):
        for quarter in range(2):
            tiles = []
            for g in range(8):
                pencil, ri = quarter * 4 + g // 2, g % 2
                start = pencil * 128 + half * 64 + ri * 32
                tiles.append(in_ref[start : start + 32, :])
            for i, tile in enumerate(swap_groups(tiles)):
                x = half * 8 + i
                after_ref[x * 32 : x * 32 + 32, quarter * 128 : quarter * 128 + 128] = tile
    high, low = split(mm3(split(after_ref[...]), z_ref[...]))
    first, second, third = anchor_parts(anchor_ref[0])
    y_place(second, y_ref)

    fill_rows(rows_ref, first, weight_ref)
    total = jnp.zeros((8, SLOTS), F32)
    for dz in range(EDGE):
        hot = z_hot(third, dz)
        grid_ref[dz] = mm(high, hot) + mm(low, hot)
        for x in range(SLAB_ROWS):
            rows = rows_ref[x * 32 + dz * 8 : x * 32 + dz * 8 + 8, :]
            cells = grid_ref[dz, x * 32 : x * 32 + 32, :] * place_rows(rows, y_ref)
            total += jnp.sum(cells.reshape(4, 8, SLOTS), axis=0)
    far = jnp.sum(total, axis=0, keepdims=True)
    high, low = split(jnp.where(received_slots(), jnp.broadcast_to(far, (N_SLAB, SLOTS)), 0.0))
    spread = received_place()
    out_ref[...] = mm(high, spread) + mm(low, spread)


def near(flag_ref, arrived_ref, slot_ref, own_ref, index_ref, factor_ref, out_ref, hot_ref):
    slots = jnp.transpose(jnp.broadcast_to(slot_ref[0], (128, SLOTS)))
    panel = lax.broadcasted_iota(jnp.int32, (SLOTS, 128), 1)
    for half in range(2):
        hot = jnp.where(slots == panel + half * 128, 1.0, 0.0)
        hot_ref[:, half * 128 : half * 128 + 128] = hot.astype(BF16)
    before = [arrived_ref[pl.ds(flag_ref[4] + half, 1), :] for half in range(2)]
    after = [arrived_ref[pl.ds(flag_ref[5] + half, 1), :] for half in range(2)]
    tables = before + [own_ref[:, :128], own_ref[:, 128:]] + after
    for lane in range(2):
        total = jnp.zeros((8, 128), F32)
        for block in range(4):
            at = (slice(block * 8, block * 8 + 8), slice(lane * 128, lane * 128 + 128))
            total += lookup(tables, index_ref[at]) * factor_ref[at]
        out_ref[:, lane * 128 : lane * 128 + 128] = jnp.sum(total, axis=0, keepdims=True)


def finish(far_ref, hot_ref, near_ref, out_ref):
    index = lax.broadcasted_iota(jnp.int32, (SLOTS, 128), 0)
    lane = lax.broadcasted_iota(jnp.int32, (SLOTS, 128), 1)
    spread = jnp.where((lane < CAP) & (quotient(index, CAP) * CAP + lane == index), 1.0, 0.0)
    by_slot = mm_nt(jnp.concatenate(split(far_ref[...]), axis=0), spread.astype(BF16))
    by_slot = jnp.where(own_slots(CAP, SLOTS), by_slot[:N_SLAB] + by_slot[N_SLAB:], 0.0)
    row = jnp.broadcast_to(jnp.sum(by_slot, axis=0, keepdims=True), (8, SLOTS))
    high, low = split(row)
    hot = hot_ref[...]
    out_ref[...] = (mm(high, hot) + mm(low, hot))[:1] + near_ref[...]


def swap(value, axis, count):
    rows = value.shape[0]
    return lax.all_to_all(value.reshape(count, rows // count, 128), axis, 0, 0, tiled=True).reshape(rows, 128)


def arrange_green(flag_ref, green_ref, plane_ref, out_ref, other_ref):
    shared, ends, upper, straight = (flag_ref[i] == 1 for i in range(4))
    place = lax.broadcasted_iota(jnp.int32, (KZ, GX), 0) == 0
    group = lax.broadcasted_iota(jnp.int32, (32, 128), 1) // KZ

    def lay(rows):
        turned = jnp.transpose(jnp.concatenate([rows] * 8, axis=0))
        halves = []
        for half in range(2):
            total = jnp.zeros((32, 128), F32)
            for k2 in range(8):
                start = (half * 8 + k2) * 32
                total = jnp.where(group == k2, turned[start : start + 32], total)
            halves.append(total)
        return jnp.concatenate(halves, axis=1)

    for k in range(8):
        up = green_ref[k, :KZ, :]
        down = jnp.concatenate([green_ref[k, KZ - i : KZ - i + 1, :] for i in range(KZ)], axis=0)
        rows = jnp.where(straight, up, down)
        zero, plane = rows[0:1], plane_ref[k : k + 1, :]
        line = jnp.where(upper, plane, zero)
        if k == 0:
            line = jnp.where(ends, 0.5 * (zero + plane), line)
            differ = jnp.where(ends, 0.5 * (zero - plane), 0.0)
            other_ref[...] = lay(jnp.where(place, differ, 0.0))
        rows = jnp.where(place & shared, line, rows)
        laid = lay(rows)
        for half in range(2):
            out_ref[half, pl.ds(k, 32, stride=8), :] = laid[:, half * 128 : half * 128 + 128]


def per_device(strength, stencil_weight, slot_panel, slot_anchor, green_spectrum, near_index, near_factor):
    slab = lax.axis_index("slab")
    pencil = lax.axis_index("pencil")
    ends = (pencil == 0) & ((slab == 0) | (slab == 16))
    flags = jnp.stack([pencil == 0, ends, slab >= 16, pencil < 4]).astype(jnp.int32)
    around = jnp.stack([(slab + N_SLAB - 1) % N_SLAB, (slab + 1) % N_SLAB])
    flags = jnp.concatenate([flags, around.astype(jnp.int32) * LINES + 13])
    row = strength.reshape(1, PAN_DEV)

    z_fwd, z_bwd = (pair(t) for t in z_tables())
    y_fwd, y_fwd_shared, y_bwd, y_bwd_shared = (pair(t) for t in y_tables())
    rows, twist, lanes, line = x_tables()
    rows, lanes, line = (pair(t) for t in (rows, lanes, line))
    twist = jnp.asarray(twist, F32)

    anchor = slot_anchor.reshape(N_SLAB, 2, 12).transpose(1, 0, 2).reshape(1, 1, SLOTS)

    shape = jax.ShapeDtypeStruct
    payload = call(
        pack, shape((ROWS, 128), F32), slot_panel, stencil_weight, row, limit=56)

    payload, spectrum = lax.optimization_barrier((payload, green_spectrum))
    plane = lax.ppermute(spectrum[:, 0, :], "pencil", [(4, 0)])
    arrived = lax.all_to_all(payload.reshape(N_SLAB, 1, LINES * 128), "slab", 0, 0, tiled=True).reshape(ROWS, 128)
    green, other = call(
        arrange_green, [shape((2, 256, 128), F32), shape((32, 256), F32)], flags, spectrum, plane, smem=(0,), limit=LIMIT_N
    )
    arrived, green, other, flags, anchor = lax.optimization_barrier((arrived, green, other, flags, anchor))
    near_field, hot = call(
        near, [shape((1, PAN_DEV), F32), shape((SLOTS, PAN_DEV), BF16)], flags, arrived, slot_panel, row, near_index, near_factor,
        smem=(0,), limit=LIMIT_N,
    )
    after_z, weights = call(
        project, [shape((1024, 128), F32), shape((128, SLOTS), F32)], arrived, anchor, z_fwd,
        scratch=[pltpu.VMEM((128, SLOTS), F32), pltpu.VMEM((PENCIL_ROWS, SLOTS), jnp.int32)]
        + [pltpu.VMEM((512, SLOTS), F32), pltpu.VMEM((SLOTS // 2, 128), F32)]
        + [pltpu.VMEM((EDGE, 512, SLOTS), BF16)] * 2,
        limit=LIMIT_P,
    )
    by_y = swap(after_z, "pencil", N_PENCIL)
    after_y = call(
        y_forward, shape((1024, 128), F32), flags, by_y, y_fwd, y_fwd_shared,
        scratch=[pltpu.VMEM((512, 256), F32)], smem=(0,), limit=LIMIT_Y,
    )
    by_x = swap(after_y, "slab", N_SLAB)
    after_x = call(
        x_stage, shape((1024, 128), F32), flags, by_x, rows, green, other, twist, lanes, line,
        scratch=[pltpu.VMEM((2, 256, 128), F32)] * 2, smem=(0,), limit=LIMIT_X,
    )
    back_x = swap(after_x, "slab", N_SLAB)
    back_y = call(
        y_backward, shape((1024, 128), F32), flags, back_x, y_bwd, y_bwd_shared,
        scratch=[pltpu.VMEM((512, 256), F32)], smem=(0,), limit=LIMIT_Y,
    )
    by_z = swap(back_y, "pencil", N_PENCIL)
    sampled = call(
        sample, shape((N_SLAB, 128), F32), by_z, weights, anchor, z_bwd,
        scratch=[pltpu.VMEM((PENCIL_ROWS, SLOTS), jnp.int32), pltpu.VMEM((512, 256), F32)]
        + [pltpu.VMEM((512, SLOTS), F32), pltpu.VMEM((EDGE, 512, SLOTS), F32)],
        limit=LIMIT_S,
    )
    far = lax.all_to_all(sampled, "slab", 0, 0, tiled=True)
    return call(finish, shape((1, PAN_DEV), F32), far, hot, near_field, limit=40).reshape(PAN_DEV)


def solution(mesh):
    in_specs = (
        P(("slab", "pencil")),
        P(None, ("slab", "pencil")),
        P("slab", "pencil", None),
        P("slab", "pencil", None),
        P("slab", "pencil", None),
        P(None, ("slab", "pencil")),
        P(None, ("slab", "pencil")),
    )
    out_specs = P(("slab", "pencil"))
    return jax.shard_map(
        per_device, mesh=mesh, in_specs=in_specs, out_specs=out_specs, check_vma=False
    )
```

```python
import math

import jax
import jax.numpy as jnp
import numpy as np
from jax import lax
from jax.experimental import pallas as pl
from jax.experimental.pallas import tpu as pltpu
from jax.sharding import PartitionSpec as P

GX = 512
GY = 256
GZ = 256
EDGE = 4
PAN_DEV = 256
CAP = 24
N_SLAB = 32
N_PENCIL = 8
SLOTS = N_SLAB * CAP
SLAB_ROWS = 16
PENCIL_ROWS = 32
STENCIL = 64
KZ = 16
LINES = 15
ROWS = LINES * N_SLAB
LIMIT_P, LIMIT_Y, LIMIT_X, LIMIT_S = 48, 40, 51, 40
LIMIT_N = 40
F32 = jnp.float32
BF16 = jnp.bfloat16


def kz_of(pencil, place):
    return np.where(
        pencil < 4, 32 * pencil + place, -(32 * (7 - pencil) + 16 + place)
    )


def z_tables():
    pencil, ri, place = np.meshgrid(np.arange(8), np.arange(2), np.arange(KZ), indexing="ij")
    kz = kz_of(pencil, place).reshape(-1)
    ri = ri.reshape(-1)
    shared = (pencil.reshape(-1) == 0) & (place.reshape(-1) == 0)
    z = np.arange(GZ)
    theta = 2 * np.pi * ((z[:, None] * kz[None, :]) % GZ) / GZ
    sign = 1.0 - 2.0 * (z % 2)
    forward = np.where(ri == 0, np.cos(theta), -np.sin(theta))
    forward = np.where(shared & (ri == 1), sign[:, None], forward)
    scale = np.where(shared, 1.0, 2.0) / GZ
    backward = (forward * scale).T
    return forward, backward


def y_tables():
    slab, ro, k8 = (a.reshape(-1) for a in np.meshgrid(np.arange(32), np.arange(2), np.arange(8), indexing="ij"))
    pencil, ri, y32 = (a.reshape(-1) for a in np.meshgrid(np.arange(8), np.arange(2), np.arange(32), indexing="ij"))
    ky = (8 * slab + k8)[:, None]
    ro = ro[:, None]
    y = (32 * pencil + y32)[None, :]
    ri = ri[None, :]
    theta = 2 * np.pi * ((ky * y) % GY) / GY
    cosine, sine = np.cos(theta), np.sin(theta)
    forward = np.where(ro == ri, cosine, np.where(ro == 0, sine, -sine))
    backward = forward.T / GY
    low = (ky > 0) & (ky < 128)
    high = ky > 128
    ends = (ky == 0) | (ky == 128)
    part = np.where(ro == 0, cosine, -sine)
    shared = np.where(low & (ri == 0), part, 0.0)
    shared = np.where(high & (ri == 1), part, shared)
    shared = np.where(ends & (ro == ri), cosine, shared)
    shared_back = (shared * np.where(ends, 1.0, 2.0)).T / GY
    return forward, shared, backward, shared_back


def x_tables():
    ro, k1 = (a.reshape(-1)[:, None] for a in np.meshgrid(np.arange(2), np.arange(32), indexing="ij"))
    ri, slab = (a.reshape(-1)[None, :] for a in np.meshgrid(np.arange(2), np.arange(32), indexing="ij"))
    theta = 2 * np.pi * ((k1 * slab) % 32) / 32
    rows = np.where(ro == ri, np.cos(theta), np.where(ro == 0, np.sin(theta), -np.sin(theta)))
    x16 = np.arange(16)
    twist = 2 * np.pi * np.arange(32)[:, None] * x16[None, :] / GX
    twist = np.repeat(twist, KZ, axis=1)
    inner = 2 * np.pi * ((x16[:, None] * x16[None, :]) % 16) / 16
    eye = np.eye(KZ)
    cosine, sine = np.kron(np.cos(inner), eye), np.kron(np.sin(inner), eye)
    lanes = np.block([[cosine, -sine], [sine, cosine]])
    return rows, np.stack([np.cos(twist), np.sin(twist)]), lanes


def pair(table):
    high = np.asarray(table, np.float32).astype(jnp.bfloat16)
    low = (np.asarray(table, np.float64) - high.astype(np.float64)).astype(jnp.bfloat16)
    return jnp.asarray(np.stack([high, low]))


def split(value):
    high = value.astype(BF16)
    return high, (value - high.astype(F32)).astype(BF16)


def mm(left, right):
    return jnp.dot(left, right, preferred_element_type=F32)


def mm_nt(left, right):
    return lax.dot_general(left, right, (((1,), (1,)), ((), ())), preferred_element_type=F32)


def mm3(left, right):
    return mm(left[0], right[0]) + (mm(left[0], right[1]) + mm(left[1], right[0]))


def call(kernel, out_shape, *args, scratch=(), smem=(), limit):
    space = {i: pltpu.SMEM for i in smem}
    out_spec = pl.BlockSpec(memory_space=pltpu.VMEM)
    return pl.pallas_call(
        kernel,
        out_shape=out_shape,
        in_specs=[pl.BlockSpec(memory_space=space.get(i, pltpu.VMEM)) for i in range(len(args))],
        out_specs=[out_spec] * len(out_shape) if isinstance(out_shape, list) else out_spec,
        scratch_shapes=list(scratch),
        compiler_params=pltpu.CompilerParams(vmem_limit_bytes=limit * 2**20),
        name=kernel.__name__,
    )(*args)


def swap_groups(tiles):
    tiles = list(tiles)
    group = lax.broadcasted_iota(jnp.int32, tiles[0].shape, 1) // 16
    for bit in range(3):
        step = 1 << bit
        upper = (group & step) != 0
        for i in range(8):
            if i & step:
                continue
            low, high = tiles[i], tiles[i + step]
            tiles[i] = jnp.where(upper, pltpu.roll(high, 16 * step, 1), low)
            tiles[i + step] = jnp.where(upper, high, pltpu.roll(low, 128 - 16 * step, 1))
    return tiles


def lookup(tables, index):
    inner, outer = index & 127, index >> 7
    found = jnp.zeros((8, 128), F32)
    for part, table in enumerate(tables):
        row = jnp.broadcast_to(table, (8, 128))
        value = jnp.take_along_axis(row, inner, axis=1, mode="promise_in_bounds")
        found = jnp.where(outer == part, value, found)
    return found


def quotient(value, divisor):
    return ((value.astype(F32) + 0.5) * (1.0 / divisor)).astype(jnp.int32)


def pick(table, slab, place):
    sublane = lax.broadcasted_iota(jnp.int32, (8, 128), 0)
    total = jnp.zeros((8, 128), F32)
    for block in range(N_SLAB // 8):
        value = jnp.take_along_axis(table[block * 8 : block * 8 + 8], place, axis=1, mode="promise_in_bounds")
        total = jnp.where(slab == sublane + block * 8, value, total)
    return jnp.sum(total, axis=0, keepdims=True)


def pack(slot_ref, weight_ref, strength_ref, out_ref, by_slot_ref):
    strength = strength_ref[...]
    halves = [strength[:, :128], strength[:, 128:]]
    tables = []
    for tile in range(SLOTS // 128):
        at = slice(tile * 128, tile * 128 + 128)
        index = jnp.broadcast_to(slot_ref[0, :, at], (8, 128))
        inner, outer = index & 127, index >> 7
        tables.append(lookup(halves, index)[:1])
        found = []
        for block in range(8):
            low, high = (
                jnp.take_along_axis(
                    weight_ref[block * 8 : block * 8 + 8, half * 128 : half * 128 + 128],
                    inner,
                    axis=1,
                    mode="promise_in_bounds",
                )
                for half in range(2)
            )
            found.append(jnp.where(outer == 0, low, jnp.where(outer == 1, high, 0.0)))
        by_slot_ref[at, :] = jnp.transpose(jnp.concatenate(found * 2, axis=0))
    first = lax.broadcasted_iota(jnp.int32, (12, 128), 1) < STENCIL
    for d in range(N_SLAB):
        out_ref[d * LINES : d * LINES + 12, :] = jnp.where(
            first, by_slot_ref[d * CAP : d * CAP + 12, :], by_slot_ref[d * CAP + 12 : d * CAP + 24, :]
        )
    sent = []
    for block in range(N_SLAB // 8):
        slab = lax.broadcasted_iota(jnp.int32, (8, 128), 0) + block * 8
        place = lax.broadcasted_iota(jnp.int32, (8, 128), 1)
        sent.append(lookup(tables, jnp.where(place < CAP, slab * CAP + place, SLOTS)))
    out_ref[pl.ds(12, N_SLAB, stride=LINES), :] = jnp.concatenate(sent, axis=0)
    for half in range(2):
        out_ref[pl.ds(13 + half, N_SLAB, stride=LINES), :] = jnp.broadcast_to(halves[half], (N_SLAB, 128))


def anchor_parts(anchor):
    return anchor >> 13, (anchor >> 8) & 31, anchor & 255


def z_hot(third, dz):
    z = lax.broadcasted_iota(jnp.int32, (GZ, SLOTS), 0)
    return jnp.where(z - dz == third, 1.0, 0.0).astype(BF16)


def y_place(second, y_ref):
    rel = lax.broadcasted_iota(jnp.int32, (PENCIL_ROWS, SLOTS), 0) - second
    y_ref[...] = jnp.where((rel >= 0) & (rel < EDGE), rel, EDGE)


def stencil_row(x, first, weight_ref):
    total = jnp.zeros((32, SLOTS), F32)
    for dx in range(EDGE):
        total = jnp.where(first == x - dx, weight_ref[dx * 32 : dx * 32 + 32, :], total)
    return total


def place_rows(rows, y_ref):
    out = []
    for block in range(PENCIL_ROWS // 8):
        pieces = []
        for lane in range(SLOTS // 128):
            at = slice(lane * 128, lane * 128 + 128)
            index = y_ref[block * 8 : block * 8 + 8, at]
            pieces.append(jnp.take_along_axis(rows[:, at], index, axis=0, mode="promise_in_bounds"))
        out.append(jnp.concatenate(pieces, axis=1))
    return jnp.concatenate(out, axis=0)


def fill_rows(rows_ref, first, weight_ref):
    def step(x, carry):
        rows_ref[pl.ds(pl.multiple_of(x * 32, 32), 32), :] = stencil_row(x, first, weight_ref)
        return carry

    lax.fori_loop(0, SLAB_ROWS, step, 0)


def slot_order():
    row = lax.broadcasted_iota(jnp.int32, (256, 128), 0)
    lane = lax.broadcasted_iota(jnp.int32, (256, 128), 1)
    dy = row & 7
    picked = ((row >> 5) << 4) + (dy << 2) + ((row >> 3) & 3)
    return jnp.where((lane == picked) & (dy < EDGE), 1.0, 0.0).astype(BF16)


def project(arrived_ref, anchor_ref, z_ref, out_ref, weight_ref, scaled_ref, y_ref, rows_ref, packed_ref, high_ref, low_ref):
    for s in range(N_SLAB):
        packed_ref[s * 12 : s * 12 + 12, :] = arrived_ref[s * LINES : s * LINES + 12, :]
    packed = jnp.concatenate(split(packed_ref[...]), axis=0)
    order = slot_order()
    turned = [mm_nt(order[half * 128 : half * 128 + 128, :], packed) for half in range(2)]
    turned = [part[:, : SLOTS // 2] + part[:, SLOTS // 2 :] for part in turned]
    weights = jnp.concatenate(turned, axis=1)
    weight_ref[...] = weights
    sent = arrived_ref[pl.ds(12, N_SLAB, stride=LINES), :]
    strength = []
    for tile in range(SLOTS // 128):
        slot = lax.broadcasted_iota(jnp.int32, (8, 128), 1) + tile % 3 * 128
        slab = quotient(slot, 12)
        strength.append(pick(sent, slab, slot - slab * 12 + tile // 3 * 12))
    scaled_ref[...] = weights * jnp.concatenate(strength, axis=1)
    first, second, third = anchor_parts(anchor_ref[0])
    y_place(second, y_ref)
    fill_rows(rows_ref, first, scaled_ref)
    hot = z_hot(third, 0)
    charge = jnp.zeros((512, GZ), F32)
    for dz in range(EDGE):
        for x in range(SLAB_ROWS):
            at = slice(x * PENCIL_ROWS, x * PENCIL_ROWS + PENCIL_ROWS)
            high, low = split(place_rows(rows_ref[x * 32 + dz * 8 : x * 32 + dz * 8 + 8, :], y_ref))
            high_ref[dz, at, :] = high
            low_ref[dz, at, :] = low
        part = mm_nt(high_ref[dz], hot) + mm_nt(low_ref[dz], hot)
        charge += pltpu.roll(part, dz, 1) if dz else part
    after = mm3(split(charge), z_ref[...])
    for half in range(2):
        for quarter in range(2):
            tiles = [
                after[x * 32 : x * 32 + 32, quarter * 128 : quarter * 128 + 128]
                for x in range(half * 8, half * 8 + 8)
            ]
            for g, tile in enumerate(swap_groups(tiles)):
                pencil, ri = quarter * 4 + g // 2, g % 2
                start = pencil * 128 + half * 64 + ri * 32
                out_ref[start : start + 32, :] = tile


def gathered(ref, count, rows):
    block = ref[...].reshape(count, 2, rows, 128)
    return jnp.concatenate([block[:, half].reshape(count * rows, 128) for half in range(2)], axis=1)


def scattered(value, ref, count, rows):
    for half in range(2):
        part = value[:, half * 128 : half * 128 + 128].reshape(count, rows, 128)
        for i in range(count):
            ref[(i * 2 + half) * rows : (i * 2 + half + 1) * rows, :] = part[i]


def shared_lane(shape):
    return lax.broadcasted_iota(jnp.int32, shape, 1) % KZ == 0


def y_stage(source, target):
    def kernel(flag_ref, in_ref, table_ref, shared_ref, out_ref, work_ref):
        data = split(gathered(in_ref, *source))
        work_ref[...] = mm3(table_ref[...], data)

        @pl.when(flag_ref[0] == 1)
        def _():
            other = mm3(shared_ref[...], data)
            work_ref[...] = jnp.where(shared_lane(other.shape), other, work_ref[...])

        scattered(work_ref[...], out_ref, *target)

    return kernel


def y_forward(*refs):
    y_stage((8, 64), (32, 16))(*refs)


def y_backward(*refs):
    y_stage((32, 16), (8, 64))(*refs)


def x_stage(flag_ref, in_ref, green_ref, other_ref, twist_ref, row_ref, lane_ref, out_ref, re_ref, im_ref):
    row_tables, lane_tables = row_ref[...], lane_ref[...]
    cosine, sine = twist_ref[0], twist_ref[1]

    def line(k, ri):
        return [in_ref[pl.ds(half * 16 + ri * 8 + k, 32, stride=32), :] for half in range(2)]

    def turn(re, im):
        return jnp.concatenate([re * cosine + im * sine, im * cosine - re * sine], axis=1)

    data = [jnp.concatenate(sum((line(k, ri) for k in range(8)), []), axis=1) for ri in range(2)]
    rows = mm3(row_tables, split(jnp.concatenate(data, axis=0)))
    columns = [slice(k * 256, k * 256 + 256) for k in range(8)]
    full = mm3(split(jnp.concatenate([turn(rows[:32, at], rows[32:, at]) for at in columns], axis=0)), lane_tables)
    for half in range(2):
        at = slice(half * 128, half * 128 + 128)
        re_ref[half] = full[:, at] * green_ref[half]
        im_ref[half] = full[:, 256 + half * 128 : 384 + half * 128] * green_ref[half]

    @pl.when(flag_ref[1] == 1)
    def _():
        conjugate = jnp.concatenate([data[0][:, :256], -data[1][:, :256]], axis=0)
        rows = mm3(row_tables, split(conjugate))
        mirror = mm3(split(turn(rows[:32], rows[32:])), lane_tables)
        for half in range(2):
            at = slice(half * 128, half * 128 + 128)
            other = other_ref[:, at]
            re_ref[half, :32, :] += mirror[:, at] * other
            im_ref[half, :32, :] += mirror[:, 256 + half * 128 : 384 + half * 128] * other

    product = jnp.concatenate([re_ref[0], re_ref[1], -im_ref[0], -im_ref[1]], axis=1)
    back = mm3(split(product), lane_tables)
    back = [turn(back[k * 32 : k * 32 + 32, :256], back[k * 32 : k * 32 + 32, 256:]) for k in range(8)]
    data = [jnp.concatenate([part[:, ri * 256 : ri * 256 + 256] for part in back], axis=1) for ri in range(2)]
    rows = mm3(row_tables, split(jnp.concatenate(data, axis=0)))
    for k in range(8):
        for ri in range(2):
            for half in range(2):
                part = rows[ri * 32 : ri * 32 + 32, k * 256 + half * 128 : k * 256 + half * 128 + 128]
                out_ref[pl.ds(half * 16 + ri * 8 + k, 32, stride=32), :] = part * ((1 - 2 * ri) / GX)


def sample(in_ref, weight_ref, anchor_ref, z_ref, out_ref, y_ref, after_ref, rows_ref, grid_ref):
    for half in range(2):
        for quarter in range(2):
            tiles = []
            for g in range(8):
                pencil, ri = quarter * 4 + g // 2, g % 2
                start = pencil * 128 + half * 64 + ri * 32
                tiles.append(in_ref[start : start + 32, :])
            for i, tile in enumerate(swap_groups(tiles)):
                x = half * 8 + i
                after_ref[x * 32 : x * 32 + 32, quarter * 128 : quarter * 128 + 128] = tile
    high, low = split(mm3(split(after_ref[...]), z_ref[...]))
    first, second, third = anchor_parts(anchor_ref[0])
    y_place(second, y_ref)

    fill_rows(rows_ref, first, weight_ref)
    total = jnp.zeros((8, SLOTS), F32)
    for dz in range(EDGE):
        hot = z_hot(third, dz)
        grid_ref[dz] = mm(high, hot) + mm(low, hot)
        for x in range(SLAB_ROWS):
            rows = rows_ref[x * 32 + dz * 8 : x * 32 + dz * 8 + 8, :]
            cells = grid_ref[dz, x * 32 : x * 32 + 32, :] * place_rows(rows, y_ref)
            total += jnp.sum(cells.reshape(4, 8, SLOTS), axis=0)
    far = jnp.sum(total, axis=0, keepdims=True)
    tables = [far[:, tile * 128 : tile * 128 + 128] for tile in range(SLOTS // 128)]
    for block in range(N_SLAB // 8):
        slab = lax.broadcasted_iota(jnp.int32, (8, 128), 0) + block * 8
        place = lax.broadcasted_iota(jnp.int32, (8, 128), 1)
        index = slab * 12 + place + jnp.where(place < 12, 0, SLOTS // 2 - 12)
        out_ref[block * 8 : block * 8 + 8, :] = lookup(tables, jnp.where(place < CAP, index, SLOTS))


def near(flag_ref, arrived_ref, slot_ref, own_ref, index_ref, factor_ref, out_ref, slab_ref, place_ref):
    slots = jnp.transpose(jnp.broadcast_to(slot_ref[0], (128, SLOTS)))
    panel = lax.broadcasted_iota(jnp.int32, (SLOTS, 128), 1)
    slot = lax.broadcasted_iota(jnp.int32, (SLOTS, 128), 0).astype(F32)
    for half in range(2):
        at = slice(half * 128, half * 128 + 128)
        own = jnp.sum(jnp.where(slots == panel + half * 128, slot, 0.0), axis=0, keepdims=True)
        own = jnp.broadcast_to(own, (8, 128)).astype(jnp.int32)
        slab = quotient(own, CAP)
        slab_ref[:, at] = slab
        place_ref[:, at] = own - slab * CAP
    before = [arrived_ref[pl.ds(flag_ref[4] + half, 1), :] for half in range(2)]
    after = [arrived_ref[pl.ds(flag_ref[5] + half, 1), :] for half in range(2)]
    tables = before + [own_ref[:, :128], own_ref[:, 128:]] + after
    for lane in range(2):
        total = jnp.zeros((8, 128), F32)
        for block in range(4):
            at = (slice(block * 8, block * 8 + 8), slice(lane * 128, lane * 128 + 128))
            total += lookup(tables, index_ref[at]) * factor_ref[at]
        out_ref[:, lane * 128 : lane * 128 + 128] = jnp.sum(total, axis=0, keepdims=True)


def finish(far_ref, slab_ref, place_ref, near_ref, out_ref):
    far = far_ref[...]
    for half in range(2):
        at = slice(half * 128, half * 128 + 128)
        out_ref[:, at] = pick(far, slab_ref[:, at], place_ref[:, at]) + near_ref[:, at]


def swap(value, axis, count):
    rows = value.shape[0]
    return lax.all_to_all(value.reshape(count, rows // count, 128), axis, 0, 0, tiled=True).reshape(rows, 128)


def arrange_green(flag_ref, green_ref, plane_ref, out_ref, other_ref):
    shared, ends, upper, straight = (flag_ref[i] == 1 for i in range(4))
    place = lax.broadcasted_iota(jnp.int32, (KZ, GX), 0) == 0
    group = lax.broadcasted_iota(jnp.int32, (32, 128), 1) // KZ

    def lay(rows):
        turned = jnp.transpose(jnp.concatenate([rows] * 8, axis=0))
        halves = []
        for half in range(2):
            total = jnp.zeros((32, 128), F32)
            for k2 in range(8):
                start = (half * 8 + k2) * 32
                total = jnp.where(group == k2, turned[start : start + 32], total)
            halves.append(total)
        return jnp.concatenate(halves, axis=1)

    for k in range(8):
        up = green_ref[k, :KZ, :]
        down = jnp.concatenate([green_ref[k, KZ - i : KZ - i + 1, :] for i in range(KZ)], axis=0)
        rows = jnp.where(straight, up, down)
        zero, plane = rows[0:1], plane_ref[k : k + 1, :]
        line = jnp.where(upper, plane, zero)
        if k == 0:
            line = jnp.where(ends, 0.5 * (zero + plane), line)
            differ = jnp.where(ends, 0.5 * (zero - plane), 0.0)
            other_ref[...] = lay(jnp.where(place, differ, 0.0))
        rows = jnp.where(place & shared, line, rows)
        laid = lay(rows)
        for half in range(2):
            out_ref[half, k * 32 : k * 32 + 32, :] = laid[:, half * 128 : half * 128 + 128]


def per_device(strength, stencil_weight, slot_panel, slot_anchor, green_spectrum, near_index, near_factor):
    slab = lax.axis_index("slab")
    pencil = lax.axis_index("pencil")
    ends = (pencil == 0) & ((slab == 0) | (slab == 16))
    flags = jnp.stack([pencil == 0, ends, slab >= 16, pencil < 4]).astype(jnp.int32)
    around = jnp.stack([(slab + N_SLAB - 1) % N_SLAB, (slab + 1) % N_SLAB])
    flags = jnp.concatenate([flags, around.astype(jnp.int32) * LINES + 13])
    row = strength.reshape(1, PAN_DEV)

    z_fwd, z_bwd = (pair(t) for t in z_tables())
    y_fwd, y_fwd_shared, y_bwd, y_bwd_shared = (pair(t) for t in y_tables())
    rows, twist, lanes = x_tables()
    rows, lanes = pair(rows), pair(lanes)
    twist = jnp.asarray(twist, F32)

    anchor = slot_anchor.reshape(N_SLAB, 2, 12).transpose(1, 0, 2).reshape(1, 1, SLOTS)

    shape = jax.ShapeDtypeStruct
    payload = call(
        pack, shape((ROWS, 128), F32), slot_panel, stencil_weight, row,
        scratch=[pltpu.VMEM((SLOTS, 128), F32)], limit=56,
    )

    payload, spectrum = lax.optimization_barrier((payload, green_spectrum))
    plane = lax.ppermute(spectrum[:, 0, :], "pencil", [(4, 0)])
    arrived = lax.all_to_all(payload.reshape(N_SLAB, 1, LINES * 128), "slab", 0, 0, tiled=True).reshape(ROWS, 128)
    green, other = call(
        arrange_green, [shape((2, 256, 128), F32), shape((32, 256), F32)], flags, spectrum, plane, smem=(0,), limit=LIMIT_N
    )
    arrived, green, other, flags, anchor = lax.optimization_barrier((arrived, green, other, flags, anchor))
    near_field, *home = call(
        near, [shape((1, PAN_DEV), F32)] + [shape((8, PAN_DEV), jnp.int32)] * 2, flags, arrived, slot_panel, row, near_index, near_factor,
        smem=(0,), limit=LIMIT_N,
    )
    after_z, weights = call(
        project, [shape((1024, 128), F32), shape((128, SLOTS), F32)], arrived, anchor, z_fwd,
        scratch=[pltpu.VMEM((128, SLOTS), F32), pltpu.VMEM((PENCIL_ROWS, SLOTS), jnp.int32)]
        + [pltpu.VMEM((512, SLOTS), F32), pltpu.VMEM((SLOTS // 2, 128), F32)]
        + [pltpu.VMEM((EDGE, 512, SLOTS), BF16)] * 2,
        limit=LIMIT_P,
    )
    by_y = swap(after_z, "pencil", N_PENCIL)
    after_y = call(
        y_forward, shape((1024, 128), F32), flags, by_y, y_fwd, y_fwd_shared,
        scratch=[pltpu.VMEM((512, 256), F32)], smem=(0,), limit=LIMIT_Y,
    )
    by_x = swap(after_y, "slab", N_SLAB)
    after_x = call(
        x_stage, shape((1024, 128), F32), flags, by_x, green, other, twist, rows, lanes,
        scratch=[pltpu.VMEM((2, 256, 128), F32)] * 2, smem=(0,), limit=LIMIT_X,
    )
    back_x = swap(after_x, "slab", N_SLAB)
    back_y = call(
        y_backward, shape((1024, 128), F32), flags, back_x, y_bwd, y_bwd_shared,
        scratch=[pltpu.VMEM((512, 256), F32)], smem=(0,), limit=LIMIT_Y,
    )
    by_z = swap(back_y, "pencil", N_PENCIL)
    sampled = call(
        sample, shape((N_SLAB, 128), F32), by_z, weights, anchor, z_bwd,
        scratch=[pltpu.VMEM((PENCIL_ROWS, SLOTS), jnp.int32), pltpu.VMEM((512, 256), F32)]
        + [pltpu.VMEM((512, SLOTS), F32), pltpu.VMEM((EDGE, 512, SLOTS), F32)],
        limit=LIMIT_S,
    )
    far = lax.all_to_all(sampled, "slab", 0, 0, tiled=True)
    return call(finish, shape((1, PAN_DEV), F32), far, *home, near_field, limit=40).reshape(PAN_DEV)


def solution(mesh):
    in_specs = (
        P(("slab", "pencil")),
        P(None, ("slab", "pencil")),
        P("slab", "pencil", None),
        P("slab", "pencil", None),
        P("slab", "pencil", None),
        P(None, ("slab", "pencil")),
        P(None, ("slab", "pencil")),
    )
    out_specs = P(("slab", "pencil"))
    return jax.shard_map(
        per_device, mesh=mesh, in_specs=in_specs, out_specs=out_specs, check_vma=False
    )
```

```python
import math

import jax
import jax.numpy as jnp
import numpy as np
from jax import lax
from jax.experimental import pallas as pl
from jax.experimental.pallas import tpu as pltpu
from jax.sharding import PartitionSpec as P

GX = 512
GY = 256
GZ = 256
EDGE = 4
PAN_DEV = 256
CAP = 24
N_SLAB = 32
N_PENCIL = 8
SLOTS = N_SLAB * CAP
SLAB_ROWS = 16
PENCIL_ROWS = 32
STENCIL = 64
KZ = 16
LINES = 15
ROWS = LINES * N_SLAB
LIMIT_P, LIMIT_Y, LIMIT_X, LIMIT_S = 48, 40, 51, 40
LIMIT_N = 40
F32 = jnp.float32
BF16 = jnp.bfloat16


def kz_of(pencil, place):
    return np.where(
        pencil < 4, 32 * pencil + place, -(32 * (7 - pencil) + 16 + place)
    )


def z_tables():
    pencil, ri, place = np.meshgrid(np.arange(8), np.arange(2), np.arange(KZ), indexing="ij")
    kz = kz_of(pencil, place).reshape(-1)
    ri = ri.reshape(-1)
    shared = (pencil.reshape(-1) == 0) & (place.reshape(-1) == 0)
    z = np.arange(GZ)
    theta = 2 * np.pi * ((z[:, None] * kz[None, :]) % GZ) / GZ
    sign = 1.0 - 2.0 * (z % 2)
    forward = np.where(ri == 0, np.cos(theta), -np.sin(theta))
    forward = np.where(shared & (ri == 1), sign[:, None], forward)
    scale = np.where(shared, 1.0, 2.0) / GZ
    backward = (forward * scale).T
    return forward, backward


def y_tables():
    slab, ro, k8 = (a.reshape(-1) for a in np.meshgrid(np.arange(32), np.arange(2), np.arange(8), indexing="ij"))
    pencil, ri, y32 = (a.reshape(-1) for a in np.meshgrid(np.arange(8), np.arange(2), np.arange(32), indexing="ij"))
    ky = (8 * slab + k8)[:, None]
    ro = ro[:, None]
    y = (32 * pencil + y32)[None, :]
    ri = ri[None, :]
    theta = 2 * np.pi * ((ky * y) % GY) / GY
    cosine, sine = np.cos(theta), np.sin(theta)
    forward = np.where(ro == ri, cosine, np.where(ro == 0, sine, -sine))
    backward = forward.T / GY
    part = np.where(ro == 0, cosine, -sine)
    ends = (ky == 0) | (ky == 128)
    part = np.where(ends, np.where(ro == 0, 1.0, 1.0 - 2.0 * (y % 2)), part)
    first = part[:, np.broadcast_to(ri == 0, y.shape)[0]]
    shared = np.stack([first[:256], first[256:]])
    scale = (np.where(ends, 1.0, 2.0) / GY).reshape(2, 256, 1)
    shared_back = (shared * scale).transpose(0, 2, 1)
    return forward, shared, backward, shared_back


def x_tables():
    ro, k1 = (a.reshape(-1)[:, None] for a in np.meshgrid(np.arange(2), np.arange(32), indexing="ij"))
    ri, slab = (a.reshape(-1)[None, :] for a in np.meshgrid(np.arange(2), np.arange(32), indexing="ij"))
    theta = 2 * np.pi * ((k1 * slab) % 32) / 32
    rows = np.where(ro == ri, np.cos(theta), np.where(ro == 0, np.sin(theta), -np.sin(theta)))
    x16 = np.arange(16)
    twist = 2 * np.pi * np.arange(32)[:, None] * x16[None, :] / GX
    twist = np.repeat(twist, KZ, axis=1)
    inner = 2 * np.pi * ((x16[:, None] * x16[None, :]) % 16) / 16
    eye = np.eye(KZ)
    cosine, sine = np.kron(np.cos(inner), eye), np.kron(np.sin(inner), eye)
    lanes = np.block([[cosine, -sine], [sine, cosine]])
    return rows, np.stack([np.cos(twist), np.sin(twist)]), lanes


def pair(table):
    high = np.asarray(table, np.float32).astype(jnp.bfloat16)
    low = (np.asarray(table, np.float64) - high.astype(np.float64)).astype(jnp.bfloat16)
    return jnp.asarray(np.stack([high, low]))


def split(value):
    high = value.astype(BF16)
    return high, (value - high.astype(F32)).astype(BF16)


def mm(left, right):
    return jnp.dot(left, right, preferred_element_type=F32)


def mm_nt(left, right):
    return lax.dot_general(left, right, (((1,), (1,)), ((), ())), preferred_element_type=F32)


def mm3(left, right):
    return mm(left[0], right[0]) + (mm(left[0], right[1]) + mm(left[1], right[0]))


def call(kernel, out_shape, *args, scratch=(), smem=(), limit):
    space = {i: pltpu.SMEM for i in smem}
    out_spec = pl.BlockSpec(memory_space=pltpu.VMEM)
    return pl.pallas_call(
        kernel,
        out_shape=out_shape,
        in_specs=[pl.BlockSpec(memory_space=space.get(i, pltpu.VMEM)) for i in range(len(args))],
        out_specs=[out_spec] * len(out_shape) if isinstance(out_shape, list) else out_spec,
        scratch_shapes=list(scratch),
        compiler_params=pltpu.CompilerParams(vmem_limit_bytes=limit * 2**20),
        name=kernel.__name__,
    )(*args)


def swap_groups(tiles):
    tiles = list(tiles)
    group = lax.broadcasted_iota(jnp.int32, tiles[0].shape, 1) // 16
    for bit in range(3):
        step = 1 << bit
        upper = (group & step) != 0
        for i in range(8):
            if i & step:
                continue
            low, high = tiles[i], tiles[i + step]
            tiles[i] = jnp.where(upper, pltpu.roll(high, 16 * step, 1), low)
            tiles[i + step] = jnp.where(upper, high, pltpu.roll(low, 128 - 16 * step, 1))
    return tiles


def lookup(tables, index):
    inner, outer = index & 127, index >> 7
    found = jnp.zeros((8, 128), F32)
    for part, table in enumerate(tables):
        row = jnp.broadcast_to(table, (8, 128))
        value = jnp.take_along_axis(row, inner, axis=1, mode="promise_in_bounds")
        found = jnp.where(outer == part, value, found)
    return found


def quotient(value, divisor):
    return ((value.astype(F32) + 0.5) * (1.0 / divisor)).astype(jnp.int32)


def pick(table, slab, place):
    sublane = lax.broadcasted_iota(jnp.int32, (8, 128), 0)
    total = jnp.zeros((8, 128), F32)
    for block in range(N_SLAB // 8):
        value = jnp.take_along_axis(table[block * 8 : block * 8 + 8], place, axis=1, mode="promise_in_bounds")
        total = jnp.where(slab == sublane + block * 8, value, total)
    return jnp.sum(total, axis=0, keepdims=True)


def pack(slot_ref, weight_ref, strength_ref, out_ref, by_slot_ref):
    strength = strength_ref[...]
    halves = [strength[:, :128], strength[:, 128:]]
    tables = []
    for tile in range(SLOTS // 128):
        at = slice(tile * 128, tile * 128 + 128)
        index = jnp.broadcast_to(slot_ref[0, :, at], (8, 128))
        inner, outer = index & 127, index >> 7
        tables.append(lookup(halves, index)[:1])
        found = []
        for block in range(8):
            low, high = (
                jnp.take_along_axis(
                    weight_ref[block * 8 : block * 8 + 8, half * 128 : half * 128 + 128],
                    inner,
                    axis=1,
                    mode="promise_in_bounds",
                )
                for half in range(2)
            )
            found.append(jnp.where(outer == 0, low, jnp.where(outer == 1, high, 0.0)))
        by_slot_ref[at, :] = jnp.transpose(jnp.concatenate(found * 2, axis=0))
    first = lax.broadcasted_iota(jnp.int32, (12, 128), 1) < STENCIL
    for d in range(N_SLAB):
        out_ref[d * LINES : d * LINES + 12, :] = jnp.where(
            first, by_slot_ref[d * CAP : d * CAP + 12, :], by_slot_ref[d * CAP + 12 : d * CAP + 24, :]
        )
    sent = []
    for block in range(N_SLAB // 8):
        slab = lax.broadcasted_iota(jnp.int32, (8, 128), 0) + block * 8
        place = lax.broadcasted_iota(jnp.int32, (8, 128), 1)
        sent.append(lookup(tables, jnp.where(place < CAP, slab * CAP + place, SLOTS)))
    out_ref[pl.ds(12, N_SLAB, stride=LINES), :] = jnp.concatenate(sent, axis=0)
    for half in range(2):
        out_ref[pl.ds(13 + half, N_SLAB, stride=LINES), :] = jnp.broadcast_to(halves[half], (N_SLAB, 128))


def anchor_parts(anchor):
    return anchor >> 13, (anchor >> 8) & 31, anchor & 255


def z_hot(third, dz):
    z = lax.broadcasted_iota(jnp.int32, (GZ, SLOTS), 0)
    return jnp.where(z - dz == third, 1.0, 0.0).astype(BF16)


def y_place(second, y_ref):
    rel = lax.broadcasted_iota(jnp.int32, (PENCIL_ROWS, SLOTS), 0) - second
    y_ref[...] = jnp.where((rel >= 0) & (rel < EDGE), rel, EDGE)


def stencil_row(x, dz, first, weight_ref):
    total = jnp.zeros((8, SLOTS), F32)
    for dx in range(EDGE):
        start = dx * 32 + dz * 8
        total = jnp.where(first == x - dx, weight_ref[start : start + 8, :], total)
    return total


def place_rows(rows, y_ref):
    out = []
    for block in range(PENCIL_ROWS // 8):
        pieces = []
        for lane in range(SLOTS // 128):
            at = slice(lane * 128, lane * 128 + 128)
            index = y_ref[block * 8 : block * 8 + 8, at]
            pieces.append(jnp.take_along_axis(rows[:, at], index, axis=0, mode="promise_in_bounds"))
        out.append(jnp.concatenate(pieces, axis=1))
    return jnp.concatenate(out, axis=0)


def slot_order():
    row = lax.broadcasted_iota(jnp.int32, (256, 128), 0)
    lane = lax.broadcasted_iota(jnp.int32, (256, 128), 1)
    dy = row & 7
    picked = ((row >> 5) << 4) + (dy << 2) + ((row >> 3) & 3)
    return jnp.where((lane == picked) & (dy < EDGE), 1.0, 0.0).astype(BF16)


def project(flag_ref, arrived_ref, anchor_ref, z_ref, own_ref, index_ref, factor_ref, out_ref, weight_ref, near_ref, scaled_ref, y_ref, packed_ref, high_ref, low_ref):
    near(flag_ref, arrived_ref, own_ref, index_ref, factor_ref, near_ref)
    for s in range(N_SLAB):
        packed_ref[s * 12 : s * 12 + 12, :] = arrived_ref[s * LINES : s * LINES + 12, :]
    packed = jnp.concatenate(split(packed_ref[...]), axis=0)
    order = slot_order()
    turned = [mm_nt(order[half * 128 : half * 128 + 128, :], packed) for half in range(2)]
    turned = [part[:, : SLOTS // 2] + part[:, SLOTS // 2 :] for part in turned]
    weights = jnp.concatenate(turned, axis=1)
    weight_ref[...] = weights
    sent = arrived_ref[pl.ds(12, N_SLAB, stride=LINES), :]
    strength = []
    for tile in range(SLOTS // 128):
        slot = lax.broadcasted_iota(jnp.int32, (8, 128), 1) + tile % 3 * 128
        slab = quotient(slot, 12)
        strength.append(pick(sent, slab, slot - slab * 12 + tile // 3 * 12))
    scaled_ref[...] = weights * jnp.concatenate(strength, axis=1)
    first, second, third = anchor_parts(anchor_ref[0])
    y_place(second, y_ref)
    hot = z_hot(third, 0)
    charge = jnp.zeros((512, GZ), F32)
    for dz in range(EDGE):
        for x in range(SLAB_ROWS):
            at = slice(x * PENCIL_ROWS, x * PENCIL_ROWS + PENCIL_ROWS)
            high, low = split(place_rows(stencil_row(x, dz, first, scaled_ref), y_ref))
            high_ref[dz, at, :] = high
            low_ref[dz, at, :] = low
        part = mm_nt(high_ref[dz], hot) + mm_nt(low_ref[dz], hot)
        charge += pltpu.roll(part, dz, 1) if dz else part
    after = mm3(split(charge), z_ref[...])
    for half in range(2):
        for quarter in range(2):
            tiles = [
                after[x * 32 : x * 32 + 32, quarter * 128 : quarter * 128 + 128]
                for x in range(half * 8, half * 8 + 8)
            ]
            for g, tile in enumerate(swap_groups(tiles)):
                pencil, ri = quarter * 4 + g // 2, g % 2
                start = pencil * 128 + half * 64 + ri * 32
                out_ref[start : start + 32, :] = tile


def gathered(ref, count, rows):
    block = ref[...].reshape(count, 2, rows, 128)
    return jnp.concatenate([block[:, half].reshape(count * rows, 128) for half in range(2)], axis=1)


def scattered(value, ref, count, rows):
    for half in range(2):
        part = value[:, half * 128 : half * 128 + 128].reshape(count, rows, 128)
        for i in range(count):
            ref[(i * 2 + half) * rows : (i * 2 + half + 1) * rows, :] = part[i]


def shared_lane(shape):
    return lax.broadcasted_iota(jnp.int32, shape, 1) % KZ == 0


def halves_of(value, group):
    return value[group * 256 : group * 256 + 256]


def planes_of(value, plane):
    return value.reshape(8, 2, 32, 256)[:, plane].reshape(256, 256)


def y_stage(source, target, join, fuse):
    def kernel(flag_ref, in_ref, table_ref, shared_ref, out_ref, work_ref):
        data = split(gathered(in_ref, *source))
        work_ref[...] = mm3(table_ref[...], data)

        @pl.when(flag_ref[0] == 1)
        def _():
            parts = [[join(part, group) for part in data] for group in range(2)]
            other = fuse([mm3(shared_ref[:, group], parts[group]) for group in range(2)])
            work_ref[...] = jnp.where(shared_lane(other.shape), other, work_ref[...])

        scattered(work_ref[...], out_ref, *target)

    return kernel


def y_forward(*refs):
    y_stage((8, 64), (32, 16), planes_of, lambda parts: jnp.concatenate(parts, axis=0))(*refs)


def y_backward(*refs):
    def fuse(parts):
        return jnp.stack([part.reshape(8, 32, 256) for part in parts], axis=1).reshape(512, 256)

    y_stage((32, 16), (8, 64), halves_of, fuse)(*refs)


def x_stage(flag_ref, in_ref, green_ref, other_ref, twist_ref, row_ref, lane_ref, out_ref, re_ref, im_ref):
    row_tables, lane_tables = row_ref[...], lane_ref[...]
    cosine, sine = twist_ref[0], twist_ref[1]

    def line(k, ri):
        return [in_ref[pl.ds(half * 16 + ri * 8 + k, 32, stride=32), :] for half in range(2)]

    def turn(re, im):
        return jnp.concatenate([re * cosine + im * sine, im * cosine - re * sine], axis=1)

    data = [jnp.concatenate(sum((line(k, ri) for k in range(8)), []), axis=1) for ri in range(2)]
    rows = mm3(row_tables, split(jnp.concatenate(data, axis=0)))
    columns = [slice(k * 256, k * 256 + 256) for k in range(8)]
    full = mm3(split(jnp.concatenate([turn(rows[:32, at], rows[32:, at]) for at in columns], axis=0)), lane_tables)
    for half in range(2):
        at = slice(half * 128, half * 128 + 128)
        re_ref[half] = full[:, at] * green_ref[half]
        im_ref[half] = full[:, 256 + half * 128 : 384 + half * 128] * green_ref[half]

    @pl.when(flag_ref[1] == 1)
    def _():
        conjugate = jnp.concatenate([data[0][:, :256], -data[1][:, :256]], axis=0)
        rows = mm3(row_tables, split(conjugate))
        mirror = mm3(split(turn(rows[:32], rows[32:])), lane_tables)
        for half in range(2):
            at = slice(half * 128, half * 128 + 128)
            other = other_ref[:, at]
            re_ref[half, :32, :] += mirror[:, at] * other
            im_ref[half, :32, :] += mirror[:, 256 + half * 128 : 384 + half * 128] * other

    product = jnp.concatenate([re_ref[0], re_ref[1], -im_ref[0], -im_ref[1]], axis=1)
    back = mm3(split(product), lane_tables)
    back = [turn(back[k * 32 : k * 32 + 32, :256], back[k * 32 : k * 32 + 32, 256:]) for k in range(8)]
    data = [jnp.concatenate([part[:, ri * 256 : ri * 256 + 256] for part in back], axis=1) for ri in range(2)]
    rows = mm3(row_tables, split(jnp.concatenate(data, axis=0)))
    for k in range(8):
        for ri in range(2):
            for half in range(2):
                part = rows[ri * 32 : ri * 32 + 32, k * 256 + half * 128 : k * 256 + half * 128 + 128]
                out_ref[pl.ds(half * 16 + ri * 8 + k, 32, stride=32), :] = part * ((1 - 2 * ri) / GX)


def sample(in_ref, weight_ref, anchor_ref, z_ref, out_ref, y_ref, after_ref, grid_ref):
    for half in range(2):
        for quarter in range(2):
            tiles = []
            for g in range(8):
                pencil, ri = quarter * 4 + g // 2, g % 2
                start = pencil * 128 + half * 64 + ri * 32
                tiles.append(in_ref[start : start + 32, :])
            for i, tile in enumerate(swap_groups(tiles)):
                x = half * 8 + i
                after_ref[x * 32 : x * 32 + 32, quarter * 128 : quarter * 128 + 128] = tile
    high, low = split(mm3(split(after_ref[...]), z_ref[...]))
    first, second, third = anchor_parts(anchor_ref[0])
    y_place(second, y_ref)

    total = jnp.zeros((8, SLOTS), F32)
    for dz in range(EDGE):
        hot = z_hot(third, dz)
        grid_ref[dz] = mm(high, hot) + mm(low, hot)
        for x in range(SLAB_ROWS):
            rows = place_rows(stencil_row(x, dz, first, weight_ref), y_ref)
            cells = grid_ref[dz, x * 32 : x * 32 + 32, :] * rows
            total += jnp.sum(cells.reshape(4, 8, SLOTS), axis=0)
    far = jnp.sum(total, axis=0, keepdims=True)
    tables = [far[:, tile * 128 : tile * 128 + 128] for tile in range(SLOTS // 128)]
    for block in range(N_SLAB // 8):
        slab = lax.broadcasted_iota(jnp.int32, (8, 128), 0) + block * 8
        place = lax.broadcasted_iota(jnp.int32, (8, 128), 1)
        index = slab * 12 + place + jnp.where(place < 12, 0, SLOTS // 2 - 12)
        out_ref[block * 8 : block * 8 + 8, :] = lookup(tables, jnp.where(place < CAP, index, SLOTS))


def home(slot_ref, slab_ref, place_ref):
    slots = jnp.transpose(jnp.broadcast_to(slot_ref[0], (128, SLOTS)))
    panel = lax.broadcasted_iota(jnp.int32, (SLOTS, 128), 1)
    slot = lax.broadcasted_iota(jnp.int32, (SLOTS, 128), 0).astype(F32)
    for half in range(2):
        at = slice(half * 128, half * 128 + 128)
        own = jnp.sum(jnp.where(slots == panel + half * 128, slot, 0.0), axis=0, keepdims=True)
        own = jnp.broadcast_to(own, (8, 128)).astype(jnp.int32)
        slab = quotient(own, CAP)
        slab_ref[:, at] = slab
        place_ref[:, at] = own - slab * CAP


def near(flag_ref, arrived_ref, own_ref, index_ref, factor_ref, out_ref):
    before = [arrived_ref[pl.ds(flag_ref[4] + half, 1), :] for half in range(2)]
    after = [arrived_ref[pl.ds(flag_ref[5] + half, 1), :] for half in range(2)]
    tables = before + [own_ref[:, :128], own_ref[:, 128:]] + after
    for lane in range(2):
        total = jnp.zeros((8, 128), F32)
        for block in range(4):
            at = (slice(block * 8, block * 8 + 8), slice(lane * 128, lane * 128 + 128))
            total += lookup(tables, index_ref[at]) * factor_ref[at]
        out_ref[:, lane * 128 : lane * 128 + 128] = jnp.sum(total, axis=0, keepdims=True)


def finish(far_ref, slab_ref, place_ref, near_ref, out_ref):
    far = far_ref[...]
    for half in range(2):
        at = slice(half * 128, half * 128 + 128)
        out_ref[:, at] = pick(far, slab_ref[:, at], place_ref[:, at]) + near_ref[:, at]


def swap(value, axis, count):
    rows = value.shape[0]
    return lax.all_to_all(value.reshape(count, rows // count, 128), axis, 0, 0, tiled=True).reshape(rows, 128)


def arrange_green(flag_ref, green_ref, plane_ref, across_ref, out_ref, other_ref):
    shared, ends, upper, straight = (flag_ref[i] == 1 for i in range(4))
    place = lax.broadcasted_iota(jnp.int32, (KZ, GX), 0) == 0
    group = lax.broadcasted_iota(jnp.int32, (32, 128), 1) // KZ

    def lay(rows):
        turned = jnp.transpose(jnp.concatenate([rows] * 8, axis=0))
        halves = []
        for half in range(2):
            total = jnp.zeros((32, 128), F32)
            for k2 in range(8):
                start = (half * 8 + k2) * 32
                total = jnp.where(group == k2, turned[start : start + 32], total)
            halves.append(total)
        return jnp.concatenate(halves, axis=1)

    for k in range(8):
        up = green_ref[k, :KZ, :]
        down = jnp.concatenate([green_ref[k, KZ - i : KZ - i + 1, :] for i in range(KZ)], axis=0)
        rows = jnp.where(straight, up, down)
        zero, plane = rows[0:1], plane_ref[k : k + 1, :]
        line = jnp.where(upper, plane, zero)
        if k == 0:
            across = across_ref[...]
            re, im = jnp.where(upper, across, zero), jnp.where(upper, plane, across)
            line = jnp.where(ends, 0.5 * (re + im), line)
            differ = jnp.where(ends, 0.5 * (re - im), 0.0)
            other_ref[...] = lay(jnp.where(place, differ, 0.0))
        rows = jnp.where(place & shared, line, rows)
        laid = lay(rows)
        for half in range(2):
            out_ref[half, k * 32 : k * 32 + 32, :] = laid[:, half * 128 : half * 128 + 128]


def per_device(strength, stencil_weight, slot_panel, slot_anchor, green_spectrum, near_index, near_factor):
    slab = lax.axis_index("slab")
    pencil = lax.axis_index("pencil")
    ends = (pencil == 0) & ((slab == 0) | (slab == 16))
    flags = jnp.stack([pencil == 0, ends, slab >= 16, pencil < 4]).astype(jnp.int32)
    around = jnp.stack([(slab + N_SLAB - 1) % N_SLAB, (slab + 1) % N_SLAB])
    flags = jnp.concatenate([flags, around.astype(jnp.int32) * LINES + 13])
    row = strength.reshape(1, PAN_DEV)

    z_fwd, z_bwd = (pair(t) for t in z_tables())
    y_fwd, y_fwd_shared, y_bwd, y_bwd_shared = (pair(t) for t in y_tables())
    rows, twist, lanes = x_tables()
    rows, lanes = pair(rows), pair(lanes)
    twist = jnp.asarray(twist, F32)

    anchor = slot_anchor.reshape(N_SLAB, 2, 12).transpose(1, 0, 2).reshape(1, 1, SLOTS)

    shape = jax.ShapeDtypeStruct
    payload = call(
        pack, shape((ROWS, 128), F32), slot_panel, stencil_weight, row,
        scratch=[pltpu.VMEM((SLOTS, 128), F32)], limit=56,
    )

    payload, spectrum, own_slots = lax.optimization_barrier((payload, green_spectrum, slot_panel))
    sent = spectrum[:, 0, :]
    plane = lax.ppermute(sent, "pencil", [(4, 0)])
    across = lax.ppermute(
        sent[:1], ("slab", "pencil"), [(16 * N_PENCIL, 0), (4, 16 * N_PENCIL)]
    )
    arrived = lax.all_to_all(payload.reshape(N_SLAB, 1, LINES * 128), "slab", 0, 0, tiled=True).reshape(ROWS, 128)
    green, other = call(
        arrange_green, [shape((2, 256, 128), F32), shape((32, 256), F32)], flags, spectrum, plane, across, smem=(0,), limit=LIMIT_N
    )
    homes = call(home, [shape((8, PAN_DEV), jnp.int32)] * 2, own_slots, limit=LIMIT_N)
    arrived, green, other, flags, anchor, homes = lax.optimization_barrier(
        (arrived, green, other, flags, anchor, homes)
    )
    after_z, weights, near_field = call(
        project,
        [shape((1024, 128), F32), shape((128, SLOTS), F32), shape((1, PAN_DEV), F32)],
        flags, arrived, anchor, z_fwd, row, near_index, near_factor,
        scratch=[pltpu.VMEM((128, SLOTS), F32), pltpu.VMEM((PENCIL_ROWS, SLOTS), jnp.int32)]
        + [pltpu.VMEM((SLOTS // 2, 128), F32)]
        + [pltpu.VMEM((EDGE, 512, SLOTS), BF16)] * 2,
        smem=(0,), limit=LIMIT_P,
    )
    by_y = swap(after_z, "pencil", N_PENCIL)
    after_y = call(
        y_forward, shape((1024, 128), F32), flags, by_y, y_fwd, y_fwd_shared,
        scratch=[pltpu.VMEM((512, 256), F32)], smem=(0,), limit=LIMIT_Y,
    )
    by_x = swap(after_y, "slab", N_SLAB)
    after_x = call(
        x_stage, shape((1024, 128), F32), flags, by_x, green, other, twist, rows, lanes,
        scratch=[pltpu.VMEM((2, 256, 128), F32)] * 2, smem=(0,), limit=LIMIT_X,
    )
    back_x = swap(after_x, "slab", N_SLAB)
    back_y = call(
        y_backward, shape((1024, 128), F32), flags, back_x, y_bwd, y_bwd_shared,
        scratch=[pltpu.VMEM((512, 256), F32)], smem=(0,), limit=LIMIT_Y,
    )
    by_z = swap(back_y, "pencil", N_PENCIL)
    sampled = call(
        sample, shape((N_SLAB, 128), F32), by_z, weights, anchor, z_bwd,
        scratch=[pltpu.VMEM((PENCIL_ROWS, SLOTS), jnp.int32), pltpu.VMEM((512, 256), F32)]
        + [pltpu.VMEM((EDGE, 512, SLOTS), F32)],
        limit=LIMIT_S,
    )
    far = lax.all_to_all(sampled, "slab", 0, 0, tiled=True)
    return call(finish, shape((1, PAN_DEV), F32), far, *homes, near_field, limit=40).reshape(PAN_DEV)


def solution(mesh):
    in_specs = (
        P(("slab", "pencil")),
        P(None, ("slab", "pencil")),
        P("slab", "pencil", None),
        P("slab", "pencil", None),
        P("slab", "pencil", None),
        P(None, ("slab", "pencil")),
        P(None, ("slab", "pencil")),
    )
    out_specs = P(("slab", "pencil"))
    return jax.shard_map(
        per_device, mesh=mesh, in_specs=in_specs, out_specs=out_specs, check_vma=False
    )
```

```python
import math

import jax
import jax.numpy as jnp
import numpy as np
from jax import lax
from jax.experimental import pallas as pl
from jax.experimental.pallas import tpu as pltpu
from jax.sharding import PartitionSpec as P

GX = 512
GY = 256
GZ = 256
EDGE = 4
PAN_DEV = 256
CAP = 24
N_SLAB = 32
N_PENCIL = 8
SLOTS = N_SLAB * CAP
SLAB_ROWS = 16
PENCIL_ROWS = 32
STENCIL = 64
KZ = 16
LINES = 15
ROWS = LINES * N_SLAB
LIMIT_P, LIMIT_Y, LIMIT_X, LIMIT_S = 48, 40, 51, 40
LIMIT_N = 40
F32 = jnp.float32
BF16 = jnp.bfloat16


def kz_of(pencil, place):
    return np.where(
        pencil < 4, 32 * pencil + place, -(32 * (7 - pencil) + 16 + place)
    )


def z_tables():
    pencil, ri, place = np.meshgrid(np.arange(8), np.arange(2), np.arange(KZ), indexing="ij")
    kz = kz_of(pencil, place).reshape(-1)
    ri = ri.reshape(-1)
    shared = (pencil.reshape(-1) == 0) & (place.reshape(-1) == 0)
    z = np.arange(GZ)
    theta = 2 * np.pi * ((z[:, None] * kz[None, :]) % GZ) / GZ
    sign = 1.0 - 2.0 * (z % 2)
    forward = np.where(ri == 0, np.cos(theta), -np.sin(theta))
    forward = np.where(shared & (ri == 1), sign[:, None], forward)
    scale = np.where(shared, 1.0, 2.0) / GZ
    backward = (forward * scale).T
    return forward, backward


def y_tables():
    slab, ro, k8 = (a.reshape(-1) for a in np.meshgrid(np.arange(32), np.arange(2), np.arange(8), indexing="ij"))
    pencil, ri, y32 = (a.reshape(-1) for a in np.meshgrid(np.arange(8), np.arange(2), np.arange(32), indexing="ij"))
    ky = (8 * slab + k8)[:, None]
    ro = ro[:, None]
    y = (32 * pencil + y32)[None, :]
    ri = ri[None, :]
    theta = 2 * np.pi * ((ky * y) % GY) / GY
    cosine, sine = np.cos(theta), np.sin(theta)
    forward = np.where(ro == ri, cosine, np.where(ro == 0, sine, -sine))
    backward = forward.T / GY
    part = np.where(ro == 0, cosine, -sine)
    ends = (ky == 0) | (ky == 128)
    part = np.where(ends, np.where(ro == (ky == 128), cosine, 0.0), part)
    first = part[:, np.broadcast_to(ri == 0, y.shape)[0]]
    shared = np.stack([first[:256], first[256:]])
    scale = (np.where(ends, 1.0, 2.0) / GY).reshape(2, 256, 1)
    shared_back = (shared * scale).transpose(0, 2, 1)
    return forward, shared, backward, shared_back


def x_tables():
    ro, k1 = (a.reshape(-1)[:, None] for a in np.meshgrid(np.arange(2), np.arange(32), indexing="ij"))
    ri, slab = (a.reshape(-1)[None, :] for a in np.meshgrid(np.arange(2), np.arange(32), indexing="ij"))
    theta = 2 * np.pi * ((k1 * slab) % 32) / 32
    rows = np.where(ro == ri, np.cos(theta), np.where(ro == 0, np.sin(theta), -np.sin(theta)))
    x16 = np.arange(16)
    twist = 2 * np.pi * np.arange(32)[:, None] * x16[None, :] / GX
    twist = np.repeat(twist, KZ, axis=1)
    inner = 2 * np.pi * ((x16[:, None] * x16[None, :]) % 16) / 16
    eye = np.eye(KZ)
    cosine, sine = np.kron(np.cos(inner), eye), np.kron(np.sin(inner), eye)
    lanes = np.block([[cosine, -sine], [sine, cosine]])
    return rows, np.stack([np.cos(twist), np.sin(twist)]), lanes


def pair(table):
    high = np.asarray(table, np.float32).astype(jnp.bfloat16)
    low = (np.asarray(table, np.float64) - high.astype(np.float64)).astype(jnp.bfloat16)
    return jnp.asarray(np.stack([high, low]))


def split(value):
    high = value.astype(BF16)
    return high, (value - high.astype(F32)).astype(BF16)


def mm(left, right):
    return jnp.dot(left, right, preferred_element_type=F32)


def mm_nt(left, right):
    return lax.dot_general(left, right, (((1,), (1,)), ((), ())), preferred_element_type=F32)


def mm3(left, right):
    return mm(left[0], right[0]) + (mm(left[0], right[1]) + mm(left[1], right[0]))


def call(kernel, out_shape, *args, scratch=(), limit):
    out_spec = pl.BlockSpec(memory_space=pltpu.VMEM)
    return pl.pallas_call(
        kernel,
        out_shape=out_shape,
        in_specs=[pl.BlockSpec(memory_space=pltpu.VMEM)] * len(args),
        out_specs=[out_spec] * len(out_shape) if isinstance(out_shape, list) else out_spec,
        scratch_shapes=list(scratch),
        compiler_params=pltpu.CompilerParams(vmem_limit_bytes=limit * 2**20),
        name=kernel.__name__,
    )(*args)


def swap_groups(tiles):
    tiles = list(tiles)
    group = lax.broadcasted_iota(jnp.int32, tiles[0].shape, 1) // 16
    for bit in range(3):
        step = 1 << bit
        upper = (group & step) != 0
        for i in range(8):
            if i & step:
                continue
            low, high = tiles[i], tiles[i + step]
            tiles[i] = jnp.where(upper, pltpu.roll(high, 16 * step, 1), low)
            tiles[i + step] = jnp.where(upper, high, pltpu.roll(low, 128 - 16 * step, 1))
    return tiles


def position():
    slab, pencil = lax.axis_index("slab"), lax.axis_index("pencil")
    return slab, pencil, (pencil == 0) & ((slab == 0) | (slab == 16))


def lookup(tables, index):
    inner, outer = index & 127, index >> 7
    found = jnp.zeros((8, 128), F32)
    for part, table in enumerate(tables):
        row = jnp.broadcast_to(table, (8, 128))
        value = jnp.take_along_axis(row, inner, axis=1, mode="promise_in_bounds")
        found = jnp.where(outer == part, value, found)
    return found


def quotient(value, divisor):
    return ((value.astype(F32) + 0.5) * (1.0 / divisor)).astype(jnp.int32)


def pick(table, slab, place):
    sublane = lax.broadcasted_iota(jnp.int32, (8, 128), 0)
    total = jnp.zeros((8, 128), F32)
    for block in range(N_SLAB // 8):
        value = jnp.take_along_axis(table[block * 8 : block * 8 + 8], place, axis=1, mode="promise_in_bounds")
        total = jnp.where(slab == sublane + block * 8, value, total)
    return jnp.sum(total, axis=0, keepdims=True)


def pack(slot_ref, weight_ref, strength_ref, out_ref, by_slot_ref):
    strength = strength_ref[...]
    halves = [strength[:, :128], strength[:, 128:]]
    tables = []
    for tile in range(SLOTS // 128):
        at = slice(tile * 128, tile * 128 + 128)
        index = jnp.broadcast_to(slot_ref[0, :, at], (8, 128))
        inner, outer = index & 127, index >> 7
        tables.append(lookup(halves, index)[:1])
        found = []
        for block in range(8):
            low, high = (
                jnp.take_along_axis(
                    weight_ref[block * 8 : block * 8 + 8, half * 128 : half * 128 + 128],
                    inner,
                    axis=1,
                    mode="promise_in_bounds",
                )
                for half in range(2)
            )
            found.append(jnp.where(outer == 0, low, jnp.where(outer == 1, high, 0.0)))
        by_slot_ref[at, :] = jnp.transpose(jnp.concatenate(found * 2, axis=0))
    first = lax.broadcasted_iota(jnp.int32, (12, 128), 1) < STENCIL
    for d in range(N_SLAB):
        out_ref[d * LINES : d * LINES + 12, :] = jnp.where(
            first, by_slot_ref[d * CAP : d * CAP + 12, :], by_slot_ref[d * CAP + 12 : d * CAP + 24, :]
        )
    sent = []
    for block in range(N_SLAB // 8):
        slab = lax.broadcasted_iota(jnp.int32, (8, 128), 0) + block * 8
        place = lax.broadcasted_iota(jnp.int32, (8, 128), 1)
        sent.append(lookup(tables, jnp.where(place < CAP, slab * CAP + place, SLOTS)))
    out_ref[pl.ds(12, N_SLAB, stride=LINES), :] = jnp.concatenate(sent, axis=0)
    for half in range(2):
        out_ref[pl.ds(13 + half, N_SLAB, stride=LINES), :] = jnp.broadcast_to(halves[half], (N_SLAB, 128))


def anchor_parts(anchor):
    return anchor >> 13, (anchor >> 8) & 31, anchor & 255


def z_hot(third, dz):
    z = lax.broadcasted_iota(jnp.int32, (GZ, SLOTS), 0)
    return jnp.where(z - dz == third, 1.0, 0.0).astype(BF16)


def y_place(second, y_ref):
    rel = lax.broadcasted_iota(jnp.int32, (PENCIL_ROWS, SLOTS), 0) - second
    y_ref[...] = jnp.where((rel >= 0) & (rel < EDGE), rel, EDGE)


def stencil_row(x, dz, first, weight_ref):
    total = jnp.zeros((8, SLOTS), F32)
    for dx in range(EDGE):
        start = dx * 32 + dz * 8
        total = jnp.where(first == x - dx, weight_ref[start : start + 8, :], total)
    return total


def place_rows(rows, y_ref):
    out = []
    for block in range(PENCIL_ROWS // 8):
        pieces = []
        for lane in range(SLOTS // 128):
            at = slice(lane * 128, lane * 128 + 128)
            index = y_ref[block * 8 : block * 8 + 8, at]
            pieces.append(jnp.take_along_axis(rows[:, at], index, axis=0, mode="promise_in_bounds"))
        out.append(jnp.concatenate(pieces, axis=1))
    return jnp.concatenate(out, axis=0)


def slot_order():
    row = lax.broadcasted_iota(jnp.int32, (256, 128), 0)
    lane = lax.broadcasted_iota(jnp.int32, (256, 128), 1)
    dy = row & 7
    picked = ((row >> 5) << 4) + (dy << 2) + ((row >> 3) & 3)
    return jnp.where((lane == picked) & (dy < EDGE), 1.0, 0.0).astype(BF16)


def project(arrived_ref, anchor_ref, z_ref, out_ref, weight_ref, scaled_ref, y_ref, packed_ref, high_ref, low_ref):
    for s in range(N_SLAB):
        packed_ref[s * 12 : s * 12 + 12, :] = arrived_ref[s * LINES : s * LINES + 12, :]
    packed = jnp.concatenate(split(packed_ref[...]), axis=0)
    order = slot_order()
    turned = [mm_nt(order[half * 128 : half * 128 + 128, :], packed) for half in range(2)]
    turned = [part[:, : SLOTS // 2] + part[:, SLOTS // 2 :] for part in turned]
    weights = jnp.concatenate(turned, axis=1)
    weight_ref[...] = weights
    sent = arrived_ref[pl.ds(12, N_SLAB, stride=LINES), :]
    strength = []
    for tile in range(SLOTS // 128):
        slot = lax.broadcasted_iota(jnp.int32, (8, 128), 1) + tile % 3 * 128
        slab = quotient(slot, 12)
        strength.append(pick(sent, slab, slot - slab * 12 + tile // 3 * 12))
    scaled_ref[...] = weights * jnp.concatenate(strength, axis=1)
    first, second, third = anchor_parts(anchor_ref[0])
    y_place(second, y_ref)
    hot = z_hot(third, 0)
    charge = jnp.zeros((512, GZ), F32)
    for dz in range(EDGE):
        for x in range(SLAB_ROWS):
            at = slice(x * PENCIL_ROWS, x * PENCIL_ROWS + PENCIL_ROWS)
            high, low = split(place_rows(stencil_row(x, dz, first, scaled_ref), y_ref))
            high_ref[dz, at, :] = high
            low_ref[dz, at, :] = low
        part = mm_nt(high_ref[dz], hot) + mm_nt(low_ref[dz], hot)
        charge += pltpu.roll(part, dz, 1) if dz else part
    after = mm3(split(charge), z_ref[...])
    for half in range(2):
        for quarter in range(2):
            tiles = [
                after[x * 32 : x * 32 + 32, quarter * 128 : quarter * 128 + 128]
                for x in range(half * 8, half * 8 + 8)
            ]
            for g, tile in enumerate(swap_groups(tiles)):
                pencil, ri = quarter * 4 + g // 2, g % 2
                start = pencil * 128 + half * 64 + ri * 32
                out_ref[start : start + 32, :] = tile


def gathered(ref, count, rows):
    block = ref[...].reshape(count, 2, rows, 128)
    return jnp.concatenate([block[:, half].reshape(count * rows, 128) for half in range(2)], axis=1)


def scattered(value, ref, count, rows):
    for half in range(2):
        part = value[:, half * 128 : half * 128 + 128].reshape(count, rows, 128)
        for i in range(count):
            ref[(i * 2 + half) * rows : (i * 2 + half + 1) * rows, :] = part[i]


def shared_lane(shape):
    return lax.broadcasted_iota(jnp.int32, shape, 1) % KZ == 0


def sign_of_y():
    return (1 - 2 * (lax.broadcasted_iota(jnp.int32, (256, 256), 0) % 2)).astype(F32)


def shared_forward(value, data, table_ref):
    def plane(part, index):
        return part.reshape(8, 2, 32, 256)[:, index].reshape(256, 256)

    parts = [mm3(table_ref[:, i], [plane(part, i) for part in data]) for i in range(2)]
    row = lax.broadcasted_iota(jnp.int32, (256, 256), 0)
    second = jnp.sum(plane(value, 1), axis=0, keepdims=True)
    first = jnp.sum(plane(value, 0) * sign_of_y(), axis=0, keepdims=True)
    return jnp.concatenate([jnp.where(row == 8, second, parts[0]), jnp.where(row == 0, first, parts[1])], axis=0)


def shared_backward(value, data, table_ref):
    parts = [mm3(table_ref[:, i], [part[i * 256 : i * 256 + 256] for part in data]) for i in range(2)]
    parts[0] += value[256:257] * (sign_of_y() * (1.0 / GY))
    parts[1] += value[8:9] * (1.0 / GY)
    return jnp.stack([part.reshape(8, 32, 256) for part in parts], axis=1).reshape(512, 256)


def y_stage(source, target, shared):
    def kernel(in_ref, table_ref, shared_ref, out_ref, work_ref):
        value = gathered(in_ref, *source)
        data = split(value)
        work_ref[...] = mm3(table_ref[...], data)

        @pl.when(lax.axis_index("pencil") == 0)
        def _():
            other = shared(value, data, shared_ref)
            work_ref[...] = jnp.where(shared_lane(other.shape), other, work_ref[...])

        scattered(work_ref[...], out_ref, *target)

    return kernel


def y_forward(*refs):
    y_stage((8, 64), (32, 16), shared_forward)(*refs)


def y_backward(*refs):
    y_stage((32, 16), (8, 64), shared_backward)(*refs)


def x_stage(in_ref, green_ref, other_ref, twist_ref, row_ref, lane_ref, out_ref, re_ref, im_ref):
    row_tables, lane_tables = row_ref[...], lane_ref[...]
    cosine, sine = twist_ref[0], twist_ref[1]

    def line(k, ri):
        return [in_ref[pl.ds(half * 16 + ri * 8 + k, 32, stride=32), :] for half in range(2)]

    def turn(re, im):
        return jnp.concatenate([re * cosine + im * sine, im * cosine - re * sine], axis=1)

    data = [jnp.concatenate(sum((line(k, ri) for k in range(8)), []), axis=1) for ri in range(2)]
    rows = mm3(row_tables, split(jnp.concatenate(data, axis=0)))
    columns = [slice(k * 256, k * 256 + 256) for k in range(8)]
    full = mm3(split(jnp.concatenate([turn(rows[:32, at], rows[32:, at]) for at in columns], axis=0)), lane_tables)
    for half in range(2):
        at = slice(half * 128, half * 128 + 128)
        re_ref[half] = full[:, at] * green_ref[half]
        im_ref[half] = full[:, 256 + half * 128 : 384 + half * 128] * green_ref[half]

    @pl.when(position()[2])
    def _():
        conjugate = jnp.concatenate([data[0][:, :256], -data[1][:, :256]], axis=0)
        rows = mm3(row_tables, split(conjugate))
        mirror = mm3(split(turn(rows[:32], rows[32:])), lane_tables)
        for half in range(2):
            at = slice(half * 128, half * 128 + 128)
            other = other_ref[:, at]
            re_ref[half, :32, :] += mirror[:, at] * other
            im_ref[half, :32, :] += mirror[:, 256 + half * 128 : 384 + half * 128] * other

    product = jnp.concatenate([re_ref[0], re_ref[1], -im_ref[0], -im_ref[1]], axis=1)
    back = mm3(split(product), lane_tables)
    back = [turn(back[k * 32 : k * 32 + 32, :256], back[k * 32 : k * 32 + 32, 256:]) for k in range(8)]
    data = [jnp.concatenate([part[:, ri * 256 : ri * 256 + 256] for part in back], axis=1) for ri in range(2)]
    rows = mm3(row_tables, split(jnp.concatenate(data, axis=0)))
    for k in range(8):
        for ri in range(2):
            for half in range(2):
                part = rows[ri * 32 : ri * 32 + 32, k * 256 + half * 128 : k * 256 + half * 128 + 128]
                out_ref[pl.ds(half * 16 + ri * 8 + k, 32, stride=32), :] = part * ((1 - 2 * ri) / GX)


def sample(in_ref, weight_ref, anchor_ref, z_ref, out_ref, y_ref, after_ref, grid_ref):
    for half in range(2):
        for quarter in range(2):
            tiles = []
            for g in range(8):
                pencil, ri = quarter * 4 + g // 2, g % 2
                start = pencil * 128 + half * 64 + ri * 32
                tiles.append(in_ref[start : start + 32, :])
            for i, tile in enumerate(swap_groups(tiles)):
                x = half * 8 + i
                after_ref[x * 32 : x * 32 + 32, quarter * 128 : quarter * 128 + 128] = tile
    high, low = split(mm3(split(after_ref[...]), z_ref[...]))
    first, second, third = anchor_parts(anchor_ref[0])
    y_place(second, y_ref)

    total = jnp.zeros((8, SLOTS), F32)
    for dz in range(EDGE):
        hot = z_hot(third, dz)
        grid_ref[dz] = mm(high, hot) + mm(low, hot)
        for x in range(SLAB_ROWS):
            rows = place_rows(stencil_row(x, dz, first, weight_ref), y_ref)
            cells = grid_ref[dz, x * 32 : x * 32 + 32, :] * rows
            total += jnp.sum(cells.reshape(4, 8, SLOTS), axis=0)
    far = jnp.sum(total, axis=0, keepdims=True)
    tables = [far[:, tile * 128 : tile * 128 + 128] for tile in range(SLOTS // 128)]
    for block in range(N_SLAB // 8):
        slab = lax.broadcasted_iota(jnp.int32, (8, 128), 0) + block * 8
        place = lax.broadcasted_iota(jnp.int32, (8, 128), 1)
        index = slab * 12 + place + jnp.where(place < 12, 0, SLOTS // 2 - 12)
        out_ref[block * 8 : block * 8 + 8, :] = lookup(tables, jnp.where(place < CAP, index, SLOTS))


def home(slot_ref, slab_ref, place_ref):
    slots = jnp.transpose(jnp.broadcast_to(slot_ref[0], (128, SLOTS)))
    panel = lax.broadcasted_iota(jnp.int32, (SLOTS, 128), 1)
    slot = lax.broadcasted_iota(jnp.int32, (SLOTS, 128), 0).astype(F32)
    for half in range(2):
        at = slice(half * 128, half * 128 + 128)
        own = jnp.sum(jnp.where(slots == panel + half * 128, slot, 0.0), axis=0, keepdims=True)
        own = jnp.broadcast_to(own, (8, 128)).astype(jnp.int32)
        slab = quotient(own, CAP)
        slab_ref[:, at] = slab
        place_ref[:, at] = own - slab * CAP


def near(arrived_ref, own_ref, index_ref, factor_ref, out_ref):
    slab = lax.axis_index("slab")
    before, after = (
        [arrived_ref[pl.ds(lax.rem(slab + shift, N_SLAB) * LINES + 13 + half, 1), :] for half in range(2)]
        for shift in (N_SLAB - 1, 1)
    )
    tables = before + [own_ref[:, :128], own_ref[:, 128:]] + after
    for lane in range(2):
        total = jnp.zeros((8, 128), F32)
        for block in range(4):
            at = (slice(block * 8, block * 8 + 8), slice(lane * 128, lane * 128 + 128))
            total += lookup(tables, index_ref[at]) * factor_ref[at]
        out_ref[:, lane * 128 : lane * 128 + 128] = jnp.sum(total, axis=0, keepdims=True)


def finish(far_ref, slab_ref, place_ref, near_ref, out_ref):
    far = far_ref[...]
    for half in range(2):
        at = slice(half * 128, half * 128 + 128)
        out_ref[:, at] = pick(far, slab_ref[:, at], place_ref[:, at]) + near_ref[:, at]


def swap(value, axis, count):
    rows = value.shape[0]
    return lax.all_to_all(value.reshape(count, rows // count, 128), axis, 0, 0, tiled=True).reshape(rows, 128)


def arrange_green(green_ref, plane_ref, out_ref, other_ref):
    slab, pencil, ends = position()
    shared, upper, straight = pencil == 0, slab >= 16, pencil < 4
    place = lax.broadcasted_iota(jnp.int32, (KZ, GX), 0) == 0
    group = lax.broadcasted_iota(jnp.int32, (32, 128), 1) // KZ

    def lay(rows):
        turned = jnp.transpose(jnp.concatenate([rows] * 8, axis=0))
        halves = []
        for half in range(2):
            total = jnp.zeros((32, 128), F32)
            for k2 in range(8):
                start = (half * 8 + k2) * 32
                total = jnp.where(group == k2, turned[start : start + 32], total)
            halves.append(total)
        return jnp.concatenate(halves, axis=1)

    for k in range(8):
        up = green_ref[k, :KZ, :]
        down = jnp.concatenate([green_ref[k, KZ - i : KZ - i + 1, :] for i in range(KZ)], axis=0)
        rows = jnp.where(straight, up, down)
        zero, plane = rows[0:1], plane_ref[k : k + 1, :]
        line = jnp.where(upper, plane, zero)
        if k == 0:
            line = jnp.where(ends, 0.5 * (zero + plane), line)
            differ = jnp.where(ends, 0.5 * (zero - plane), 0.0)
            other_ref[...] = lay(jnp.where(place, differ, 0.0))
        rows = jnp.where(place & shared, line, rows)
        laid = lay(rows)
        for half in range(2):
            out_ref[half, k * 32 : k * 32 + 32, :] = laid[:, half * 128 : half * 128 + 128]


def per_device(strength, stencil_weight, slot_panel, slot_anchor, green_spectrum, near_index, near_factor):
    row = strength.reshape(1, PAN_DEV)

    z_fwd, z_bwd = (pair(t) for t in z_tables())
    y_fwd, y_fwd_shared, y_bwd, y_bwd_shared = (pair(t) for t in y_tables())
    rows, twist, lanes = x_tables()
    rows, lanes = pair(rows), pair(lanes)
    twist = jnp.asarray(twist, F32)

    anchor = slot_anchor.reshape(N_SLAB, 2, 12).transpose(1, 0, 2).reshape(1, 1, SLOTS)

    shape = jax.ShapeDtypeStruct
    payload = call(
        pack, shape((ROWS, 128), F32), slot_panel, stencil_weight, row,
        scratch=[pltpu.VMEM((SLOTS, 128), F32)], limit=56,
    )

    payload, spectrum, own_slots = lax.optimization_barrier((payload, green_spectrum, slot_panel))
    plane = lax.ppermute(spectrum[:, 0, :], "pencil", [(4, 0)])
    arrived = lax.all_to_all(payload.reshape(N_SLAB, 1, LINES * 128), "slab", 0, 0, tiled=True).reshape(ROWS, 128)
    green, other = call(
        arrange_green, [shape((2, 256, 128), F32), shape((32, 256), F32)], spectrum, plane, limit=LIMIT_N
    )
    homes = call(home, [shape((8, PAN_DEV), jnp.int32)] * 2, own_slots, limit=LIMIT_N)
    arrived, green, other, anchor, homes = lax.optimization_barrier((arrived, green, other, anchor, homes))
    near_field = call(
        near, shape((1, PAN_DEV), F32), arrived, row, near_index, near_factor, limit=LIMIT_N
    )
    after_z, weights = call(
        project, [shape((1024, 128), F32), shape((128, SLOTS), F32)], arrived, anchor, z_fwd,
        scratch=[pltpu.VMEM((128, SLOTS), F32), pltpu.VMEM((PENCIL_ROWS, SLOTS), jnp.int32)]
        + [pltpu.VMEM((SLOTS // 2, 128), F32)]
        + [pltpu.VMEM((EDGE, 512, SLOTS), BF16)] * 2,
        limit=LIMIT_P,
    )
    after_z, near_field = lax.optimization_barrier((after_z, near_field))
    by_y = swap(after_z, "pencil", N_PENCIL)
    after_y = call(
        y_forward, shape((1024, 128), F32), by_y, y_fwd, y_fwd_shared,
        scratch=[pltpu.VMEM((512, 256), F32)], limit=LIMIT_Y,
    )
    by_x = swap(after_y, "slab", N_SLAB)
    after_x = call(
        x_stage, shape((1024, 128), F32), by_x, green, other, twist, rows, lanes,
        scratch=[pltpu.VMEM((2, 256, 128), F32)] * 2, limit=LIMIT_X,
    )
    back_x = swap(after_x, "slab", N_SLAB)
    back_y = call(
        y_backward, shape((1024, 128), F32), back_x, y_bwd, y_bwd_shared,
        scratch=[pltpu.VMEM((512, 256), F32)], limit=LIMIT_Y,
    )
    by_z = swap(back_y, "pencil", N_PENCIL)
    sampled = call(
        sample, shape((N_SLAB, 128), F32), by_z, weights, anchor, z_bwd,
        scratch=[pltpu.VMEM((PENCIL_ROWS, SLOTS), jnp.int32), pltpu.VMEM((512, 256), F32)]
        + [pltpu.VMEM((EDGE, 512, SLOTS), F32)],
        limit=LIMIT_S,
    )
    far = lax.all_to_all(sampled, "slab", 0, 0, tiled=True)
    return call(finish, shape((1, PAN_DEV), F32), far, *homes, near_field, limit=40).reshape(PAN_DEV)


def solution(mesh):
    in_specs = (
        P(("slab", "pencil")),
        P(None, ("slab", "pencil")),
        P("slab", "pencil", None),
        P("slab", "pencil", None),
        P("slab", "pencil", None),
        P(None, ("slab", "pencil")),
        P(None, ("slab", "pencil")),
    )
    out_specs = P(("slab", "pencil"))
    return jax.shard_map(
        per_device, mesh=mesh, in_specs=in_specs, out_specs=out_specs, check_vma=False
    )
```

```python
import math

import jax
import jax.numpy as jnp
import numpy as np
from jax import lax
from jax.experimental import pallas as pl
from jax.experimental.pallas import tpu as pltpu
from jax.sharding import PartitionSpec as P

GX = 512
GY = 256
GZ = 256
EDGE = 4
PAN_DEV = 256
CAP = 24
N_SLAB = 32
N_PENCIL = 8
SLOTS = N_SLAB * CAP
SLAB_ROWS = 16
PENCIL_ROWS = 32
STENCIL = 64
KZ = 16
LINES = 15
ROWS = LINES * N_SLAB
LIMIT_P, LIMIT_Y, LIMIT_X, LIMIT_S = 48, 40, 51, 40
LIMIT_N = 40
F32 = jnp.float32
BF16 = jnp.bfloat16


def kz_of(pencil, place):
    return np.where(
        pencil < 4, 32 * pencil + place, -(32 * (7 - pencil) + 16 + place)
    )


def z_tables():
    pencil, ri, place = np.meshgrid(np.arange(8), np.arange(2), np.arange(KZ), indexing="ij")
    kz = kz_of(pencil, place).reshape(-1)
    ri = ri.reshape(-1)
    shared = (pencil.reshape(-1) == 0) & (place.reshape(-1) == 0)
    z = np.arange(GZ)
    theta = 2 * np.pi * ((z[:, None] * kz[None, :]) % GZ) / GZ
    sign = 1.0 - 2.0 * (z % 2)
    forward = np.where(ri == 0, np.cos(theta), -np.sin(theta))
    forward = np.where(shared & (ri == 1), sign[:, None], forward)
    scale = np.where(shared, 1.0, 2.0) / GZ
    backward = (forward * scale).T
    return forward, backward


def y_tables():
    slab, ro, k8 = (a.reshape(-1) for a in np.meshgrid(np.arange(32), np.arange(2), np.arange(8), indexing="ij"))
    pencil, ri, y32 = (a.reshape(-1) for a in np.meshgrid(np.arange(8), np.arange(2), np.arange(32), indexing="ij"))
    ky = (8 * slab + k8)[:, None]
    ro = ro[:, None]
    y = (32 * pencil + y32)[None, :]
    ri = ri[None, :]
    theta = 2 * np.pi * ((ky * y) % GY) / GY
    cosine, sine = np.cos(theta), np.sin(theta)
    forward = np.where(ro == ri, cosine, np.where(ro == 0, sine, -sine))
    backward = forward.T / GY
    part = np.where(ro == 0, cosine, -sine)
    ends = (ky == 0) | (ky == 128)
    part = np.where(ends, np.where(ro == (ky == 128), cosine, 0.0), part)
    first = part[:, np.broadcast_to(ri == 0, y.shape)[0]]
    shared = np.stack([first[:256], first[256:]])
    scale = (np.where(ends, 1.0, 2.0) / GY).reshape(2, 256, 1)
    shared_back = (shared * scale).transpose(0, 2, 1)
    return forward, shared, backward, shared_back


def x_tables():
    ro, k1 = (a.reshape(-1)[:, None] for a in np.meshgrid(np.arange(2), np.arange(32), indexing="ij"))
    ri, slab = (a.reshape(-1)[None, :] for a in np.meshgrid(np.arange(2), np.arange(32), indexing="ij"))
    theta = 2 * np.pi * ((k1 * slab) % 32) / 32
    rows = np.where(ro == ri, np.cos(theta), np.where(ro == 0, np.sin(theta), -np.sin(theta)))
    x16 = np.arange(16)
    twist = 2 * np.pi * np.arange(32)[:, None] * x16[None, :] / GX
    twist = np.repeat(twist, KZ, axis=1)
    inner = 2 * np.pi * ((x16[:, None] * x16[None, :]) % 16) / 16
    eye = np.eye(KZ)
    cosine, sine = np.kron(np.cos(inner), eye), np.kron(np.sin(inner), eye)
    lanes = np.block([[cosine, -sine], [sine, cosine]])
    return rows, np.stack([np.cos(twist), np.sin(twist)]), lanes


def pair(table):
    high = np.asarray(table, np.float32).astype(jnp.bfloat16)
    low = (np.asarray(table, np.float64) - high.astype(np.float64)).astype(jnp.bfloat16)
    return jnp.asarray(np.stack([high, low]))


def split(value):
    high = value.astype(BF16)
    return high, (value - high.astype(F32)).astype(BF16)


def mm(left, right):
    return jnp.dot(left, right, preferred_element_type=F32)


def mm_nt(left, right):
    return lax.dot_general(left, right, (((1,), (1,)), ((), ())), preferred_element_type=F32)


def mm3(left, right):
    return mm(left[0], right[0]) + (mm(left[0], right[1]) + mm(left[1], right[0]))


def call(kernel, out_shape, *args, scratch=(), limit):
    out_spec = pl.BlockSpec(memory_space=pltpu.VMEM)
    return pl.pallas_call(
        kernel,
        out_shape=out_shape,
        in_specs=[pl.BlockSpec(memory_space=pltpu.VMEM)] * len(args),
        out_specs=[out_spec] * len(out_shape) if isinstance(out_shape, list) else out_spec,
        scratch_shapes=list(scratch),
        compiler_params=pltpu.CompilerParams(vmem_limit_bytes=limit * 2**20),
        name=kernel.__name__,
    )(*args)


def swap_groups(tiles):
    tiles = list(tiles)
    group = lax.broadcasted_iota(jnp.int32, tiles[0].shape, 1) // 16
    for bit in range(3):
        step = 1 << bit
        upper = (group & step) != 0
        for i in range(8):
            if i & step:
                continue
            low, high = tiles[i], tiles[i + step]
            tiles[i] = jnp.where(upper, pltpu.roll(high, 16 * step, 1), low)
            tiles[i + step] = jnp.where(upper, high, pltpu.roll(low, 128 - 16 * step, 1))
    return tiles


def position():
    slab, pencil = lax.axis_index("slab"), lax.axis_index("pencil")
    return slab, pencil, (pencil == 0) & ((slab == 0) | (slab == 16))


def lookup(tables, index):
    inner, outer = index & 127, index >> 7
    found = jnp.zeros((8, 128), F32)
    for part, table in enumerate(tables):
        row = jnp.broadcast_to(table, (8, 128))
        value = jnp.take_along_axis(row, inner, axis=1, mode="promise_in_bounds")
        found = jnp.where(outer == part, value, found)
    return found


def quotient(value, divisor):
    return ((value.astype(F32) + 0.5) * (1.0 / divisor)).astype(jnp.int32)


def pick(table, slab, place):
    sublane = lax.broadcasted_iota(jnp.int32, (8, 128), 0)
    total = jnp.zeros((8, 128), F32)
    for block in range(N_SLAB // 8):
        value = jnp.take_along_axis(table[block * 8 : block * 8 + 8], place, axis=1, mode="promise_in_bounds")
        total = jnp.where(slab == sublane + block * 8, value, total)
    return jnp.sum(total, axis=0, keepdims=True)


def pack(slot_ref, weight_ref, strength_ref, out_ref, by_slot_ref):
    strength = strength_ref[...]
    halves = [strength[:, :128], strength[:, 128:]]
    tables = []
    for tile in range(SLOTS // 128):
        at = slice(tile * 128, tile * 128 + 128)
        index = jnp.broadcast_to(slot_ref[0, :, at], (8, 128))
        inner, outer = index & 127, index >> 7
        tables.append(lookup(halves, index)[:1])
        found = []
        for block in range(8):
            low, high = (
                jnp.take_along_axis(
                    weight_ref[block * 8 : block * 8 + 8, half * 128 : half * 128 + 128],
                    inner,
                    axis=1,
                    mode="promise_in_bounds",
                )
                for half in range(2)
            )
            found.append(jnp.where(outer == 0, low, jnp.where(outer == 1, high, 0.0)))
        by_slot_ref[at, :] = jnp.transpose(jnp.concatenate(found * 2, axis=0))
    first = lax.broadcasted_iota(jnp.int32, (12, 128), 1) < STENCIL
    for d in range(N_SLAB):
        out_ref[d * LINES : d * LINES + 12, :] = jnp.where(
            first, by_slot_ref[d * CAP : d * CAP + 12, :], by_slot_ref[d * CAP + 12 : d * CAP + 24, :]
        )
    sent = []
    for block in range(N_SLAB // 8):
        slab = lax.broadcasted_iota(jnp.int32, (8, 128), 0) + block * 8
        place = lax.broadcasted_iota(jnp.int32, (8, 128), 1)
        sent.append(lookup(tables, jnp.where(place < CAP, slab * CAP + place, SLOTS)))
    out_ref[pl.ds(12, N_SLAB, stride=LINES), :] = jnp.concatenate(sent, axis=0)
    for half in range(2):
        out_ref[pl.ds(13 + half, N_SLAB, stride=LINES), :] = jnp.broadcast_to(halves[half], (N_SLAB, 128))


def anchor_parts(anchor):
    return anchor >> 13, (anchor >> 8) & 31, anchor & 255


def z_hot(third, dz):
    z = lax.broadcasted_iota(jnp.int32, (GZ, SLOTS), 0)
    return jnp.where(z - dz == third, 1.0, 0.0).astype(BF16)


def y_place(second, y_ref):
    rel = lax.broadcasted_iota(jnp.int32, (PENCIL_ROWS, SLOTS), 0) - second
    y_ref[...] = jnp.where((rel >= 0) & (rel < EDGE), rel, EDGE)


def stencil_row(x, dz, first, weight_ref):
    total = jnp.zeros((8, SLOTS), F32)
    for dx in range(EDGE):
        start = dx * 32 + dz * 8
        total = jnp.where(first == x - dx, weight_ref[start : start + 8, :], total)
    return total


def place_rows(rows, y_ref):
    out = []
    for block in range(PENCIL_ROWS // 8):
        pieces = []
        for lane in range(SLOTS // 128):
            at = slice(lane * 128, lane * 128 + 128)
            index = y_ref[block * 8 : block * 8 + 8, at]
            pieces.append(jnp.take_along_axis(rows[:, at], index, axis=0, mode="promise_in_bounds"))
        out.append(jnp.concatenate(pieces, axis=1))
    return jnp.concatenate(out, axis=0)


def slot_order():
    row = lax.broadcasted_iota(jnp.int32, (256, 128), 0)
    lane = lax.broadcasted_iota(jnp.int32, (256, 128), 1)
    dy = row & 7
    picked = ((row >> 5) << 4) + (dy << 2) + ((row >> 3) & 3)
    return jnp.where((lane == picked) & (dy < EDGE), 1.0, 0.0).astype(BF16)


def project(arrived_ref, anchor_ref, z_ref, out_ref, weight_ref, scaled_ref, y_ref, packed_ref, high_ref, low_ref):
    for s in range(N_SLAB):
        packed_ref[s * 12 : s * 12 + 12, :] = arrived_ref[s * LINES : s * LINES + 12, :]
    packed = jnp.concatenate(split(packed_ref[...]), axis=0)
    order = slot_order()
    turned = [mm_nt(order[half * 128 : half * 128 + 128, :], packed) for half in range(2)]
    turned = [part[:, : SLOTS // 2] + part[:, SLOTS // 2 :] for part in turned]
    weights = jnp.concatenate(turned, axis=1)
    weight_ref[...] = weights
    sent = arrived_ref[pl.ds(12, N_SLAB, stride=LINES), :]
    strength = []
    for tile in range(SLOTS // 128):
        slot = lax.broadcasted_iota(jnp.int32, (8, 128), 1) + tile % 3 * 128
        slab = quotient(slot, 12)
        strength.append(pick(sent, slab, slot - slab * 12 + tile // 3 * 12))
    scaled_ref[...] = weights * jnp.concatenate(strength, axis=1)
    first, second, third = anchor_parts(anchor_ref[0])
    y_place(second, y_ref)
    hot = z_hot(third, 0)
    charge = jnp.zeros((512, GZ), F32)
    for dz in range(EDGE):
        for x in range(SLAB_ROWS):
            at = slice(x * PENCIL_ROWS, x * PENCIL_ROWS + PENCIL_ROWS)
            high, low = split(place_rows(stencil_row(x, dz, first, scaled_ref), y_ref))
            high_ref[dz, at, :] = high
            low_ref[dz, at, :] = low
        part = mm_nt(high_ref[dz], hot) + mm_nt(low_ref[dz], hot)
        charge += pltpu.roll(part, dz, 1) if dz else part
    after = mm3(split(charge), z_ref[...])
    for half in range(2):
        for quarter in range(2):
            tiles = [
                after[x * 32 : x * 32 + 32, quarter * 128 : quarter * 128 + 128]
                for x in range(half * 8, half * 8 + 8)
            ]
            for g, tile in enumerate(swap_groups(tiles)):
                pencil, ri = quarter * 4 + g // 2, g % 2
                start = pencil * 128 + half * 64 + ri * 32
                out_ref[start : start + 32, :] = tile


def gathered(ref, count, rows):
    block = ref[...].reshape(count, 2, rows, 128)
    return jnp.concatenate([block[:, half].reshape(count * rows, 128) for half in range(2)], axis=1)


def scattered(value, ref, count, rows):
    for half in range(2):
        part = value[:, half * 128 : half * 128 + 128].reshape(count, rows, 128)
        for i in range(count):
            ref[(i * 2 + half) * rows : (i * 2 + half + 1) * rows, :] = part[i]


def shared_lane(shape):
    return lax.broadcasted_iota(jnp.int32, shape, 1) % KZ == 0


def sign_of_y():
    return (1 - 2 * (lax.broadcasted_iota(jnp.int32, (256, 256), 0) % 2)).astype(F32)


def shared_forward(value, data, table_ref):
    def plane(part, index):
        return part.reshape(8, 2, 32, 256)[:, index].reshape(256, 256)

    parts = [mm3(table_ref[:, i], [plane(part, i) for part in data]) for i in range(2)]
    row = lax.broadcasted_iota(jnp.int32, (256, 256), 0)
    second = jnp.sum(plane(value, 1), axis=0, keepdims=True)
    first = jnp.sum(plane(value, 0) * sign_of_y(), axis=0, keepdims=True)
    return jnp.concatenate([jnp.where(row == 8, second, parts[0]), jnp.where(row == 0, first, parts[1])], axis=0)


def shared_backward(value, data, table_ref):
    parts = [mm3(table_ref[:, i], [part[i * 256 : i * 256 + 256] for part in data]) for i in range(2)]
    parts[0] += value[256:257] * (sign_of_y() * (1.0 / GY))
    parts[1] += value[8:9] * (1.0 / GY)
    return jnp.stack([part.reshape(8, 32, 256) for part in parts], axis=1).reshape(512, 256)


def y_stage(source, target, shared):
    def kernel(in_ref, table_ref, shared_ref, out_ref):
        value = gathered(in_ref, *source)
        data = split(value)
        out = mm3(table_ref[...], data)
        lone = shared_lane(out.shape) & (lax.axis_index("pencil") == 0)
        scattered(jnp.where(lone, shared(value, data, shared_ref), out), out_ref, *target)

    return kernel


def y_forward(*refs):
    y_stage((8, 64), (32, 16), shared_forward)(*refs)


def y_backward(*refs):
    y_stage((32, 16), (8, 64), shared_backward)(*refs)


def x_stage(in_ref, green_ref, other_ref, twist_ref, row_ref, lane_ref, out_ref):
    row_tables, lane_tables = row_ref[...], lane_ref[...]
    cosine, sine = twist_ref[0], twist_ref[1]

    def line(k, ri):
        return [in_ref[pl.ds(half * 16 + ri * 8 + k, 32, stride=32), :] for half in range(2)]

    def turn(re, im):
        return jnp.concatenate([re * cosine + im * sine, im * cosine - re * sine], axis=1)

    lines = [[jnp.concatenate(line(k, ri), axis=1) for k in range(8)] for ri in range(2)]
    data = [jnp.concatenate(lines[0] + [lines[0][0]], axis=1), jnp.concatenate(lines[1] + [-lines[1][0]], axis=1)]
    rows = mm3(row_tables, split(jnp.concatenate(data, axis=0)))
    columns = [slice(k * 256, k * 256 + 256) for k in range(9)]
    full = mm3(split(jnp.concatenate([turn(rows[:32, at], rows[32:, at]) for at in columns], axis=0)), lane_tables)
    product = []
    for part in range(4):
        at = slice(part * 128, part * 128 + 128)
        other = other_ref[:, part % 2 * 128 : part % 2 * 128 + 128]
        value = full[:256, at] * green_ref[part % 2]
        value = jnp.concatenate([value[:32] + full[256:, at] * other, value[32:]], axis=0)
        product.append(value if part < 2 else -value)

    back = mm3(split(jnp.concatenate(product, axis=1)), lane_tables)
    back = [turn(back[k * 32 : k * 32 + 32, :256], back[k * 32 : k * 32 + 32, 256:]) for k in range(8)]
    data = [jnp.concatenate([part[:, ri * 256 : ri * 256 + 256] for part in back], axis=1) for ri in range(2)]
    rows = mm3(row_tables, split(jnp.concatenate(data, axis=0)))
    for k in range(8):
        for ri in range(2):
            for half in range(2):
                part = rows[ri * 32 : ri * 32 + 32, k * 256 + half * 128 : k * 256 + half * 128 + 128]
                out_ref[pl.ds(half * 16 + ri * 8 + k, 32, stride=32), :] = part * ((1 - 2 * ri) / GX)


def sample(in_ref, weight_ref, anchor_ref, z_ref, out_ref, y_ref, after_ref, grid_ref):
    for half in range(2):
        for quarter in range(2):
            tiles = []
            for g in range(8):
                pencil, ri = quarter * 4 + g // 2, g % 2
                start = pencil * 128 + half * 64 + ri * 32
                tiles.append(in_ref[start : start + 32, :])
            for i, tile in enumerate(swap_groups(tiles)):
                x = half * 8 + i
                after_ref[x * 32 : x * 32 + 32, quarter * 128 : quarter * 128 + 128] = tile
    high, low = split(mm3(split(after_ref[...]), z_ref[...]))
    first, second, third = anchor_parts(anchor_ref[0])
    y_place(second, y_ref)

    total = jnp.zeros((8, SLOTS), F32)
    for dz in range(EDGE):
        hot = z_hot(third, dz)
        grid_ref[dz] = mm(high, hot) + mm(low, hot)
        for x in range(SLAB_ROWS):
            rows = place_rows(stencil_row(x, dz, first, weight_ref), y_ref)
            cells = grid_ref[dz, x * 32 : x * 32 + 32, :] * rows
            total += jnp.sum(cells.reshape(4, 8, SLOTS), axis=0)
    far = jnp.sum(total, axis=0, keepdims=True)
    tables = [far[:, tile * 128 : tile * 128 + 128] for tile in range(SLOTS // 128)]
    for block in range(N_SLAB // 8):
        slab = lax.broadcasted_iota(jnp.int32, (8, 128), 0) + block * 8
        place = lax.broadcasted_iota(jnp.int32, (8, 128), 1)
        index = slab * 12 + place + jnp.where(place < 12, 0, SLOTS // 2 - 12)
        out_ref[block * 8 : block * 8 + 8, :] = lookup(tables, jnp.where(place < CAP, index, SLOTS))


def home(slot_ref, slab_ref, place_ref):
    slots = jnp.transpose(jnp.broadcast_to(slot_ref[0], (128, SLOTS)))
    panel = lax.broadcasted_iota(jnp.int32, (SLOTS, 128), 1)
    slot = lax.broadcasted_iota(jnp.int32, (SLOTS, 128), 0).astype(F32)
    for half in range(2):
        at = slice(half * 128, half * 128 + 128)
        own = jnp.sum(jnp.where(slots == panel + half * 128, slot, 0.0), axis=0, keepdims=True)
        own = jnp.broadcast_to(own, (8, 128)).astype(jnp.int32)
        slab = quotient(own, CAP)
        slab_ref[:, at] = slab
        place_ref[:, at] = own - slab * CAP


def near(arrived_ref, own_ref, index_ref, factor_ref, out_ref):
    slab = lax.axis_index("slab")
    before, after = (
        [arrived_ref[pl.ds(lax.rem(slab + shift, N_SLAB) * LINES + 13 + half, 1), :] for half in range(2)]
        for shift in (N_SLAB - 1, 1)
    )
    tables = before + [own_ref[:, :128], own_ref[:, 128:]] + after
    for lane in range(2):
        total = jnp.zeros((8, 128), F32)
        for block in range(4):
            at = (slice(block * 8, block * 8 + 8), slice(lane * 128, lane * 128 + 128))
            total += lookup(tables, index_ref[at]) * factor_ref[at]
        out_ref[:, lane * 128 : lane * 128 + 128] = jnp.sum(total, axis=0, keepdims=True)


def finish(far_ref, slab_ref, place_ref, near_ref, out_ref):
    far = far_ref[...]
    for half in range(2):
        at = slice(half * 128, half * 128 + 128)
        out_ref[:, at] = pick(far, slab_ref[:, at], place_ref[:, at]) + near_ref[:, at]


def swap(value, axis, count):
    rows = value.shape[0]
    return lax.all_to_all(value.reshape(count, rows // count, 128), axis, 0, 0, tiled=True).reshape(rows, 128)


def arrange_green(green_ref, plane_ref, out_ref, other_ref):
    slab, pencil, ends = position()
    shared, upper, straight = pencil == 0, slab >= 16, pencil < 4
    place = lax.broadcasted_iota(jnp.int32, (KZ, GX), 0) == 0
    group = lax.broadcasted_iota(jnp.int32, (32, 128), 1) // KZ

    def lay(rows):
        turned = jnp.transpose(jnp.concatenate([rows] * 8, axis=0))
        halves = []
        for half in range(2):
            total = jnp.zeros((32, 128), F32)
            for k2 in range(8):
                start = (half * 8 + k2) * 32
                total = jnp.where(group == k2, turned[start : start + 32], total)
            halves.append(total)
        return jnp.concatenate(halves, axis=1)

    for k in range(8):
        up = green_ref[k, :KZ, :]
        down = jnp.concatenate([green_ref[k, KZ - i : KZ - i + 1, :] for i in range(KZ)], axis=0)
        rows = jnp.where(straight, up, down)
        zero, plane = rows[0:1], plane_ref[k : k + 1, :]
        line = jnp.where(upper, plane, zero)
        if k == 0:
            line = jnp.where(ends, 0.5 * (zero + plane), line)
            differ = jnp.where(ends, 0.5 * (zero - plane), 0.0)
            other_ref[...] = lay(jnp.where(place, differ, 0.0))
        rows = jnp.where(place & shared, line, rows)
        laid = lay(rows)
        for half in range(2):
            out_ref[half, k * 32 : k * 32 + 32, :] = laid[:, half * 128 : half * 128 + 128]


def per_device(strength, stencil_weight, slot_panel, slot_anchor, green_spectrum, near_index, near_factor):
    row = strength.reshape(1, PAN_DEV)

    z_fwd, z_bwd = (pair(t) for t in z_tables())
    y_fwd, y_fwd_shared, y_bwd, y_bwd_shared = (pair(t) for t in y_tables())
    rows, twist, lanes = x_tables()
    rows, lanes = pair(rows), pair(lanes)
    twist = jnp.asarray(twist, F32)

    anchor = slot_anchor.reshape(N_SLAB, 2, 12).transpose(1, 0, 2).reshape(1, 1, SLOTS)

    shape = jax.ShapeDtypeStruct
    payload = call(
        pack, shape((ROWS, 128), F32), slot_panel, stencil_weight, row,
        scratch=[pltpu.VMEM((SLOTS, 128), F32)], limit=56,
    )

    payload, spectrum, own_slots = lax.optimization_barrier((payload, green_spectrum, slot_panel))
    plane = lax.ppermute(spectrum[:, 0, :], "pencil", [(4, 0)])
    arrived = lax.all_to_all(payload.reshape(N_SLAB, 1, LINES * 128), "slab", 0, 0, tiled=True).reshape(ROWS, 128)
    green, other = call(
        arrange_green, [shape((2, 256, 128), F32), shape((32, 256), F32)], spectrum, plane, limit=LIMIT_N
    )
    homes = call(home, [shape((8, PAN_DEV), jnp.int32)] * 2, own_slots, limit=LIMIT_N)
    arrived, green, other, anchor, homes = lax.optimization_barrier((arrived, green, other, anchor, homes))
    near_field = call(
        near, shape((1, PAN_DEV), F32), arrived, row, near_index, near_factor, limit=LIMIT_N
    )
    after_z, weights = call(
        project, [shape((1024, 128), F32), shape((128, SLOTS), F32)], arrived, anchor, z_fwd,
        scratch=[pltpu.VMEM((128, SLOTS), F32), pltpu.VMEM((PENCIL_ROWS, SLOTS), jnp.int32)]
        + [pltpu.VMEM((SLOTS // 2, 128), F32)]
        + [pltpu.VMEM((EDGE, 512, SLOTS), BF16)] * 2,
        limit=LIMIT_P,
    )
    after_z, near_field = lax.optimization_barrier((after_z, near_field))
    by_y = swap(after_z, "pencil", N_PENCIL)
    after_y = call(
        y_forward, shape((1024, 128), F32), by_y, y_fwd, y_fwd_shared,
        limit=LIMIT_Y,
    )
    by_x = swap(after_y, "slab", N_SLAB)
    after_x = call(
        x_stage, shape((1024, 128), F32), by_x, green, other, twist, rows, lanes,
        limit=LIMIT_X,
    )
    back_x = swap(after_x, "slab", N_SLAB)
    back_y = call(
        y_backward, shape((1024, 128), F32), back_x, y_bwd, y_bwd_shared,
        limit=LIMIT_Y,
    )
    by_z = swap(back_y, "pencil", N_PENCIL)
    sampled = call(
        sample, shape((N_SLAB, 128), F32), by_z, weights, anchor, z_bwd,
        scratch=[pltpu.VMEM((PENCIL_ROWS, SLOTS), jnp.int32), pltpu.VMEM((512, 256), F32)]
        + [pltpu.VMEM((EDGE, 512, SLOTS), F32)],
        limit=LIMIT_S,
    )
    far = lax.all_to_all(sampled, "slab", 0, 0, tiled=True)
    return call(finish, shape((1, PAN_DEV), F32), far, *homes, near_field, limit=40).reshape(PAN_DEV)


def solution(mesh):
    in_specs = (
        P(("slab", "pencil")),
        P(None, ("slab", "pencil")),
        P("slab", "pencil", None),
        P("slab", "pencil", None),
        P("slab", "pencil", None),
        P(None, ("slab", "pencil")),
        P(None, ("slab", "pencil")),
    )
    out_specs = P(("slab", "pencil"))
    return jax.shard_map(
        per_device, mesh=mesh, in_specs=in_specs, out_specs=out_specs, check_vma=False
    )
```

```python
import math

import jax
import jax.numpy as jnp
import numpy as np
from jax import lax
from jax.experimental import pallas as pl
from jax.experimental.pallas import tpu as pltpu
from jax.sharding import PartitionSpec as P

GX = 512
GY = 256
GZ = 256
EDGE = 4
PAN_DEV = 256
CAP = 24
N_SLAB = 32
N_PENCIL = 8
SLOTS = N_SLAB * CAP
SLAB_ROWS = 16
PENCIL_ROWS = 32
STENCIL = 64
KZ = 16
LINES = 15
ROWS = LINES * N_SLAB
LIMIT_P, LIMIT_Y, LIMIT_X, LIMIT_S = 48, 40, 51, 40
LIMIT_N = 40
F32 = jnp.float32
BF16 = jnp.bfloat16


def kz_of(pencil, place):
    return np.where(
        pencil < 4, 32 * pencil + place, -(32 * (7 - pencil) + 16 + place)
    )


def z_tables():
    pencil, ri, place = np.meshgrid(np.arange(8), np.arange(2), np.arange(KZ), indexing="ij")
    kz = kz_of(pencil, place).reshape(-1)
    ri = ri.reshape(-1)
    shared = (pencil.reshape(-1) == 0) & (place.reshape(-1) == 0)
    z = np.arange(GZ)
    theta = 2 * np.pi * ((z[:, None] * kz[None, :]) % GZ) / GZ
    sign = 1.0 - 2.0 * (z % 2)
    forward = np.where(ri == 0, np.cos(theta), -np.sin(theta))
    forward = np.where(shared & (ri == 1), sign[:, None], forward)
    scale = np.where(shared, 1.0, 2.0) / GZ
    backward = (forward * scale).T
    return forward, backward


def y_tables():
    slab, ro, k8 = (a.reshape(-1) for a in np.meshgrid(np.arange(32), np.arange(2), np.arange(8), indexing="ij"))
    pencil, ri, y32 = (a.reshape(-1) for a in np.meshgrid(np.arange(8), np.arange(2), np.arange(32), indexing="ij"))
    ky = (8 * slab + k8)[:, None]
    ro = ro[:, None]
    y = (32 * pencil + y32)[None, :]
    ri = ri[None, :]
    theta = 2 * np.pi * ((ky * y) % GY) / GY
    cosine, sine = np.cos(theta), np.sin(theta)
    forward = np.where(ro == ri, cosine, np.where(ro == 0, sine, -sine))
    backward = forward.T / GY
    part = np.where(ro == 0, cosine, -sine)
    ends = (ky == 0) | (ky == 128)
    part = np.where(ends, np.where(ro == (ky == 128), cosine, 0.0), part)
    first = part[:, np.broadcast_to(ri == 0, y.shape)[0]]
    shared = np.stack([first[:256], first[256:]])
    scale = (np.where(ends, 1.0, 2.0) / GY).reshape(2, 256, 1)
    shared_back = (shared * scale).transpose(0, 2, 1)
    return forward, shared, backward, shared_back


def x_tables():
    ro, k1 = (a.reshape(-1)[:, None] for a in np.meshgrid(np.arange(2), np.arange(32), indexing="ij"))
    ri, slab = (a.reshape(-1)[None, :] for a in np.meshgrid(np.arange(2), np.arange(32), indexing="ij"))
    theta = 2 * np.pi * ((k1 * slab) % 32) / 32
    rows = np.where(ro == ri, np.cos(theta), np.where(ro == 0, np.sin(theta), -np.sin(theta)))
    x16 = np.arange(16)
    twist = 2 * np.pi * np.arange(32)[:, None] * x16[None, :] / GX
    twist = np.repeat(twist, KZ, axis=1)
    inner = 2 * np.pi * ((x16[:, None] * x16[None, :]) % 16) / 16
    eye = np.eye(KZ)
    cosine, sine = np.kron(np.cos(inner), eye), np.kron(np.sin(inner), eye)
    lanes = np.block([[cosine, -sine], [sine, cosine]])
    return rows, np.stack([np.cos(twist), np.sin(twist)]), lanes


def pair(table):
    high = np.asarray(table, np.float32).astype(jnp.bfloat16)
    low = (np.asarray(table, np.float64) - high.astype(np.float64)).astype(jnp.bfloat16)
    return jnp.asarray(np.stack([high, low]))


def split(value):
    high = value.astype(BF16)
    return high, (value - high.astype(F32)).astype(BF16)


def mm(left, right):
    return jnp.dot(left, right, preferred_element_type=F32)


def mm_nt(left, right):
    return lax.dot_general(left, right, (((1,), (1,)), ((), ())), preferred_element_type=F32)


def mm3(left, right):
    return mm(left[0], right[0]) + (mm(left[0], right[1]) + mm(left[1], right[0]))


def call(kernel, out_shape, *args, scratch=(), limit):
    out_spec = pl.BlockSpec(memory_space=pltpu.VMEM)
    return pl.pallas_call(
        kernel,
        out_shape=out_shape,
        in_specs=[pl.BlockSpec(memory_space=pltpu.VMEM)] * len(args),
        out_specs=[out_spec] * len(out_shape) if isinstance(out_shape, list) else out_spec,
        scratch_shapes=list(scratch),
        compiler_params=pltpu.CompilerParams(vmem_limit_bytes=limit * 2**20),
        name=kernel.__name__,
    )(*args)


def swap_groups(tiles):
    tiles = list(tiles)
    group = lax.broadcasted_iota(jnp.int32, tiles[0].shape, 1) // 16
    for bit in range(3):
        step = 1 << bit
        upper = (group & step) != 0
        for i in range(8):
            if i & step:
                continue
            low, high = tiles[i], tiles[i + step]
            tiles[i] = jnp.where(upper, pltpu.roll(high, 16 * step, 1), low)
            tiles[i + step] = jnp.where(upper, high, pltpu.roll(low, 128 - 16 * step, 1))
    return tiles


def position():
    slab, pencil = lax.axis_index("slab"), lax.axis_index("pencil")
    return slab, pencil, (pencil == 0) & ((slab == 0) | (slab == 16))


def lookup(tables, index):
    inner, outer = index & 127, index >> 7
    found = jnp.zeros((8, 128), F32)
    for part, table in enumerate(tables):
        row = jnp.broadcast_to(table, (8, 128))
        value = jnp.take_along_axis(row, inner, axis=1, mode="promise_in_bounds")
        found = jnp.where(outer == part, value, found)
    return found


def quotient(value, divisor):
    return ((value.astype(F32) + 0.5) * (1.0 / divisor)).astype(jnp.int32)


def pick(table, slab, place):
    sublane = lax.broadcasted_iota(jnp.int32, (8, 128), 0)
    total = jnp.zeros((8, 128), F32)
    for block in range(N_SLAB // 8):
        value = jnp.take_along_axis(table[block * 8 : block * 8 + 8], place, axis=1, mode="promise_in_bounds")
        total = jnp.where(slab == sublane + block * 8, value, total)
    return jnp.sum(total, axis=0, keepdims=True)


def pack(slot_ref, weight_ref, strength_ref, out_ref, by_slot_ref):
    strength = strength_ref[...]
    halves = [strength[:, :128], strength[:, 128:]]
    tables = []
    for tile in range(SLOTS // 128):
        at = slice(tile * 128, tile * 128 + 128)
        index = jnp.broadcast_to(slot_ref[0, :, at], (8, 128))
        inner, outer = index & 127, index >> 7
        tables.append(lookup(halves, index)[:1])
        found = []
        for block in range(8):
            low, high = (
                jnp.take_along_axis(
                    weight_ref[block * 8 : block * 8 + 8, half * 128 : half * 128 + 128],
                    inner,
                    axis=1,
                    mode="promise_in_bounds",
                )
                for half in range(2)
            )
            found.append(jnp.where(outer == 0, low, jnp.where(outer == 1, high, 0.0)))
        by_slot_ref[at, :] = jnp.transpose(jnp.concatenate(found * 2, axis=0))
    first = lax.broadcasted_iota(jnp.int32, (12, 128), 1) < STENCIL
    for d in range(N_SLAB):
        out_ref[d * LINES : d * LINES + 12, :] = jnp.where(
            first, by_slot_ref[d * CAP : d * CAP + 12, :], by_slot_ref[d * CAP + 12 : d * CAP + 24, :]
        )
    sent = []
    for block in range(N_SLAB // 8):
        slab = lax.broadcasted_iota(jnp.int32, (8, 128), 0) + block * 8
        place = lax.broadcasted_iota(jnp.int32, (8, 128), 1)
        sent.append(lookup(tables, jnp.where(place < CAP, slab * CAP + place, SLOTS)))
    out_ref[pl.ds(12, N_SLAB, stride=LINES), :] = jnp.concatenate(sent, axis=0)
    for half in range(2):
        out_ref[pl.ds(13 + half, N_SLAB, stride=LINES), :] = jnp.broadcast_to(halves[half], (N_SLAB, 128))


def anchor_parts(anchor):
    return anchor >> 13, (anchor >> 8) & 31, anchor & 255


def z_hot(third, dz):
    z = lax.broadcasted_iota(jnp.int32, (GZ, SLOTS), 0)
    return jnp.where(z - dz == third, 1.0, 0.0).astype(BF16)


def y_place(second, y_ref):
    rel = lax.broadcasted_iota(jnp.int32, (PENCIL_ROWS, SLOTS), 0) - second
    y_ref[...] = jnp.where((rel >= 0) & (rel < EDGE), rel, EDGE)


def stencil_row(x, dz, first, weight_ref):
    total = jnp.zeros((8, SLOTS), F32)
    for dx in range(EDGE):
        start = dx * 32 + dz * 8
        total = jnp.where(first == x - dx, weight_ref[start : start + 8, :], total)
    return total


def place_rows(rows, y_ref):
    out = []
    for block in range(PENCIL_ROWS // 8):
        pieces = []
        for lane in range(SLOTS // 128):
            at = slice(lane * 128, lane * 128 + 128)
            index = y_ref[block * 8 : block * 8 + 8, at]
            pieces.append(jnp.take_along_axis(rows[:, at], index, axis=0, mode="promise_in_bounds"))
        out.append(jnp.concatenate(pieces, axis=1))
    return jnp.concatenate(out, axis=0)


def slot_order():
    row = lax.broadcasted_iota(jnp.int32, (256, 128), 0)
    lane = lax.broadcasted_iota(jnp.int32, (256, 128), 1)
    dy = row & 7
    picked = ((row >> 5) << 4) + (dy << 2) + ((row >> 3) & 3)
    return jnp.where((lane == picked) & (dy < EDGE), 1.0, 0.0).astype(BF16)


def project(arrived_ref, anchor_ref, z_ref, out_ref, weight_ref, scaled_ref, y_ref, packed_ref, high_ref, low_ref):
    for s in range(N_SLAB):
        packed_ref[s * 12 : s * 12 + 12, :] = arrived_ref[s * LINES : s * LINES + 12, :]
    packed = jnp.concatenate(split(packed_ref[...]), axis=0)
    order = slot_order()
    turned = [mm_nt(order[half * 128 : half * 128 + 128, :], packed) for half in range(2)]
    turned = [part[:, : SLOTS // 2] + part[:, SLOTS // 2 :] for part in turned]
    weights = jnp.concatenate(turned, axis=1)
    weight_ref[...] = weights
    sent = arrived_ref[pl.ds(12, N_SLAB, stride=LINES), :]
    strength = []
    for tile in range(SLOTS // 128):
        slot = lax.broadcasted_iota(jnp.int32, (8, 128), 1) + tile % 3 * 128
        slab = quotient(slot, 12)
        strength.append(pick(sent, slab, slot - slab * 12 + tile // 3 * 12))
    scaled_ref[...] = weights * jnp.concatenate(strength, axis=1)
    first, second, third = anchor_parts(anchor_ref[0])
    y_place(second, y_ref)
    hot = z_hot(third, 0)
    charge = jnp.zeros((512, GZ), F32)
    for dz in range(EDGE):
        for x in range(SLAB_ROWS):
            at = slice(x * PENCIL_ROWS, x * PENCIL_ROWS + PENCIL_ROWS)
            high, low = split(place_rows(stencil_row(x, dz, first, scaled_ref), y_ref))
            high_ref[dz, at, :] = high
            low_ref[dz, at, :] = low
        part = mm_nt(high_ref[dz], hot) + mm_nt(low_ref[dz], hot)
        charge += pltpu.roll(part, dz, 1) if dz else part
    after = mm3(split(charge), z_ref[...])
    for half in range(2):
        for quarter in range(2):
            tiles = [
                after[x * 32 : x * 32 + 32, quarter * 128 : quarter * 128 + 128]
                for x in range(half * 8, half * 8 + 8)
            ]
            for g, tile in enumerate(swap_groups(tiles)):
                pencil, ri = quarter * 4 + g // 2, g % 2
                start = pencil * 128 + half * 64 + ri * 32
                out_ref[start : start + 32, :] = tile


def gathered(ref, count, rows):
    block = ref[...].reshape(count, 2, rows, 128)
    return jnp.concatenate([block[:, half].reshape(count * rows, 128) for half in range(2)], axis=1)


def scattered(value, ref, count, rows):
    for half in range(2):
        part = value[:, half * 128 : half * 128 + 128].reshape(count, rows, 128)
        for i in range(count):
            ref[(i * 2 + half) * rows : (i * 2 + half + 1) * rows, :] = part[i]


def shared_lane(shape):
    return lax.broadcasted_iota(jnp.int32, shape, 1) % KZ == 0


def sign_of_y():
    return (1 - 2 * (lax.broadcasted_iota(jnp.int32, (256, 256), 0) % 2)).astype(F32)


def shared_forward(value, data, table_ref):
    def plane(part, index):
        return part.reshape(8, 2, 32, 256)[:, index].reshape(256, 256)

    parts = [mm3(table_ref[:, i], [plane(part, i) for part in data]) for i in range(2)]
    row = lax.broadcasted_iota(jnp.int32, (256, 256), 0)
    second = jnp.sum(plane(value, 1), axis=0, keepdims=True)
    first = jnp.sum(plane(value, 0) * sign_of_y(), axis=0, keepdims=True)
    return jnp.concatenate([jnp.where(row == 8, second, parts[0]), jnp.where(row == 0, first, parts[1])], axis=0)


def shared_backward(value, data, table_ref):
    parts = [mm3(table_ref[:, i], [part[i * 256 : i * 256 + 256] for part in data]) for i in range(2)]
    parts[0] += value[256:257] * (sign_of_y() * (1.0 / GY))
    parts[1] += value[8:9] * (1.0 / GY)
    return jnp.stack([part.reshape(8, 32, 256) for part in parts], axis=1).reshape(512, 256)


def y_stage(source, target, shared):
    def kernel(in_ref, table_ref, shared_ref, out_ref, work_ref):
        value = gathered(in_ref, *source)
        data = split(value)
        work_ref[...] = mm3(table_ref[...], data)

        @pl.when(lax.axis_index("pencil") == 0)
        def _():
            other = shared(value, data, shared_ref)
            work_ref[...] = jnp.where(shared_lane(other.shape), other, work_ref[...])

        scattered(work_ref[...], out_ref, *target)

    return kernel


def y_forward(*refs):
    y_stage((8, 64), (32, 16), shared_forward)(*refs)


def y_backward(*refs):
    y_stage((32, 16), (8, 64), shared_backward)(*refs)


def x_stage(in_ref, green_ref, other_ref, twist_ref, row_ref, lane_ref, out_ref):
    row_tables, lane_tables = row_ref[...], lane_ref[...]
    cosine, sine = twist_ref[0], twist_ref[1]

    def line(k, ri):
        return [in_ref[pl.ds(half * 16 + ri * 8 + k, 32, stride=32), :] for half in range(2)]

    def turn(re, im):
        return jnp.concatenate([re * cosine + im * sine, im * cosine - re * sine], axis=1)

    lines = [[jnp.concatenate(line(k, ri), axis=1) for k in range(8)] for ri in range(2)]
    data = [jnp.concatenate(lines[0] + [lines[0][0]], axis=1), jnp.concatenate(lines[1] + [-lines[1][0]], axis=1)]
    rows = mm3(row_tables, split(jnp.concatenate(data, axis=0)))
    columns = [slice(k * 256, k * 256 + 256) for k in range(9)]
    full = mm3(split(jnp.concatenate([turn(rows[:32, at], rows[32:, at]) for at in columns], axis=0)), lane_tables)
    product = []
    for part in range(4):
        at = slice(part * 128, part * 128 + 128)
        other = other_ref[:, part % 2 * 128 : part % 2 * 128 + 128]
        value = full[:256, at] * green_ref[part % 2]
        value = jnp.concatenate([value[:32] + full[256:, at] * other, value[32:]], axis=0)
        product.append(value if part < 2 else -value)

    back = mm3(split(jnp.concatenate(product, axis=1)), lane_tables)
    back = [turn(back[k * 32 : k * 32 + 32, :256], back[k * 32 : k * 32 + 32, 256:]) for k in range(8)]
    data = [jnp.concatenate([part[:, ri * 256 : ri * 256 + 256] for part in back], axis=1) for ri in range(2)]
    rows = mm3(row_tables, split(jnp.concatenate(data, axis=0)))
    for k in range(8):
        for ri in range(2):
            for half in range(2):
                part = rows[ri * 32 : ri * 32 + 32, k * 256 + half * 128 : k * 256 + half * 128 + 128]
                out_ref[pl.ds(half * 16 + ri * 8 + k, 32, stride=32), :] = part * ((1 - 2 * ri) / GX)


def sample(in_ref, weight_ref, anchor_ref, z_ref, out_ref, y_ref, after_ref, grid_ref):
    for half in range(2):
        for quarter in range(2):
            tiles = []
            for g in range(8):
                pencil, ri = quarter * 4 + g // 2, g % 2
                start = pencil * 128 + half * 64 + ri * 32
                tiles.append(in_ref[start : start + 32, :])
            for i, tile in enumerate(swap_groups(tiles)):
                x = half * 8 + i
                after_ref[x * 32 : x * 32 + 32, quarter * 128 : quarter * 128 + 128] = tile
    high, low = split(mm3(split(after_ref[...]), z_ref[...]))
    first, second, third = anchor_parts(anchor_ref[0])
    y_place(second, y_ref)

    total = jnp.zeros((8, SLOTS), F32)
    for dz in range(EDGE):
        hot = z_hot(third, dz)
        grid_ref[dz] = mm(high, hot) + mm(low, hot)
        for x in range(SLAB_ROWS):
            rows = place_rows(stencil_row(x, dz, first, weight_ref), y_ref)
            cells = grid_ref[dz, x * 32 : x * 32 + 32, :] * rows
            total += jnp.sum(cells.reshape(4, 8, SLOTS), axis=0)
    far = jnp.sum(total, axis=0, keepdims=True)
    tables = [far[:, tile * 128 : tile * 128 + 128] for tile in range(SLOTS // 128)]
    for block in range(N_SLAB // 8):
        slab = lax.broadcasted_iota(jnp.int32, (8, 128), 0) + block * 8
        place = lax.broadcasted_iota(jnp.int32, (8, 128), 1)
        index = slab * 12 + place + jnp.where(place < 12, 0, SLOTS // 2 - 12)
        out_ref[block * 8 : block * 8 + 8, :] = lookup(tables, jnp.where(place < CAP, index, SLOTS))


def home(slot_ref, slab_ref, place_ref):
    slots = jnp.transpose(jnp.broadcast_to(slot_ref[0], (128, SLOTS)))
    panel = lax.broadcasted_iota(jnp.int32, (SLOTS, 128), 1)
    slot = lax.broadcasted_iota(jnp.int32, (SLOTS, 128), 0).astype(F32)
    for half in range(2):
        at = slice(half * 128, half * 128 + 128)
        own = jnp.sum(jnp.where(slots == panel + half * 128, slot, 0.0), axis=0, keepdims=True)
        own = jnp.broadcast_to(own, (8, 128)).astype(jnp.int32)
        slab = quotient(own, CAP)
        slab_ref[:, at] = slab
        place_ref[:, at] = own - slab * CAP


def near(arrived_ref, own_ref, index_ref, factor_ref, out_ref):
    slab = lax.axis_index("slab")
    before, after = (
        [arrived_ref[pl.ds(lax.rem(slab + shift, N_SLAB) * LINES + 13 + half, 1), :] for half in range(2)]
        for shift in (N_SLAB - 1, 1)
    )
    tables = before + [own_ref[:, :128], own_ref[:, 128:]] + after
    for lane in range(2):
        total = jnp.zeros((8, 128), F32)
        for block in range(4):
            at = (slice(block * 8, block * 8 + 8), slice(lane * 128, lane * 128 + 128))
            total += lookup(tables, index_ref[at]) * factor_ref[at]
        out_ref[:, lane * 128 : lane * 128 + 128] = jnp.sum(total, axis=0, keepdims=True)


def finish(far_ref, slab_ref, place_ref, near_ref, out_ref):
    far = far_ref[...]
    for half in range(2):
        at = slice(half * 128, half * 128 + 128)
        out_ref[:, at] = pick(far, slab_ref[:, at], place_ref[:, at]) + near_ref[:, at]


def swap(value, axis, count):
    rows = value.shape[0]
    return lax.all_to_all(value.reshape(count, rows // count, 128), axis, 0, 0, tiled=True).reshape(rows, 128)


def arrange_green(green_ref, plane_ref, out_ref, other_ref):
    slab, pencil, ends = position()
    shared, upper, straight = pencil == 0, slab >= 16, pencil < 4
    place = lax.broadcasted_iota(jnp.int32, (KZ, GX), 0) == 0
    group = lax.broadcasted_iota(jnp.int32, (32, 128), 1) // KZ

    def lay(rows):
        turned = jnp.transpose(jnp.concatenate([rows] * 8, axis=0))
        halves = []
        for half in range(2):
            total = jnp.zeros((32, 128), F32)
            for k2 in range(8):
                start = (half * 8 + k2) * 32
                total = jnp.where(group == k2, turned[start : start + 32], total)
            halves.append(total)
        return jnp.concatenate(halves, axis=1)

    for k in range(8):
        up = green_ref[k, :KZ, :]
        down = jnp.concatenate([green_ref[k, KZ - i : KZ - i + 1, :] for i in range(KZ)], axis=0)
        rows = jnp.where(straight, up, down)
        zero, plane = rows[0:1], plane_ref[k : k + 1, :]
        line = jnp.where(upper, plane, zero)
        if k == 0:
            line = jnp.where(ends, 0.5 * (zero + plane), line)
            differ = jnp.where(ends, 0.5 * (zero - plane), 0.0)
            other_ref[...] = lay(jnp.where(place, differ, 0.0))
        rows = jnp.where(place & shared, line, rows)
        laid = lay(rows)
        for half in range(2):
            out_ref[half, k * 32 : k * 32 + 32, :] = laid[:, half * 128 : half * 128 + 128]


def per_device(strength, stencil_weight, slot_panel, slot_anchor, green_spectrum, near_index, near_factor):
    row = strength.reshape(1, PAN_DEV)

    z_fwd, z_bwd = (pair(t) for t in z_tables())
    y_fwd, y_fwd_shared, y_bwd, y_bwd_shared = (pair(t) for t in y_tables())
    rows, twist, lanes = x_tables()
    rows, lanes = pair(rows), pair(lanes)
    twist = jnp.asarray(twist, F32)

    anchor = slot_anchor.reshape(N_SLAB, 2, 12).transpose(1, 0, 2).reshape(1, 1, SLOTS)

    shape = jax.ShapeDtypeStruct
    payload = call(
        pack, shape((ROWS, 128), F32), slot_panel, stencil_weight, row,
        scratch=[pltpu.VMEM((SLOTS, 128), F32)], limit=56,
    )

    payload, spectrum, own_slots = lax.optimization_barrier((payload, green_spectrum, slot_panel))
    plane = lax.ppermute(spectrum[:, 0, :], "pencil", [(4, 0)])
    arrived = lax.all_to_all(payload.reshape(N_SLAB, 1, LINES * 128), "slab", 0, 0, tiled=True).reshape(ROWS, 128)
    green, other = call(
        arrange_green, [shape((2, 256, 128), F32), shape((32, 256), F32)], spectrum, plane, limit=LIMIT_N
    )
    homes = call(home, [shape((8, PAN_DEV), jnp.int32)] * 2, own_slots, limit=LIMIT_N)
    arrived, green, other, anchor, homes = lax.optimization_barrier((arrived, green, other, anchor, homes))
    near_field = call(
        near, shape((1, PAN_DEV), F32), arrived, row, near_index, near_factor, limit=LIMIT_N
    )
    after_z, weights = call(
        project, [shape((1024, 128), F32), shape((128, SLOTS), F32)], arrived, anchor, z_fwd,
        scratch=[pltpu.VMEM((128, SLOTS), F32), pltpu.VMEM((PENCIL_ROWS, SLOTS), jnp.int32)]
        + [pltpu.VMEM((SLOTS // 2, 128), F32)]
        + [pltpu.VMEM((EDGE, 512, SLOTS), BF16)] * 2,
        limit=LIMIT_P,
    )
    after_z, near_field = lax.optimization_barrier((after_z, near_field))
    by_y = swap(after_z, "pencil", N_PENCIL)
    after_y = call(
        y_forward, shape((1024, 128), F32), by_y, y_fwd, y_fwd_shared,
        scratch=[pltpu.VMEM((512, 256), F32)], limit=LIMIT_Y,
    )
    by_x = swap(after_y, "slab", N_SLAB)
    after_x = call(
        x_stage, shape((1024, 128), F32), by_x, green, other, twist, rows, lanes,
        limit=LIMIT_X,
    )
    back_x = swap(after_x, "slab", N_SLAB)
    back_y = call(
        y_backward, shape((1024, 128), F32), back_x, y_bwd, y_bwd_shared,
        scratch=[pltpu.VMEM((512, 256), F32)], limit=LIMIT_Y,
    )
    by_z = swap(back_y, "pencil", N_PENCIL)
    sampled = call(
        sample, shape((N_SLAB, 128), F32), by_z, weights, anchor, z_bwd,
        scratch=[pltpu.VMEM((PENCIL_ROWS, SLOTS), jnp.int32), pltpu.VMEM((512, 256), F32)]
        + [pltpu.VMEM((EDGE, 512, SLOTS), F32)],
        limit=LIMIT_S,
    )
    far = lax.all_to_all(sampled, "slab", 0, 0, tiled=True)
    return call(finish, shape((1, PAN_DEV), F32), far, *homes, near_field, limit=40).reshape(PAN_DEV)


def solution(mesh):
    in_specs = (
        P(("slab", "pencil")),
        P(None, ("slab", "pencil")),
        P("slab", "pencil", None),
        P("slab", "pencil", None),
        P("slab", "pencil", None),
        P(None, ("slab", "pencil")),
        P(None, ("slab", "pencil")),
    )
    out_specs = P(("slab", "pencil"))
    return jax.shard_map(
        per_device, mesh=mesh, in_specs=in_specs, out_specs=out_specs, check_vma=False
    )
```
